32 devices in a mesh: member: 2 (over x), lon: 8 (over z, y), lat: 2 (over core).
Axes of the slice: x: 2, y: 2, z: 4, core: 2. Of those that a mesh axis runs over, the one named last changes fastest.
Arguments:
- iterate: float32 [4, 640, 1024], P('member', 'lat', 'lon'), parts along dimension 0, may hold values from -6 to 6
- residual: float32 [4, 640, 1024], P('member', 'lat', 'lon'), parts along dimension 0, may hold values from -6 to 6
- direction: float32 [4, 640, 1024], P('member', 'lat', 'lon'), parts along dimension 0, may hold values from -6 to 6
- land_sea: int32 [2, 640, 1024], P(None, 'lat', 'lon'), may hold values 0 or 1
- precision_weight: float32 [2, 640, 1024], P(None, 'lat', 'lon'), may hold values from 0.2 to 5
- east_kappa: float32 [640, 1024], P('lat', 'lon'), may hold values from 0.18 to 0.24
- north_kappa: float32 [640, 1024], P('lat', 'lon'), may hold values from 0.18 to 0.24
- fold_partner: int32 [1024], replicated, may hold values from 0 to 1023, as said below
Outputs:
- new_iterate: float32 [4, 640, 1024], P('member', 'lat', 'lon'), parts along dimension 0
- new_residual: float32 [4, 640, 1024], P('member', 'lat', 'lon'), parts along dimension 0
- new_direction: float32 [4, 640, 1024], P('member', 'lat', 'lon'), parts along dimension 0
The draws below stay inside these ranges and needn't reach their ends.
There are 2 independent parts, one for each index of `member`. The reference program is written for one: setup_inputs(seed, part) draws one part's arguments, and reference() takes and returns one part's arrays. A program takes and returns all parts, laid end to end along the dimension named above; an argument that names none is the same for every part. Nothing has to cross between parts.
Inputs may be any that keep to these rules, and one draw needn't show every extreme that they name: fold_partner pairs the columns: fold_partner[fold_partner[i]] = i and fold_partner[i] != i.
All inputs are finite; a program needn't handle non-finite values. No bound on the sum of `land_sea` on one device may be relied on, other than what follows from the above.
Results may differ from the reference program's by a relative error of at most 0.00002.
Values sent between devices are 32-bit elements; how exact they have to be, the bound alone decides.
No kernel may reach another device: no remote copies, remote signals or barrier semaphores. Data moves between devices by JAX's collectives and lax.ppermute only.
A program may use at most 64 MiB of HBM per device.

```python
import math
import jax
import jax.numpy as jnp

LEV = 2
STEPS = 4
NLAT = 640
NLON = 1024


def draw_fold_partner(key, part):
    key = jax.random.fold_in(key, 11)
    order = jax.random.permutation(key, NLON).astype(jnp.int32)
    pairs = order.reshape(NLON // 2, 2)
    partner = jnp.zeros((NLON,), jnp.int32)
    partner = partner.at[pairs[:, 0]].set(pairs[:, 1])
    partner = partner.at[pairs[:, 1]].set(pairs[:, 0])
    return partner


def place_ends(entries, stream_key, low, high):
    longest = entries.shape.index(max(entries.shape))
    spots = []
    for shift in (0, 1):
        where = [jax.random.randint(jax.random.fold_in(stream_key, axis), (), 0, length) for axis, length in enumerate(entries.shape)]
        where[longest] = (where[longest] + shift) % entries.shape[longest]
        spots.append(tuple(where))
    return entries.at[spots[0]].set(low).at[spots[1]].set(high)


def block_levels(key, dims, pieces, low, top_value):
    factor_of = 1.0
    for position, parts in pieces:
        draws = jax.random.uniform(jax.random.fold_in(jax.random.fold_in(key, 6), position), (parts,), jnp.float32, low / len(pieces), top_value / len(pieces))
        factor_of = factor_of * jnp.repeat(jnp.exp(draws), dims[position] // parts).reshape((-1,) + (1,) * (len(dims) - 1 - position))
    return factor_of


def scatter_about(rng, dims, width, bound, split=(), kind=jnp.bfloat16):
    level = block_levels(rng, dims, split, -0.22, 0.18) if split else 1.0
    array = jax.random.normal(rng, dims, jnp.float32) * width * level
    return jnp.minimum(jnp.maximum(array, -bound), bound).astype(kind)


def setup_inputs(seed: int = 0, part: int = 0) -> dict:
    splits = jax.random.split(jax.random.key(seed), 9)
    own_keys = jax.random.split(jax.random.fold_in(splits[8], part), 9)
    iterate = scatter_about(own_keys[0], (LEV, NLAT, NLON), 1.0, 6.0, ((1, 2), (2, 8)), jnp.float32)
    residual = scatter_about(own_keys[1], (LEV, NLAT, NLON), 1.0, 6.0, ((1, 2), (2, 8)), jnp.float32)
    direction = scatter_about(own_keys[2], (LEV, NLAT, NLON), 1.0, 6.0, ((1, 2), (2, 8)), jnp.float32)
    land_sea = place_ends((jax.random.randint(splits[3], (LEV, NLAT, NLON), 0, 32) < 31).astype(jnp.int32), jax.random.fold_in(splits[3], 1), 0, 1)
    precision_weight = jnp.clip(jnp.exp(math.log(5.0) - 3.218876 * jax.random.uniform(splits[4], (LEV, NLAT, NLON), jnp.float32) ** block_levels(splits[4], (LEV, NLAT, NLON), ((1, 2), (2, 8)), -0.2, 0.2)), 0.2, 5.0)
    east_kappa = jnp.clip(0.18 + 0.059999987 * jax.random.uniform(splits[5], (NLAT, NLON), jnp.float32) ** block_levels(splits[5], (NLAT, NLON), ((0, 2), (1, 8)), -0.2, 0.2), 0.18, 0.24)
    north_kappa = jnp.clip(0.18 + 0.059999987 * jax.random.uniform(splits[6], (NLAT, NLON), jnp.float32) ** block_levels(splits[6], (NLAT, NLON), ((0, 2), (1, 8)), -0.2, 0.2), 0.18, 0.24)
    fold_partner = draw_fold_partner(jax.random.fold_in(splits[8], 71), part)
    return dict(iterate=iterate, residual=residual, direction=direction, land_sea=land_sea, precision_weight=precision_weight, east_kappa=east_kappa, north_kappa=north_kappa, fold_partner=fold_partner)


def faces(land_sea, east_kappa, north_kappa, fold_partner):
    ocean = land_sea.astype(jnp.float32)
    east_face = east_kappa[None] * ocean * jnp.roll(ocean, -1, axis=2)
    inner = north_kappa[None, :-1] * ocean[:, :-1] * ocean[:, 1:]
    top_kappa = 0.5 * (north_kappa[-1] + north_kappa[-1][fold_partner])
    top_face = top_kappa[None] * ocean[:, -1] * ocean[:, -1][:, fold_partner]
    north_face = jnp.concatenate([inner, top_face[:, None]], axis=1)
    west_face = jnp.roll(east_face, 1, axis=2)
    zero_row = jnp.zeros((ocean.shape[0], 1, ocean.shape[2]), jnp.float32)
    south_face = jnp.concatenate([zero_row, north_face[:, :-1]], axis=1)
    return ocean, east_face, west_face, north_face, south_face


def diffuse(field, coeffs, fold_partner):
    east_face, west_face, north_face, south_face = coeffs
    east = jnp.roll(field, -1, axis=2)
    west = jnp.roll(field, 1, axis=2)
    north = jnp.concatenate([field[:, 1:], field[:, -1][:, fold_partner][:, None]], axis=1)
    zero_row = jnp.zeros((field.shape[0], 1, field.shape[2]), jnp.float32)
    south = jnp.concatenate([zero_row, field[:, :-1]], axis=1)
    return field + east_face * (east - field) - west_face * (field - west) + north_face * (north - field) - south_face * (field - south)


def reference(iterate, residual, direction, land_sea, precision_weight, east_kappa, north_kappa, fold_partner):
    ocean, east_face, west_face, north_face, south_face = faces(land_sea, east_kappa, north_kappa, fold_partner)
    coeffs = (east_face, west_face, north_face, south_face)
    old_norm = jnp.sum(residual * residual)
    field = ocean * direction
    for step in range(STEPS):
        field = diffuse(field, coeffs, fold_partner)
    field = precision_weight * ocean * field
    for step in range(STEPS):
        field = diffuse(field, coeffs, fold_partner)
    image = direction + ocean * field
    alpha = old_norm / jnp.sum(direction * image)
    new_iterate = iterate + alpha * direction
    new_residual = residual - alpha * image
    new_norm = jnp.sum(new_residual * new_residual)
    new_direction = new_residual + (new_norm / old_norm) * direction
    return new_iterate, new_residual, new_direction
```

```python
import functools

import jax
import jax.numpy as jnp
from jax import lax
from jax.experimental import pallas as pl
from jax.experimental.pallas import tpu as pltpu
from jax.sharding import PartitionSpec as P

STEPS = 4
HALO = 2 * STEPS
LANES = 128
VMEM_LIMIT = 48 * 1024 * 1024
f32 = jnp.float32


def turn(value, shift, axis=1):
    shift = shift % value.shape[axis]
    return value if shift == 0 else pltpu.roll(value, shift, axis)


def lanes_of(shape):
    return lax.broadcasted_iota(jnp.int32, shape, 1)


def place(kind, level, half):
    return 8 * kind + 32 * half + 64 * level


def pack_kernel(lon_axis, lat_axis, d, sea, pw, ek, nk, strip, rows_out, pay1, pay2):
    rows = d.shape[1]
    groups = rows // 8
    half_groups = groups // 2
    even = lax.axis_index(lon_axis) % 2 == 0
    top = lax.axis_index(lat_axis) == 1

    def plane(index, row):
        at = pl.ds(row, 8)
        if index < 2:
            return d[index, at, :]
        if index < 4:
            return sea[index - 2, at, :].astype(f32)
        if index < 6:
            return pw[index - 4, at, :]
        return (ek, nk)[index - 6][at, :]

    for index in range(8):
        high = plane(index, rows - 8)
        strip[8 * index : 8 * index + 8, :] = high
        rows_out[8 * index : 8 * index + 8, :] = jnp.where(top, plane(index, 0), high)
    lane = lanes_of((8, LANES))
    for group in range(half_groups):
        east = jnp.zeros((8, LANES), f32)
        west = jnp.zeros((8, LANES), f32)
        for half in range(2):
            for kind in range(4):
                for level in range(2):
                    at = place(kind, level, half)
                    turned = turn(plane(2 * kind + level, 8 * (group + half * half_groups)), at + 8)
                    east = jnp.where((lane >= at) & (lane < at + 8), turned, east)
                    first = (at + 8) % LANES
                    west = jnp.where((lane >= first) & (lane < first + 8), turned, west)
        pay1[8 * group : 8 * group + 8, :] = jnp.where(even, east, west)
        pay2[8 * group : 8 * group + 8, :] = jnp.where(even, west, east)


def pack(d, sea, pw, ek, nk):
    rows = d.shape[1]
    full = pl.BlockSpec(memory_space=pltpu.VMEM)
    shapes = [(64, LANES), (64, LANES), (rows // 2, LANES), (rows // 2, LANES)]
    return pl.pallas_call(
        functools.partial(pack_kernel, "lon", "lat"),
        out_shape=[jax.ShapeDtypeStruct(s, f32) for s in shapes],
        in_specs=[full] * 5,
        out_specs=[full] * 4,
        compiler_params=pltpu.CompilerParams(vmem_limit_bytes=VMEM_LIMIT),
    )(d, sea, pw, ek, nk)


def image_kernel(
    offsets, lon_axis, lat_axis,
    d, sea, pw, ek, nk, res, gathered_pieces, halo1, halo2, rows_in, corner1, corner2, partner,
    image, stats,
    blocks, folds, face_fold, ocean, weight, field, other, east_c, west_c, north_c, centre,
):
    lon = lax.axis_index(lon_axis)
    lat = lax.axis_index(lat_axis)
    count = len(offsets)
    top = lat == 1
    even = lon % 2 == 0
    rows = d.shape[1]
    groups = rows // 8
    half_groups = groups // 2
    lane = lanes_of((8, LANES))
    zero = jnp.zeros((8, LANES), f32)

    slot = 0
    for piece in gathered_pieces:
        for inside in range(piece.shape[0] // 64):
            block = lax.bitwise_xor(lon, offsets[slot])
            blocks[pl.ds(pl.multiple_of(block * 64, 64), 64), :] = piece[64 * inside : 64 * inside + 64, :]
            slot += 1
    wide = lanes_of((count, LANES))

    def strip_row(index, row):
        return blocks[pl.ds(8 * index + row, count, stride=64), :]

    def strip_east(x):
        moved = turn(x, -1)
        return jnp.where(wide == LANES - 1, turn(moved, -1, 0), moved)

    def strip_west(x):
        moved = turn(x, 1)
        return jnp.where(wide == 0, turn(moved, 1, 0), moved)

    partner_block = partner[...] // LANES
    partner_lane = partner[...] % LANES

    def across(x):
        parts = []
        for first in range(0, count, 8):
            lanes_at = partner_lane[first : first + 8]
            block_at = partner_block[first : first + 8]
            total = jnp.zeros((8, LANES), f32)
            for block in range(count):
                source = jnp.broadcast_to(x[block : block + 1, :], (8, LANES))
                picked = jnp.take_along_axis(source, lanes_at, axis=1)
                total = jnp.where(block_at == block, picked, total)
            parts.append(total)
        return parts[0] if len(parts) == 1 else jnp.concatenate(parts, axis=0)

    @pl.when(top)
    def _():
        east_k = [strip_row(6, r) for r in range(HALO)]
        north_k = [strip_row(7, r) for r in range(HALO)]
        top_k = 0.5 * (north_k[-1] + across(north_k[-1]))
        for level in range(2):
            oc = [strip_row(2 + level, r) for r in range(HALO)]
            u = [strip_row(level, r) * oc[r] for r in range(HALO)]
            e = [east_k[r] * oc[r] * strip_east(oc[r]) for r in range(HALO)]
            w = [strip_west(x) for x in e]
            n = [north_k[r] * oc[r] * oc[r + 1] for r in range(HALO - 1)]
            n.append(top_k * oc[-1] * across(oc[-1]))
            face_fold[level] = n[-1]
            c = [None] + [1.0 - e[r] - w[r] - n[r] - n[r - 1] for r in range(1, HALO)]
            for t in range(HALO):
                if t == STEPS:
                    for r in range(t, HALO):
                        u[r] = strip_row(4 + level, r) * oc[r] * u[r]
                beyond = across(u[-1])
                folds[t, level] = beyond
                if t == HALO - 1:
                    break
                new = list(u)
                for r in range(t + 1, HALO):
                    north = u[r + 1] if r + 1 < HALO else beyond
                    new[r] = (
                        c[r] * u[r] + e[r] * strip_east(u[r]) + w[r] * strip_west(u[r]) + n[r] * north + n[r - 1] * u[r - 1]
                    )
                u = new

    right = (lane % 64) < 32

    def fold_rows(read):
        to_east = lax.rem(lon + 1, count)
        to_west = lax.rem(lon + count - 1, count)
        one = lanes_of((1, LANES))
        here0 = read(0, lon)
        here1 = turn(read(1, lon), 64)
        e0, w0 = read(0, to_east), read(0, to_west)
        e1, w1 = turn(read(1, to_east), 64), turn(read(1, to_west), 64)
        beside = jnp.where(one < 32, e0, jnp.where(one >= 96, w0, jnp.where(one >= 64, e1, w1)))
        return here0, here1, beside

    def east_of(x):
        a, b, s = (turn(v, -1) for v in x)
        return (
            jnp.where(lane == 127, s, a),
            jnp.where(lane == 63, s, b),
            jnp.where(lane == 127, a, jnp.where(lane == 63, b, s)),
        )

    def west_of(x):
        a, b, s = (turn(v, 1) for v in x)
        return (
            jnp.where(lane == 0, s, a),
            jnp.where(lane == 64, s, b),
            jnp.where(lane == 0, a, jnp.where(lane == 64, b, s)),
        )

    def at(group, shift=0):
        return slice(8 + 8 * group + shift, 16 + 8 * group + shift)

    def beside_slabs(from_east, from_west, half):
        out = []
        for kind in range(4):
            r = turn(from_east, -(place(kind, 0, half) + 8))
            w = turn(from_west, 120 - place(kind, 0, half))
            out.append(jnp.where(right, r, w))
        pair = out.pop()
        pair_turned = turn(pair, 64)
        low = (lane < 32) | (lane >= 96)
        out.append(jnp.where(low, pair, pair_turned))
        out.append(jnp.where(low, pair_turned, pair))
        near = (lane % 64 < 8) | (lane % 64 >= 56)
        out[1] = jnp.where(near, out[1], 0.0)
        return out

    def set_group(group, planes, side):
        ek_here, nk_here = planes[6], planes[7]
        d_s = (planes[0], turn(planes[1], 64), side[0])
        oc_s = (planes[2], turn(planes[3], 64), side[1])
        pw_s = (planes[4], turn(planes[5], 64), side[2])
        ek_s = (ek_here, turn(ek_here, 64), side[3])
        nk_s = (nk_here, turn(nk_here, 64), side[4])
        e = [k * o * oe for k, o, oe in zip(ek_s, oc_s, east_of(oc_s))]
        w = west_of(e)
        for s in range(3):
            ocean[s, at(group), :] = oc_s[s]
            field[s, at(group), :] = d_s[s] * oc_s[s]
            weight[s, at(group), :] = pw_s[s] * oc_s[s]
            east_c[s, at(group), :] = e[s]
            west_c[s, at(group), :] = w[s]
            north_c[s, at(group), :] = nk_s[s] * oc_s[s]

    last = groups + 2
    for s in range(3):
        for buffer in (ocean, field, other, north_c):
            buffer[s, 0:8, :] = zero
            buffer[s, 8 + 8 * last : 16 + 8 * last, :] = zero
    for group in range(groups):
        here = slice(8 * group, 8 * group + 8)
        half, inside = divmod(group, half_groups)
        there = slice(8 * inside, 8 * inside + 8)
        a, b = halo1[there, :], halo2[there, :]
        side = beside_slabs(jnp.where(even, a, b), jnp.where(even, b, a), half)
        planes = [d[0, here, :], d[1, here, :], sea[0, here, :].astype(f32), sea[1, here, :].astype(f32),
                  pw[0, here, :], pw[1, here, :], ek[here, :], nk[here, :]]
        set_group(group + 1, planes, side)
    planes = [rows_in[8 * i : 8 * i + 8, :] for i in range(8)]
    a, b = corner1[...], corner2[...]
    from_east, from_west = jnp.where(even, a, b), jnp.where(even, b, a)
    for group, half, used in ((0, 1, top), (groups + 1, 0, jnp.logical_not(top))):
        side = beside_slabs(from_east, from_west, half)
        masked = list(planes)
        masked[2] = jnp.where(used, planes[2], 0.0)
        masked[3] = jnp.where(used, planes[3], 0.0)
        side[1] = jnp.where(used, side[1], 0.0)
        set_group(group, masked, side)

    for group in range(groups + 2):
        for s in range(3):
            north_c[s, at(group), :] = north_c[s, at(group), :] * ocean[s, at(group, 1), :]
    fold_at = 8 + 8 * (groups + 1)

    @pl.when(top)
    def _():
        for s, row in enumerate(fold_rows(lambda level, b: face_fold[level, pl.ds(b, 1), :])):
            north_c[s, fold_at - 1 : fold_at, :] = row

    for group in range(groups + 2):
        for s in range(3):
            here = at(group)
            centre[s, here, :] = (
                1.0 - east_c[s, here, :] - west_c[s, here, :] - north_c[s, here, :] - north_c[s, at(group, -1), :]
            )

    def step(t, source, target):
        @pl.when(top)
        def _():
            for s, row in enumerate(fold_rows(lambda level, b: folds[t, level, pl.ds(b, 1), :])):
                source[s, fold_at : fold_at + 1, :] = row

        for group in range(groups + 2):
            here, up, down = at(group), at(group, 1), at(group, -1)
            u = [source[s, here, :] for s in range(3)]
            e, w = east_of(u), west_of(u)
            for s in range(3):
                target[s, here, :] = (
                    centre[s, here, :] * u[s]
                    + east_c[s, here, :] * e[s]
                    + west_c[s, here, :] * w[s]
                    + north_c[s, here, :] * source[s, up, :]
                    + north_c[s, down, :] * source[s, down, :]
                )

    def half_steps(first):
        def two(i, carry):
            step(first + 2 * i, field, other)
            step(first + 2 * i + 1, other, field)
            return carry

        lax.fori_loop(0, STEPS // 2, two, 0)

    half_steps(0)
    for group in range(groups + 2):
        for s in range(3):
            field[s, at(group), :] = field[s, at(group), :] * weight[s, at(group), :]
    half_steps(STEPS)

    rr = rq = dq = qq = zero
    for group in range(groups):
        here = slice(8 * group, 8 * group + 8)
        for level in range(2):
            u = turn(field[level, at(group + 1), :], 64 * level)
            o = sea[level, here, :].astype(f32)
            dv, rv = d[level, here, :], res[level, here, :]
            q = dv + o * u
            image[level, here, :] = q
            rr, rq, dq, qq = rr + rv * rv, rq + rv * q, dq + dv * q, qq + q * q
    rr, rq, dq, qq = (jnp.sum(x) for x in (rr, rq, dq, qq))
    a0 = jnp.where(qq > 0.0, rq / jnp.where(qq > 0.0, qq, 1.0), 0.0)
    ss = sq = zero
    for group in range(groups):
        here = slice(8 * group, 8 * group + 8)
        for level in range(2):
            q = image[level, here, :]
            s = res[level, here, :] - a0 * q
            ss, sq = ss + s * s, sq + s * q
    ss, sq = jnp.sum(ss), jnp.sum(sq)
    one = lanes_of((1, LANES))
    row = jnp.zeros((1, LANES), f32)
    for index, value in enumerate((rr, dq, ss, sq, qq, a0)):
        row = jnp.where(one == index, value, row)
    stats[...] = row


def image_and_stats(d, sea, pw, ek, nk, res, pieces, offsets, halo1, halo2, rows_in, corner1, corner2, partner):
    levels, rows, columns = d.shape
    count = len(offsets)
    full = pl.BlockSpec(memory_space=pltpu.VMEM)
    extended = (3, rows + 32, LANES)
    inputs = [d, sea, pw, ek, nk, res, *pieces, halo1, halo2, rows_in, corner1, corner2, partner]

    def kernel(*refs):
        head, tail = refs[:6], refs[6 + len(pieces) :]
        image_kernel(offsets, "lon", "lat", *head, refs[6 : 6 + len(pieces)], *tail)

    return pl.pallas_call(
        kernel,
        out_shape=[jax.ShapeDtypeStruct(d.shape, f32), jax.ShapeDtypeStruct((1, LANES), f32)],
        in_specs=[full] * len(inputs),
        out_specs=[full] * 2,
        scratch_shapes=[
            pltpu.VMEM((64 * count, LANES), f32),
            pltpu.VMEM((HALO, 2, count, LANES), f32),
            pltpu.VMEM((2, count, LANES), f32),
        ]
        + [pltpu.VMEM(extended, f32)] * 8,
        compiler_params=pltpu.CompilerParams(vmem_limit_bytes=VMEM_LIMIT),
    )(*inputs)


def swapped(value, axis, distance):
    return lax.ppermute(value, axis, [(i, i ^ distance) for i in range(lax.axis_size(axis))])


def odd_pairs(value, axis):
    count = lax.axis_size(axis)
    pairs = []
    for i in range(1, count, 2):
        pairs += [(i, (i + 1) % count), ((i + 1) % count, i)]
    return lax.ppermute(value, axis, pairs)


def distances(count):
    found = []
    while count > 1:
        count //= 2
        found.append(count)
    return found


def butterfly(value, axis, order):
    pieces, offsets = [value], [0]
    for distance in order:
        whole = pieces[0] if len(pieces) == 1 else jnp.concatenate(pieces, axis=0)
        pieces.append(swapped(whole, axis, distance))
        offsets += [o ^ distance for o in offsets]
    return pieces, offsets


def shards(iterate, residual, direction, land_sea, precision_weight, east_kappa, north_kappa, fold_partner):
    count = lax.axis_size("lon")
    rows = direction.shape[1]
    strip, edge_rows, pay1, pay2 = pack(direction, land_sea, precision_weight, east_kappa, north_kappa)
    halo2 = odd_pairs(pay2, "lon")
    halo1 = swapped(pay1, "lon", 1)
    rows_in = swapped(edge_rows, "lat", 1)
    pieces, offsets = butterfly(strip, "lon", distances(count))
    top = lax.axis_index("lat") == 1
    first = jnp.where(top, 0, rows // 2 - 8)
    edge = lambda halo: lax.dynamic_slice_in_dim(halo, first, 8, axis=0)
    corners = swapped(jnp.concatenate([edge(halo1), edge(halo2)], axis=0), "lat", 1)
    partner = fold_partner.reshape(count, LANES)
    image, stats = image_and_stats(
        direction, land_sea, precision_weight, east_kappa, north_kappa, residual,
        pieces, offsets, halo1, halo2, rows_in, corners[:8], corners[8:], partner,
    )
    both = jnp.concatenate([stats, swapped(stats, "lat", 1)], axis=0)
    parts, _ = butterfly(both, "lon", distances(count)[::-1])
    table = jnp.concatenate(parts, axis=0)
    rr, dq, ss, sq, qq, a0 = (table[:, i] for i in range(6))
    old_norm = jnp.sum(rr)
    alpha = old_norm / jnp.sum(dq)
    t = alpha - a0
    new_norm = jnp.sum(ss + t * (t * qq - 2.0 * sq))
    new_residual = residual - alpha * image
    return (
        iterate + alpha * direction,
        new_residual,
        new_residual + (new_norm / old_norm) * direction,
    )


def solution(mesh):
    field = P("member", "lat", "lon")
    level = P(None, "lat", "lon")
    flat = P("lat", "lon")
    return jax.shard_map(
        shards,
        mesh=mesh,
        in_specs=(field, field, field, level, level, flat, flat, P()),
        out_specs=(field, field, field),
        check_vma=False,
    )
```

```python
import functools

import jax
import jax.numpy as jnp
from jax import lax
from jax.experimental import pallas as pl
from jax.experimental.pallas import tpu as pltpu
from jax.sharding import PartitionSpec as P

STEPS = 4
HALO = 2 * STEPS
LANES = 128
VMEM_LIMIT = 48 * 1024 * 1024
f32 = jnp.float32


def turn(value, shift, axis=1):
    shift = shift % value.shape[axis]
    return value if shift == 0 else pltpu.roll(value, shift, axis)


def lanes_of(shape):
    return lax.broadcasted_iota(jnp.int32, shape, 1)


def place(kind, level, half):
    return 8 * kind + 32 * half + 64 * level


def pack_kernel(
    lon_axis, lat_axis,
    d_hbm, sea_hbm, pw_hbm, ek_hbm, nk_hbm, strip, rows_out, pay1, pay2, d, sea, pw, ek, nk, arrived,
):
    sources, targets = (d_hbm, sea_hbm, pw_hbm, ek_hbm, nk_hbm), (d, sea, pw, ek, nk)
    copies = [pltpu.make_async_copy(a, b, arrived.at[i]) for i, (a, b) in enumerate(zip(sources, targets))]
    for copy in copies:
        copy.start()
    for copy in copies:
        copy.wait()
    rows = d.shape[1]
    groups = rows // 8
    half_groups = groups // 2
    even = lax.axis_index(lon_axis) % 2 == 0
    top = lax.axis_index(lat_axis) == 1

    def plane(index, row):
        at = pl.ds(row, 8)
        if index < 2:
            return d[index, at, :]
        if index < 4:
            return sea[index - 2, at, :].astype(f32)
        if index < 6:
            return pw[index - 4, at, :]
        return (ek, nk)[index - 6][at, :]

    for index in range(8):
        high = plane(index, rows - 8)
        strip[8 * index : 8 * index + 8, :] = high
        rows_out[8 * index : 8 * index + 8, :] = jnp.where(top, plane(index, 0), high)
    lane = lanes_of((8, LANES))
    for group in range(half_groups):
        east = jnp.zeros((8, LANES), f32)
        west = jnp.zeros((8, LANES), f32)
        for half in range(2):
            for kind in range(4):
                for level in range(2):
                    at = place(kind, level, half)
                    turned = turn(plane(2 * kind + level, 8 * (group + half * half_groups)), at + 8)
                    east = jnp.where((lane >= at) & (lane < at + 8), turned, east)
                    first = (at + 8) % LANES
                    west = jnp.where((lane >= first) & (lane < first + 8), turned, west)
        pay1[8 * group : 8 * group + 8, :] = jnp.where(even, east, west)
        pay2[8 * group : 8 * group + 8, :] = jnp.where(even, west, east)


def pack(d, sea, pw, ek, nk):
    rows = d.shape[1]
    full = pl.BlockSpec(memory_space=pltpu.VMEM)
    shapes = [(64, LANES), (64, LANES), (rows // 2, LANES), (rows // 2, LANES)]
    inputs = [pltpu.with_memory_space_constraint(x, pltpu.HBM) for x in (d, sea, pw, ek, nk)]
    return pl.pallas_call(
        functools.partial(pack_kernel, "lon", "lat"),
        out_shape=[jax.ShapeDtypeStruct(s, f32) for s in shapes],
        in_specs=[pl.BlockSpec(memory_space=pltpu.HBM)] * 5,
        out_specs=[full] * 4,
        scratch_shapes=[pltpu.VMEM(x.shape, x.dtype) for x in inputs] + [pltpu.SemaphoreType.DMA((5,))],
        compiler_params=pltpu.CompilerParams(vmem_limit_bytes=VMEM_LIMIT),
    )(*inputs)


def image_kernel(
    offsets, lon_axis, lat_axis,
    d, sea, pw, ek, nk, res, gathered_pieces, halo1, halo2, rows_in, corner1, corner2, partner,
    image, stats,
    blocks, folds, face_fold, ocean, weight, field, other, east_c, west_c, north_c, centre,
):
    lon = lax.axis_index(lon_axis)
    lat = lax.axis_index(lat_axis)
    count = len(offsets)
    top = lat == 1
    even = lon % 2 == 0
    rows = d.shape[1]
    groups = rows // 8
    half_groups = groups // 2
    lane = lanes_of((8, LANES))
    zero = jnp.zeros((8, LANES), f32)

    slot = 0
    for piece in gathered_pieces:
        for inside in range(piece.shape[0] // 64):
            block = lax.bitwise_xor(lon, offsets[slot])
            blocks[pl.ds(pl.multiple_of(block * 64, 64), 64), :] = piece[64 * inside : 64 * inside + 64, :]
            slot += 1
    wide = lanes_of((count, LANES))

    def strip_row(index, row):
        return blocks[pl.ds(8 * index + row, count, stride=64), :]

    def strip_shift(values, to_east):
        step, edge = (-1, LANES - 1) if to_east else (1, 0)
        moved = [turn(x, step) for x in values]
        beside = [turn(x, step, 0) for x in moved]
        return [jnp.where(wide == edge, y, x) for x, y in zip(moved, beside)]

    partner_block = partner[...] >> 7
    partner_lane = partner[...] & (LANES - 1)

    def across(x):
        parts = []
        for first in range(0, count, 8):
            lanes_at = partner_lane[first : first + 8]
            block_at = partner_block[first : first + 8]
            total = jnp.zeros((8, LANES), f32)
            for block in range(count):
                source = jnp.broadcast_to(x[block : block + 1, :], (8, LANES))
                picked = jnp.take_along_axis(source, lanes_at, axis=1)
                total = jnp.where(block_at == block, picked, total)
            parts.append(total)
        return parts[0] if len(parts) == 1 else jnp.concatenate(parts, axis=0)

    @pl.when(top)
    def _():
        east_k = [strip_row(6, r) for r in range(HALO)]
        north_k = [strip_row(7, r) for r in range(HALO)]
        top_k = 0.5 * (north_k[-1] + across(north_k[-1]))
        both = range(2)
        oc = [[strip_row(2 + level, r) for r in range(HALO)] for level in both]
        u = [[strip_row(level, r) * oc[level][r] for r in range(HALO)] for level in both]
        oc_east = strip_shift([x for level in both for x in oc[level]], True)
        e = [[east_k[r] * oc[level][r] * oc_east[HALO * level + r] for r in range(HALO)] for level in both]
        w = strip_shift([x for level in both for x in e[level]], False)
        w = [w[:HALO], w[HALO:]]
        n = [[north_k[r] * oc[level][r] * oc[level][r + 1] for r in range(HALO - 1)] for level in both]
        for level in both:
            n[level].append(top_k * oc[level][-1] * across(oc[level][-1]))
            face_fold[level] = n[level][-1]
        c = [
            [None] + [1.0 - e[level][r] - w[level][r] - n[level][r] - n[level][r - 1] for r in range(1, HALO)]
            for level in both
        ]
        for t in range(HALO):
            if t == STEPS:
                for level in both:
                    for r in range(t, HALO):
                        u[level][r] = strip_row(4 + level, r) * oc[level][r] * u[level][r]
            beyond = [across(u[level][-1]) for level in both]
            for level in both:
                folds[t, level] = beyond[level]
            if t == HALO - 1:
                break
            rest = [(level, r) for level in both for r in range(t + 1, HALO)]
            east = strip_shift([u[level][r] for level, r in rest], True)
            west = strip_shift([u[level][r] for level, r in rest], False)
            new = [list(u[0]), list(u[1])]
            for (level, r), ue, uw in zip(rest, east, west):
                north = u[level][r + 1] if r + 1 < HALO else beyond[level]
                new[level][r] = (
                    c[level][r] * u[level][r]
                    + e[level][r] * ue
                    + w[level][r] * uw
                    + n[level][r] * north
                    + n[level][r - 1] * u[level][r - 1]
                )
            u = new

    right = (lane & 63) < 32
    low = (lane < 32) | (lane >= 96)
    near = ((lane & 63) < 8) | ((lane & 63) >= 56)

    def fold_rows(read):
        to_east = lax.rem(lon + 1, count)
        to_west = lax.rem(lon + count - 1, count)
        one = lanes_of((1, LANES))
        here0 = read(0, lon)
        here1 = turn(read(1, lon), 64)
        e0, w0 = read(0, to_east), read(0, to_west)
        e1, w1 = turn(read(1, to_east), 64), turn(read(1, to_west), 64)
        beside = jnp.where(one < 32, e0, jnp.where(one >= 96, w0, jnp.where(one >= 64, e1, w1)))
        return here0, here1, beside

    def east_of(x):
        a, b, s = (turn(v, -1) for v in x)
        return (
            jnp.where(lane == 127, s, a),
            jnp.where(lane == 63, s, b),
            jnp.where(lane == 127, a, jnp.where(lane == 63, b, s)),
        )

    def west_of(x):
        a, b, s = (turn(v, 1) for v in x)
        return (
            jnp.where(lane == 0, s, a),
            jnp.where(lane == 64, s, b),
            jnp.where(lane == 0, a, jnp.where(lane == 64, b, s)),
        )

    def at(group, shift=0):
        return slice(8 + 8 * group + shift, 16 + 8 * group + shift)

    def beside_slabs(from_east, from_west, half):
        out = []
        for kind, extra in ((0, 0), (1, 0), (2, 0), (3, 0), (3, 64)):
            r = turn(from_east, extra - (place(kind, 0, half) + 8))
            w = turn(from_west, extra + 120 - place(kind, 0, half))
            out.append(jnp.where(right, r, w))
        pair, pair_turned = out[3:]
        out[3:] = [jnp.where(low, pair, pair_turned), jnp.where(low, pair_turned, pair)]
        out[1] = jnp.where(near, out[1], 0.0)
        return out

    def set_group(group, planes, side):
        ek_here, nk_here = planes[6], planes[7]
        d_s = (planes[0], turn(planes[1], 64), side[0])
        oc_s = (planes[2], turn(planes[3], 64), side[1])
        pw_s = (planes[4], turn(planes[5], 64), side[2])
        ek_s = (ek_here, turn(ek_here, 64), side[3])
        nk_s = (nk_here, turn(nk_here, 64), side[4])
        for s in range(3):
            ocean[s, at(group), :] = oc_s[s]
            field[s, at(group), :] = d_s[s] * oc_s[s]
            weight[s, at(group), :] = pw_s[s] * oc_s[s]
            east_c[s, at(group), :] = ek_s[s] * oc_s[s]
            north_c[s, at(group), :] = nk_s[s] * oc_s[s]

    last = groups + 2
    for s in range(3):
        for buffer in (ocean, field, other, north_c):
            buffer[s, 0:8, :] = zero
            buffer[s, 8 + 8 * last : 16 + 8 * last, :] = zero
    for group in range(groups):
        here = slice(8 * group, 8 * group + 8)
        half, inside = divmod(group, half_groups)
        there = slice(8 * inside, 8 * inside + 8)
        a, b = halo1[there, :], halo2[there, :]
        side = beside_slabs(jnp.where(even, a, b), jnp.where(even, b, a), half)
        planes = [d[0, here, :], d[1, here, :], sea[0, here, :].astype(f32), sea[1, here, :].astype(f32),
                  pw[0, here, :], pw[1, here, :], ek[here, :], nk[here, :]]
        set_group(group + 1, planes, side)
    planes = [rows_in[8 * i : 8 * i + 8, :] for i in range(8)]
    a, b = corner1[...], corner2[...]
    from_east, from_west = jnp.where(even, a, b), jnp.where(even, b, a)
    for group, half, used in ((0, 1, top), (groups + 1, 0, jnp.logical_not(top))):
        side = beside_slabs(from_east, from_west, half)
        masked = list(planes)
        masked[2] = jnp.where(used, planes[2], 0.0)
        masked[3] = jnp.where(used, planes[3], 0.0)
        side[1] = jnp.where(used, side[1], 0.0)
        set_group(group, masked, side)

    fold_at = 8 + 8 * (groups + 1)
    for group in range(groups + 2):
        here = at(group)
        oc = [ocean[s, here, :] for s in range(3)]
        half_face = [east_c[s, here, :] for s in range(3)]
        e, w = east_of(oc), west_of(half_face)
        for s in range(3):
            east_c[s, here, :] = half_face[s] * e[s]
            west_c[s, here, :] = oc[s] * w[s]
            north_c[s, here, :] = north_c[s, here, :] * ocean[s, at(group, 1), :]

    @pl.when(top)
    def _():
        for s, row in enumerate(fold_rows(lambda level, b: face_fold[level, pl.ds(b, 1), :])):
            north_c[s, fold_at - 1 : fold_at, :] = row

    for group in range(groups + 2):
        for s in range(3):
            here = at(group)
            centre[s, here, :] = (
                1.0 - east_c[s, here, :] - west_c[s, here, :] - north_c[s, here, :] - north_c[s, at(group, -1), :]
            )

    def step(t, source, target):
        @pl.when(top)
        def _():
            for s, row in enumerate(fold_rows(lambda level, b: folds[t, level, pl.ds(b, 1), :])):
                source[s, fold_at : fold_at + 1, :] = row

        for group in range(groups + 2):
            here, up, down = at(group), at(group, 1), at(group, -1)
            u = [source[s, here, :] for s in range(3)]
            e, w = east_of(u), west_of(u)
            for s in range(3):
                target[s, here, :] = (
                    centre[s, here, :] * u[s]
                    + east_c[s, here, :] * e[s]
                    + west_c[s, here, :] * w[s]
                    + north_c[s, here, :] * source[s, up, :]
                    + north_c[s, down, :] * source[s, down, :]
                )

    def half_steps(first):
        def two(i, carry):
            step(first + 2 * i, field, other)
            step(first + 2 * i + 1, other, field)
            return carry

        lax.fori_loop(0, STEPS // 2, two, 0)

    half_steps(0)
    for group in range(groups + 2):
        for s in range(3):
            field[s, at(group), :] = field[s, at(group), :] * weight[s, at(group), :]
    half_steps(STEPS)

    rr = rq = dq = qq = zero
    for group in range(groups):
        here = slice(8 * group, 8 * group + 8)
        for level in range(2):
            u = turn(field[level, at(group + 1), :], 64 * level)
            o = sea[level, here, :].astype(f32)
            dv, rv = d[level, here, :], res[level, here, :]
            q = dv + o * u
            image[level, here, :] = q
            rr, rq, dq, qq = rr + rv * rv, rq + rv * q, dq + dv * q, qq + q * q
    rr, rq, dq, qq = (jnp.sum(x) for x in (rr, rq, dq, qq))
    a0 = jnp.where(qq > 0.0, rq / jnp.where(qq > 0.0, qq, 1.0), 0.0)
    ss = sq = zero
    for group in range(groups):
        here = slice(8 * group, 8 * group + 8)
        for level in range(2):
            q = image[level, here, :]
            s = res[level, here, :] - a0 * q
            ss, sq = ss + s * s, sq + s * q
    ss, sq = jnp.sum(ss), jnp.sum(sq)
    one = lanes_of((1, LANES))
    row = jnp.zeros((1, LANES), f32)
    for index, value in enumerate((rr, dq, ss, sq, qq, a0)):
        row = jnp.where(one == index, value, row)
    stats[...] = row


def image_and_stats(d, sea, pw, ek, nk, res, pieces, offsets, halo1, halo2, rows_in, corner1, corner2, partner):
    levels, rows, columns = d.shape
    count = len(offsets)
    full = pl.BlockSpec(memory_space=pltpu.VMEM)
    extended = (3, rows + 32, LANES)
    inputs = [d, sea, pw, ek, nk, res, *pieces, halo1, halo2, rows_in, corner1, corner2, partner]

    def kernel(*refs):
        head, tail = refs[:6], refs[6 + len(pieces) :]
        image_kernel(offsets, "lon", "lat", *head, refs[6 : 6 + len(pieces)], *tail)

    return pl.pallas_call(
        kernel,
        out_shape=[jax.ShapeDtypeStruct(d.shape, f32), jax.ShapeDtypeStruct((1, LANES), f32)],
        in_specs=[full] * len(inputs),
        out_specs=[full] * 2,
        scratch_shapes=[
            pltpu.VMEM((64 * count, LANES), f32),
            pltpu.VMEM((HALO, 2, count, LANES), f32),
            pltpu.VMEM((2, count, LANES), f32),
        ]
        + [pltpu.VMEM(extended, f32)] * 8,
        compiler_params=pltpu.CompilerParams(vmem_limit_bytes=VMEM_LIMIT),
    )(*inputs)


def update_kernel(count, *refs):
    parts = refs[:count]
    iterate, res, d, image, iterate_hbm, res_hbm, d_hbm, new_iterate, new_res, new_d, sent = refs[count:]
    table = jnp.concatenate([part[...] for part in parts], axis=0)
    lane = lanes_of(table.shape)
    sums = jnp.sum(table, axis=0, keepdims=True)
    one = lanes_of(sums.shape)
    pick = lambda row, index: jnp.sum(jnp.where(one == index, row, 0.0), axis=1, keepdims=True)
    old_norm = pick(sums, 0)
    alpha = old_norm / pick(sums, 1)
    t = alpha - turn(table, -3)
    norms = table + t * (t * turn(table, -2) - 2.0 * turn(table, -1))
    new_norm = pick(jnp.sum(norms, axis=0, keepdims=True), 2)
    beta = new_norm / old_norm
    rows = d.shape[1]
    pieces = 2
    alpha = jnp.broadcast_to(alpha, (8, LANES))
    beta = jnp.broadcast_to(beta, (8, LANES))
    copies = []
    for level in range(2):
        for piece in range(pieces):
            first, size = piece * (rows // pieces), rows // pieces
            for row in range(first, first + size, 8):
                here = slice(row, row + 8)
                dv = d[level, here, :]
                rv = res[level, here, :] - alpha * image[level, here, :]
                new_iterate[level, here, :] = iterate[level, here, :] + alpha * dv
                new_res[level, here, :] = rv
                new_d[level, here, :] = rv + beta * dv
            for index, (a, b) in enumerate(((new_iterate, iterate_hbm), (new_res, res_hbm), (new_d, d_hbm))):
                part = (level, pl.ds(first, size), slice(None))
                copies.append(pltpu.make_async_copy(a.at[part], b.at[part], sent.at[len(copies)]))
                copies[-1].start()
    for copy in copies:
        copy.wait()


def update(parts, iterate, res, d, image):
    full = pl.BlockSpec(memory_space=pltpu.VMEM)
    return pl.pallas_call(
        functools.partial(update_kernel, len(parts)),
        out_shape=[jax.ShapeDtypeStruct(d.shape, f32)] * 3,
        in_specs=[full] * (len(parts) + 4),
        out_specs=[pl.BlockSpec(memory_space=pltpu.HBM)] * 3,
        scratch_shapes=[pltpu.VMEM(d.shape, f32)] * 3 + [pltpu.SemaphoreType.DMA((12,))],
        compiler_params=pltpu.CompilerParams(vmem_limit_bytes=VMEM_LIMIT),
    )(*parts, iterate, res, d, image)


def swapped(value, axis, distance):
    return lax.ppermute(value, axis, [(i, i ^ distance) for i in range(lax.axis_size(axis))])


def odd_pairs(value, axis):
    count = lax.axis_size(axis)
    pairs = []
    for i in range(1, count, 2):
        pairs += [(i, (i + 1) % count), ((i + 1) % count, i)]
    return lax.ppermute(value, axis, pairs)


def distances(count):
    found = []
    while count > 1:
        count //= 2
        found.append(count)
    return found


def butterfly(value, axis, order):
    pieces, offsets = [value], [0]
    for distance in order:
        whole = pieces[0] if len(pieces) == 1 else jnp.concatenate(pieces, axis=0)
        pieces.append(swapped(whole, axis, distance))
        offsets += [o ^ distance for o in offsets]
    return pieces, offsets


def shards(iterate, residual, direction, land_sea, precision_weight, east_kappa, north_kappa, fold_partner):
    count = lax.axis_size("lon")
    rows = direction.shape[1]
    strip, edge_rows, pay1, pay2 = pack(direction, land_sea, precision_weight, east_kappa, north_kappa)
    halo2 = odd_pairs(pay2, "lon")
    halo1 = swapped(pay1, "lon", 1)
    rows_in = swapped(edge_rows, "lat", 1)
    pieces, offsets = butterfly(strip, "lon", distances(count))
    top = lax.axis_index("lat") == 1
    first = jnp.where(top, 0, rows // 2 - 8)
    edge = lambda halo: lax.dynamic_slice_in_dim(halo, first, 8, axis=0)
    corners = swapped(jnp.concatenate([edge(halo1), edge(halo2)], axis=0), "lat", 1)
    partner = fold_partner.reshape(count, LANES)
    image, stats = image_and_stats(
        direction, land_sea, precision_weight, east_kappa, north_kappa, residual,
        pieces, offsets, halo1, halo2, rows_in, corners[:8], corners[8:], partner,
    )
    both = jnp.concatenate([stats, swapped(stats, "lat", 1)], axis=0)
    parts, _ = butterfly(both, "lon", distances(count)[::-1])
    return tuple(update(parts, iterate, residual, direction, image))


def solution(mesh):
    field = P("member", "lat", "lon")
    level = P(None, "lat", "lon")
    flat = P("lat", "lon")
    return jax.shard_map(
        shards,
        mesh=mesh,
        in_specs=(field, field, field, level, level, flat, flat, P()),
        out_specs=(field, field, field),
        check_vma=False,
    )
```

```python
import functools

import jax
import jax.numpy as jnp
from jax import lax
from jax.experimental import pallas as pl
from jax.experimental.pallas import tpu as pltpu
from jax.sharding import PartitionSpec as P

STEPS = 4
HALO = 2 * STEPS
LANES = 128
VMEM_LIMIT = 24 * 1024 * 1024
PAY_ROWS = 168
STEP_CHUNK = 42
f32 = jnp.float32


def turn(value, shift, axis=1):
    shift = shift % value.shape[axis]
    return value if shift == 0 else pltpu.roll(value, shift, axis)


def lanes_of(shape):
    return lax.broadcasted_iota(jnp.int32, shape, 1)


def place(kind, level, half):
    return 8 * kind + 32 * half + 64 * level


STRIP = 56
STRIP_AT = (0, 8, 16, 24, 48 - STEPS, 52 - STEPS, 32, 40)


def rows_kernel(lat_axis, d, sea, pw, ek, nk, fold, strip, edge, partner, sea_strip, sea_edge, pw_strip, arrived):
    rows = d.shape[1]
    top_rows = pl.ds(rows - 8, 8)
    first = jnp.where(lax.axis_index(lat_axis) == 1, 0, rows - 8)
    edge_rows = pl.ds(pl.multiple_of(first, 8), 8)
    moves = [
        (sea.at[:, top_rows, :], sea_strip),
        (pw.at[:, top_rows, :], pw_strip),
        (sea.at[:, edge_rows, :], sea_edge),
        (d.at[0, top_rows, :], strip.at[0:8]),
        (d.at[1, top_rows, :], strip.at[8:16]),
        (ek.at[top_rows, :], strip.at[32:40]),
        (nk.at[top_rows, :], strip.at[40:48]),
        (d.at[:, edge_rows, :], edge.at[0:2]),
        (pw.at[:, edge_rows, :], edge.at[4:6]),
        (ek.at[edge_rows, :], edge.at[6]),
        (nk.at[edge_rows, :], edge.at[7]),
        (fold, partner),
    ]
    copies = [pltpu.make_async_copy(a, b, arrived.at[i]) for i, (a, b) in enumerate(moves)]
    for copy in copies:
        copy.start()
    for copy in copies:
        copy.wait()
    for level in range(2):
        strip[16 + 8 * level : 24 + 8 * level, :] = sea_strip[level].astype(f32)
    strip[48:56, :] = jnp.concatenate([pw_strip[0, STEPS:, :], pw_strip[1, STEPS:, :]], axis=0)
    edge[2:4] = sea_edge[...].astype(f32)


def rows_to_send(d, sea, pw, ek, nk, fold):
    full = pl.BlockSpec(memory_space=pltpu.VMEM)
    inputs = [pltpu.with_memory_space_constraint(x, pltpu.HBM) for x in (d, sea, pw, ek, nk, fold)]
    return pl.pallas_call(
        functools.partial(rows_kernel, "lat"),
        out_shape=[
            jax.ShapeDtypeStruct((STRIP, LANES), f32),
            jax.ShapeDtypeStruct((8, 8, LANES), f32),
            jax.ShapeDtypeStruct(fold.shape, jnp.int32),
        ],
        in_specs=[pl.BlockSpec(memory_space=pltpu.HBM)] * 6,
        out_specs=[full] * 3,
        scratch_shapes=[
            pltpu.VMEM((2, 8, LANES), jnp.int32),
            pltpu.VMEM((2, 8, LANES), jnp.int32),
            pltpu.VMEM((2, 8, LANES), f32),
            pltpu.SemaphoreType.DMA((12,)),
        ],
        compiler_params=pltpu.CompilerParams(vmem_limit_bytes=VMEM_LIMIT),
    )(*inputs)


def pack_kernel(lon_axis, d, sea, pw, ek, nk, rows_in, strip1, strip2, pay1, pay2, strips):
    strips[:STRIP, :] = strip1[...]
    strips[STRIP:, :] = strip2[...]
    rows = d.shape[1]
    groups = rows // 8
    half_groups = groups // 2
    even = lax.axis_index(lon_axis) % 2 == 0

    def plane(index, group):
        if group == groups:
            return rows_in[index]
        at = pl.ds(8 * group, 8)
        if index < 2:
            return d[index, at, :]
        if index < 4:
            return sea[index - 2, at, :].astype(f32)
        if index < 6:
            return pw[index - 4, at, :]
        return (ek, nk)[index - 6][at, :]

    lane = lanes_of((8, LANES))
    for line in range(half_groups + 1):
        east = jnp.zeros((8, LANES), f32)
        west = jnp.zeros((8, LANES), f32)
        for half, group in enumerate((line, line + half_groups) if line < half_groups else (groups,)):
            for kind in range(4):
                for level in range(2):
                    at = place(kind, level, half)
                    turned = turn(plane(2 * kind + level, group), at + 8)
                    east = jnp.where((lane >= at) & (lane < at + 8), turned, east)
                    first = (at + 8) % LANES
                    west = jnp.where((lane >= first) & (lane < first + 8), turned, west)
        pay1[8 * line : 8 * line + 8, :] = jnp.where(even, east, west)
        pay2[8 * line : 8 * line + 8, :] = jnp.where(even, west, east)


def columns_to_send(d, sea, pw, ek, nk, rows_in, strip1, strip2):
    size = PAY_ROWS
    full = pl.BlockSpec(memory_space=pltpu.VMEM)
    return pl.pallas_call(
        functools.partial(pack_kernel, "lon"),
        out_shape=[jax.ShapeDtypeStruct((size, LANES), f32) for size in (size, size, 2 * STRIP)],
        in_specs=[full] * 8,
        out_specs=[full] * 3,
        compiler_params=pltpu.CompilerParams(vmem_limit_bytes=VMEM_LIMIT),
    )(d, sea, pw, ek, nk, rows_in, strip1, strip2)


def slab_index(group, shift=0):
    if isinstance(group, int):
        return slice(8 + 8 * group + shift, 16 + 8 * group + shift)
    return pl.ds(pl.multiple_of(8 * group, 8) + 8 + shift, 8)


def over_groups(count, chunk, body):
    def turn_of(i, carry):
        for k in range(chunk):
            body(i * chunk + k)
        return carry

    lax.fori_loop(0, count // chunk, turn_of, 0)
    for group in range(count - count % chunk, count):
        body(group)


def east_of(x):
    lane = lanes_of(x[0].shape)
    a, b, s = (turn(v, -1) for v in x)
    return (
        jnp.where(lane == 127, s, a),
        jnp.where(lane == 63, s, b),
        jnp.where(lane == 127, a, jnp.where(lane == 63, b, s)),
    )


def west_of(x):
    lane = lanes_of(x[0].shape)
    a, b, s = (turn(v, 1) for v in x)
    return (
        jnp.where(lane == 0, s, a),
        jnp.where(lane == 64, s, b),
        jnp.where(lane == 0, a, jnp.where(lane == 64, b, s)),
    )


def coefficient_kernel(
    lon_axis, lat_axis, d, sea, pw, ek, nk, halo1, halo2, rows_in, field, weight, east_c, west_c, north_c, centre, ocean
):
    top = lax.axis_index(lat_axis) == 1
    even = lax.axis_index(lon_axis) % 2 == 0
    groups = d.shape[1] // 8
    half_groups = groups // 2
    lane = lanes_of((8, LANES))
    zero = jnp.zeros((8, LANES), f32)
    right = (lane & 63) < 32
    low = (lane < 32) | (lane >= 96)
    near = ((lane & 63) < 8) | ((lane & 63) >= 56)
    at = slab_index

    def beside_slabs(from_east, from_west, half):
        out = []
        for kind, extra in ((0, 0), (1, 0), (2, 0), (3, 0), (3, 64)):
            r = turn(from_east, extra - (place(kind, 0, half) + 8))
            w = turn(from_west, extra + 120 - place(kind, 0, half))
            out.append(jnp.where(right, r, w))
        pair, pair_turned = out[3:]
        out[3:] = [jnp.where(low, pair, pair_turned), jnp.where(low, pair_turned, pair)]
        out[1] = jnp.where(near, out[1], 0.0)
        return out

    def set_group(group, planes, side):
        ek_here, nk_here = planes[6], planes[7]
        d_s = (planes[0], turn(planes[1], 64), side[0])
        oc_s = (planes[2], turn(planes[3], 64), side[1])
        pw_s = (planes[4], turn(planes[5], 64), side[2])
        ek_s = (ek_here, turn(ek_here, 64), side[3])
        nk_s = (nk_here, turn(nk_here, 64), side[4])
        for s in range(3):
            ocean[s, at(group), :] = oc_s[s]
            field[s, at(group), :] = d_s[s] * oc_s[s]
            weight[s, at(group), :] = pw_s[s] * oc_s[s]
            east_c[s, at(group), :] = ek_s[s] * oc_s[s]
            north_c[s, at(group), :] = nk_s[s] * oc_s[s]

    last = groups + 2
    for s in range(3):
        for buffer in (ocean, north_c):
            buffer[s, 0:8, :] = zero
            buffer[s, 8 + 8 * last : 16 + 8 * last, :] = zero
    for group in range(groups):
        here = slice(8 * group, 8 * group + 8)
        half, inside = divmod(group, half_groups)
        there = slice(8 * inside, 8 * inside + 8)
        a, b = halo1[there, :], halo2[there, :]
        side = beside_slabs(jnp.where(even, a, b), jnp.where(even, b, a), half)
        planes = [d[0, here, :], d[1, here, :], sea[0, here, :].astype(f32), sea[1, here, :].astype(f32),
                  pw[0, here, :], pw[1, here, :], ek[here, :], nk[here, :]]
        set_group(group + 1, planes, side)
    planes = [rows_in[i] for i in range(8)]
    corner = slice(8 * half_groups, 8 * half_groups + 8)
    a, b = halo1[corner, :], halo2[corner, :]
    side = beside_slabs(jnp.where(even, a, b), jnp.where(even, b, a), 0)
    for group, used in ((0, top), (groups + 1, jnp.logical_not(top))):
        masked, masked_side = list(planes), list(side)
        masked[2] = jnp.where(used, planes[2], 0.0)
        masked[3] = jnp.where(used, planes[3], 0.0)
        masked_side[1] = jnp.where(used, side[1], 0.0)
        set_group(group, masked, masked_side)

    for group in range(groups + 2):
        here = at(group)
        oc = [ocean[s, here, :] for s in range(3)]
        half_face = [east_c[s, here, :] for s in range(3)]
        e, w = east_of(oc), west_of(half_face)
        for s in range(3):
            east_c[s, here, :] = half_face[s] * e[s]
            west_c[s, here, :] = oc[s] * w[s]
            north_c[s, here, :] = north_c[s, here, :] * ocean[s, at(group, 1), :]

    for group in range(groups + 2):
        for s in range(3):
            here = at(group)
            centre[s, here, :] = (
                1.0 - east_c[s, here, :] - west_c[s, here, :] - north_c[s, here, :] - north_c[s, at(group, -1), :]
            )


def coefficients(d, sea, pw, ek, nk, halo1, halo2, rows_in):
    full = pl.BlockSpec(memory_space=pltpu.VMEM)
    extended = (3, d.shape[1] + 32, LANES)
    return pl.pallas_call(
        functools.partial(coefficient_kernel, "lon", "lat"),
        out_shape=[jax.ShapeDtypeStruct(extended, f32)] * 6,
        in_specs=[full] * 8,
        out_specs=[full] * 6,
        scratch_shapes=[pltpu.VMEM(extended, f32)],
        compiler_params=pltpu.CompilerParams(vmem_limit_bytes=VMEM_LIMIT),
    )(d, sea, pw, ek, nk, halo1, halo2, rows_in)


def image_kernel(
    offsets, lon_axis, lat_axis,
    d, sea, res, first_field, weight, east_c, west_c, north_c, centre, partner, gathered_pieces,
    image, stats,
    blocks, folds, face_fold, field, other,
):
    lon = lax.axis_index(lon_axis)
    count = len(offsets)
    top = lax.axis_index(lat_axis) == 1
    groups = d.shape[1] // 8
    zero = jnp.zeros((8, LANES), f32)
    at = slab_index

    slot = 0
    for piece in gathered_pieces:
        for inside in range(piece.shape[0] // STRIP):
            block = lax.bitwise_xor(lon, offsets[slot])
            blocks[pl.ds(pl.multiple_of(block * STRIP, 8), STRIP), :] = piece[STRIP * inside : STRIP * (inside + 1), :]
            slot += 1
    wide = lanes_of((count, LANES))

    def strip_row(index, row):
        return blocks[pl.ds(STRIP_AT[index] + row, count, stride=STRIP), :]

    def strip_shift(values, to_east):
        step, edge = (-1, LANES - 1) if to_east else (1, 0)
        moved = [turn(x, step) for x in values]
        beside = [turn(x, step, 0) for x in moved]
        return [jnp.where(wide == edge, y, x) for x, y in zip(moved, beside)]

    partner_block = partner[...] >> 7
    partner_lane = partner[...] & (LANES - 1)

    def across(x):
        parts = []
        for first in range(0, count, 8):
            lanes_at = partner_lane[first : first + 8]
            block_at = partner_block[first : first + 8]
            total = jnp.zeros((8, LANES), f32)
            for block in range(count):
                source = jnp.broadcast_to(x[block : block + 1, :], (8, LANES))
                picked = jnp.take_along_axis(source, lanes_at, axis=1)
                total = jnp.where(block_at == block, picked, total)
            parts.append(total)
        return parts[0] if len(parts) == 1 else jnp.concatenate(parts, axis=0)

    @pl.when(top)
    def _():
        east_k = [strip_row(6, r) for r in range(HALO)]
        north_k = [strip_row(7, r) for r in range(HALO)]
        top_k = 0.5 * (north_k[-1] + across(north_k[-1]))
        both = range(2)
        oc = [[strip_row(2 + level, r) for r in range(HALO)] for level in both]
        u = [[strip_row(level, r) * oc[level][r] for r in range(HALO)] for level in both]
        oc_east = strip_shift([x for level in both for x in oc[level]], True)
        e = [[east_k[r] * oc[level][r] * oc_east[HALO * level + r] for r in range(HALO)] for level in both]
        w = strip_shift([x for level in both for x in e[level]], False)
        w = [w[:HALO], w[HALO:]]
        n = [[north_k[r] * oc[level][r] * oc[level][r + 1] for r in range(HALO - 1)] for level in both]
        for level in both:
            n[level].append(top_k * oc[level][-1] * across(oc[level][-1]))
            face_fold[level] = n[level][-1]
        c = [
            [None] + [1.0 - e[level][r] - w[level][r] - n[level][r] - n[level][r - 1] for r in range(1, HALO)]
            for level in both
        ]
        for t in range(HALO):
            if t == STEPS:
                for level in both:
                    for r in range(t, HALO):
                        u[level][r] = strip_row(4 + level, r) * oc[level][r] * u[level][r]
            beyond = [across(u[level][-1]) for level in both]
            for level in both:
                folds[t, level] = beyond[level]
            if t == HALO - 1:
                break
            rest = [(level, r) for level in both for r in range(t + 1, HALO)]
            east = strip_shift([u[level][r] for level, r in rest], True)
            west = strip_shift([u[level][r] for level, r in rest], False)
            new = [list(u[0]), list(u[1])]
            for (level, r), ue, uw in zip(rest, east, west):
                north = u[level][r + 1] if r + 1 < HALO else beyond[level]
                new[level][r] = (
                    c[level][r] * u[level][r]
                    + e[level][r] * ue
                    + w[level][r] * uw
                    + n[level][r] * north
                    + n[level][r - 1] * u[level][r - 1]
                )
            u = new

    def fold_rows(read):
        to_east = lax.rem(lon + 1, count)
        to_west = lax.rem(lon + count - 1, count)
        one = lanes_of((1, LANES))
        here0 = read(0, lon)
        here1 = turn(read(1, lon), 64)
        e0, w0 = read(0, to_east), read(0, to_west)
        e1, w1 = turn(read(1, to_east), 64), turn(read(1, to_west), 64)
        beside = jnp.where(one < 32, e0, jnp.where(one >= 96, w0, jnp.where(one >= 64, e1, w1)))
        return here0, here1, beside

    last = groups + 2
    fold_at = 8 + 8 * (groups + 1)
    for s in range(3):
        for buffer in (field, other):
            buffer[s, 0:8, :] = zero
            buffer[s, 8 + 8 * last : 16 + 8 * last, :] = zero
        for group in range(groups + 2):
            field[s, at(group), :] = first_field[s, at(group), :]

    def step(t, source, target):
        def one_group(group):
            here, up, down = at(group), at(group, 1), at(group, -1)
            u = [source[s, here, :] for s in range(3)]
            e, w = east_of(u), west_of(u)
            for s in range(3):
                target[s, here, :] = (
                    centre[s, here, :] * u[s]
                    + east_c[s, here, :] * e[s]
                    + west_c[s, here, :] * w[s]
                    + north_c[s, here, :] * source[s, up, :]
                    + north_c[s, down, :] * source[s, down, :]
                )

        over_groups(groups + 2, STEP_CHUNK, one_group)

        @pl.when(top)
        def _():
            face = fold_rows(lambda level, b: face_fold[level, pl.ds(b, 1), :])
            beyond = fold_rows(lambda level, b: folds[t, level, pl.ds(b, 1), :])
            row = slice(fold_at - 1, fold_at)
            for s in range(3):
                target[s, row, :] = target[s, row, :] + face[s] * (beyond[s] - source[s, row, :])

    def two_steps(i, carry):
        @pl.when(2 * i == STEPS)
        def _():
            for group in range(groups + 2):
                for s in range(3):
                    field[s, at(group), :] = field[s, at(group), :] * weight[s, at(group), :]

        step(2 * i, field, other)
        step(2 * i + 1, other, field)
        return carry

    lax.fori_loop(0, STEPS, two_steps, 0)

    rr = rq = dq = qq = zero
    for group in range(groups):
        here = slice(8 * group, 8 * group + 8)
        for level in range(2):
            u = turn(field[level, at(group + 1), :], 64 * level)
            o = sea[level, here, :].astype(f32)
            dv, rv = d[level, here, :], res[level, here, :]
            q = dv + o * u
            image[level, here, :] = q
            rr, rq, dq, qq = rr + rv * rv, rq + rv * q, dq + dv * q, qq + q * q
    rr, rq, dq, qq = (jnp.sum(x) for x in (rr, rq, dq, qq))
    a0 = jnp.where(qq > 0.0, rq / jnp.where(qq > 0.0, qq, 1.0), 0.0)
    ss = sq = zero
    for group in range(groups):
        here = slice(8 * group, 8 * group + 8)
        for level in range(2):
            q = image[level, here, :]
            s = res[level, here, :] - a0 * q
            ss, sq = ss + s * s, sq + s * q
    ss, sq = jnp.sum(ss), jnp.sum(sq)
    one = lanes_of((1, LANES))
    row = jnp.zeros((1, LANES), f32)
    for index, value in enumerate((rr, dq, ss, sq, qq, a0)):
        row = jnp.where(one == index, value, row)
    stats[...] = row


def image_and_stats(d, sea, res, coeffs, partner, pieces, offsets):
    count = len(offsets)
    full = pl.BlockSpec(memory_space=pltpu.VMEM)
    extended = coeffs[0].shape
    inputs = [d, sea, res, *coeffs, partner, *pieces]

    def kernel(*refs):
        image_kernel(offsets, "lon", "lat", *refs[:10], refs[10 : len(inputs)], *refs[len(inputs) :])

    return pl.pallas_call(
        kernel,
        out_shape=[jax.ShapeDtypeStruct(d.shape, f32), jax.ShapeDtypeStruct((1, LANES), f32)],
        in_specs=[full] * len(inputs),
        out_specs=[full] * 2,
        scratch_shapes=[
            pltpu.VMEM((STRIP * count, LANES), f32),
            pltpu.VMEM((HALO, 2, count, LANES), f32),
            pltpu.VMEM((2, count, LANES), f32),
            pltpu.VMEM(extended, f32),
            pltpu.VMEM(extended, f32),
        ],
        compiler_params=pltpu.CompilerParams(vmem_limit_bytes=VMEM_LIMIT),
    )(*inputs)


def update_kernel(count, *refs):
    parts = refs[:count]
    iterate, res, d, image, iterate_hbm, res_hbm, d_hbm, new_iterate, new_res, new_d, sent = refs[count:]
    table = jnp.concatenate([part[...] for part in parts], axis=0)
    lane = lanes_of(table.shape)
    sums = jnp.sum(table, axis=0, keepdims=True)
    one = lanes_of(sums.shape)
    pick = lambda row, index: jnp.sum(jnp.where(one == index, row, 0.0), axis=1, keepdims=True)
    old_norm = pick(sums, 0)
    alpha = old_norm / pick(sums, 1)
    t = alpha - turn(table, -3)
    norms = table + t * (t * turn(table, -2) - 2.0 * turn(table, -1))
    new_norm = pick(jnp.sum(norms, axis=0, keepdims=True), 2)
    beta = new_norm / old_norm
    rows = d.shape[1]
    pieces = 2
    alpha = jnp.broadcast_to(alpha, (8, LANES))
    beta = jnp.broadcast_to(beta, (8, LANES))
    copies = []
    for level in range(2):
        for piece in range(pieces):
            first, size = piece * (rows // pieces), rows // pieces
            for row in range(first, first + size, 8):
                here = slice(row, row + 8)
                dv = d[level, here, :]
                rv = res[level, here, :] - alpha * image[level, here, :]
                new_iterate[level, here, :] = iterate[level, here, :] + alpha * dv
                new_res[level, here, :] = rv
                new_d[level, here, :] = rv + beta * dv
            for index, (a, b) in enumerate(((new_iterate, iterate_hbm), (new_res, res_hbm), (new_d, d_hbm))):
                part = (level, pl.ds(first, size), slice(None))
                copies.append(pltpu.make_async_copy(a.at[part], b.at[part], sent.at[len(copies)]))
                copies[-1].start()
    for copy in copies:
        copy.wait()


def update(parts, iterate, res, d, image):
    full = pl.BlockSpec(memory_space=pltpu.VMEM)
    return pl.pallas_call(
        functools.partial(update_kernel, len(parts)),
        out_shape=[jax.ShapeDtypeStruct(d.shape, f32)] * 3,
        in_specs=[full] * (len(parts) + 4),
        out_specs=[pl.BlockSpec(memory_space=pltpu.HBM)] * 3,
        scratch_shapes=[pltpu.VMEM(d.shape, f32)] * 3 + [pltpu.SemaphoreType.DMA((12,))],
        compiler_params=pltpu.CompilerParams(vmem_limit_bytes=VMEM_LIMIT),
    )(*parts, iterate, res, d, image)


def swapped(value, axis, distance):
    return lax.ppermute(value, axis, [(i, i ^ distance) for i in range(lax.axis_size(axis))])


def odd_pairs(value, axis):
    count = lax.axis_size(axis)
    pairs = []
    for i in range(1, count, 2):
        pairs += [(i, (i + 1) % count), ((i + 1) % count, i)]
    return lax.ppermute(value, axis, pairs)


def distances(count):
    found = []
    while count > 1:
        count //= 2
        found.append(count)
    return found


def strip_swap(value, distance):
    members, count, halves = (lax.axis_size(axis) for axis in ("member", "lon", "lat"))
    number = lambda m, i, t: (m * count + i) * halves + t
    other = lambda m, i, t: number(m, i ^ distance, t) if t or members % 2 else number(m ^ 1, i, t)
    places = [(m, i, t) for m in range(members) for i in range(count) for t in range(halves)]
    return lax.ppermute(value, ("member", "lon", "lat"), [(number(*p), other(*p)) for p in places])


def butterfly(pieces, offsets, swap, order):
    pieces, offsets = list(pieces), list(offsets)
    for distance in order:
        whole = pieces[0] if len(pieces) == 1 else jnp.concatenate(pieces, axis=0)
        pieces.append(swap(whole, distance))
        offsets += [o ^ distance for o in offsets]
    return pieces, offsets


def shards(iterate, residual, direction, land_sea, precision_weight, east_kappa, north_kappa, fold_partner):
    count = lax.axis_size("lon")
    fields = (direction, land_sea, precision_weight, east_kappa, north_kappa)
    strip, edge, partner = rows_to_send(*fields, fold_partner.reshape(count, LANES))
    rows_in = swapped(edge, "lat", 1)
    strip2 = strip_swap(strip, count // 2)
    pay1, pay2, strips = columns_to_send(*fields, rows_in, strip, strip2)
    halo2 = odd_pairs(pay2, "lon")
    halo1 = swapped(pay1, "lon", 1)
    rest = distances(count)[1:]
    pieces, offsets = butterfly([strips], [0, count // 2], strip_swap, rest[:-1])
    pieces += [strip_swap(piece, rest[-1]) for piece in pieces]
    offsets += [o ^ rest[-1] for o in offsets]
    coeffs = coefficients(*fields, halo1, halo2, rows_in)
    image, stats = image_and_stats(direction, land_sea, residual, coeffs, partner, pieces, offsets)
    parts, _ = butterfly([stats], [0], lambda value, distance: swapped(value, "lon", distance), distances(count)[::-1])
    parts.append(swapped(jnp.concatenate(parts, axis=0), "lat", 1))
    return tuple(update(parts, iterate, residual, direction, image))


def solution(mesh):
    field = P("member", "lat", "lon")
    level = P(None, "lat", "lon")
    flat = P("lat", "lon")
    return jax.shard_map(
        shards,
        mesh=mesh,
        in_specs=(field, field, field, level, level, flat, flat, P()),
        out_specs=(field, field, field),
        check_vma=False,
    )
```

```python
import functools

import jax
import jax.numpy as jnp
from jax import lax
from jax.experimental import pallas as pl
from jax.experimental.pallas import tpu as pltpu
from jax.sharding import PartitionSpec as P

STEPS = 4
HALO = 2 * STEPS
LANES = 128
VMEM_LIMIT = 24 * 1024 * 1024
PAY_ROWS = 168
STEP_CHUNK = 42
f32 = jnp.float32


def turn(value, shift, axis=1):
    shift = shift % value.shape[axis]
    return value if shift == 0 else pltpu.roll(value, shift, axis)


def lanes_of(shape):
    return lax.broadcasted_iota(jnp.int32, shape, 1)


def place(kind, level, half):
    return 8 * kind + 32 * half + 64 * level


STRIP = 56
STRIP_AT = (0, 8, 16, 24, 48 - STEPS, 52 - STEPS, 32, 40)


def rows_kernel(lat_axis, d, sea, pw, ek, nk, fold, strip, edge, partner, sea_strip, sea_edge, pw_strip, arrived):
    rows = d.shape[1]
    top_rows = pl.ds(rows - 8, 8)
    first = jnp.where(lax.axis_index(lat_axis) == 1, 0, rows - 8)
    edge_rows = pl.ds(pl.multiple_of(first, 8), 8)
    moves = [
        (sea.at[:, top_rows, :], sea_strip),
        (pw.at[:, top_rows, :], pw_strip),
        (sea.at[:, edge_rows, :], sea_edge),
        (d.at[0, top_rows, :], strip.at[0:8]),
        (d.at[1, top_rows, :], strip.at[8:16]),
        (ek.at[top_rows, :], strip.at[32:40]),
        (nk.at[top_rows, :], strip.at[40:48]),
        (d.at[:, edge_rows, :], edge.at[0:2]),
        (pw.at[:, edge_rows, :], edge.at[4:6]),
        (ek.at[edge_rows, :], edge.at[6]),
        (nk.at[edge_rows, :], edge.at[7]),
        (fold, partner),
    ]
    copies = [pltpu.make_async_copy(a, b, arrived.at[i]) for i, (a, b) in enumerate(moves)]
    for copy in copies:
        copy.start()
    for copy in copies:
        copy.wait()
    for level in range(2):
        strip[16 + 8 * level : 24 + 8 * level, :] = sea_strip[level].astype(f32)
    strip[48:56, :] = jnp.concatenate([pw_strip[0, STEPS:, :], pw_strip[1, STEPS:, :]], axis=0)
    edge[2:4] = sea_edge[...].astype(f32)


def rows_to_send(d, sea, pw, ek, nk, fold):
    full = pl.BlockSpec(memory_space=pltpu.VMEM)
    inputs = [pltpu.with_memory_space_constraint(x, pltpu.HBM) for x in (d, sea, pw, ek, nk, fold)]
    return pl.pallas_call(
        functools.partial(rows_kernel, "lat"),
        out_shape=[
            jax.ShapeDtypeStruct((STRIP, LANES), f32),
            jax.ShapeDtypeStruct((8, 8, LANES), f32),
            jax.ShapeDtypeStruct(fold.shape, jnp.int32),
        ],
        in_specs=[pl.BlockSpec(memory_space=pltpu.HBM)] * 6,
        out_specs=[full] * 3,
        scratch_shapes=[
            pltpu.VMEM((2, 8, LANES), jnp.int32),
            pltpu.VMEM((2, 8, LANES), jnp.int32),
            pltpu.VMEM((2, 8, LANES), f32),
            pltpu.SemaphoreType.DMA((12,)),
        ],
        compiler_params=pltpu.CompilerParams(vmem_limit_bytes=VMEM_LIMIT),
    )(*inputs)


def pack_kernel(lon_axis, d, sea, pw, ek, nk, rows_in, strip1, strip2, pay1, pay2, strips):
    strips[:STRIP, :] = strip1[...]
    strips[STRIP:, :] = strip2[...]
    rows = d.shape[1]
    groups = rows // 8
    half_groups = groups // 2
    even = lax.axis_index(lon_axis) % 2 == 0

    def plane(index, group):
        if group == groups:
            return rows_in[index]
        at = pl.ds(8 * group, 8)
        if index < 2:
            return d[index, at, :]
        if index < 4:
            return sea[index - 2, at, :].astype(f32)
        if index < 6:
            return pw[index - 4, at, :]
        return (ek, nk)[index - 6][at, :]

    lane = lanes_of((8, LANES))
    for line in range(half_groups + 1):
        east = jnp.zeros((8, LANES), f32)
        west = jnp.zeros((8, LANES), f32)
        for half, group in enumerate((line, line + half_groups) if line < half_groups else (groups,)):
            for kind in range(4):
                for level in range(2):
                    at = place(kind, level, half)
                    turned = turn(plane(2 * kind + level, group), at + 8)
                    east = jnp.where((lane >= at) & (lane < at + 8), turned, east)
                    first = (at + 8) % LANES
                    west = jnp.where((lane >= first) & (lane < first + 8), turned, west)
        pay1[8 * line : 8 * line + 8, :] = jnp.where(even, east, west)
        pay2[8 * line : 8 * line + 8, :] = jnp.where(even, west, east)


def columns_to_send(d, sea, pw, ek, nk, rows_in, strip1, strip2):
    size = PAY_ROWS
    full = pl.BlockSpec(memory_space=pltpu.VMEM)
    return pl.pallas_call(
        functools.partial(pack_kernel, "lon"),
        out_shape=[jax.ShapeDtypeStruct((size, LANES), f32) for size in (size, size, 2 * STRIP)],
        in_specs=[full] * 8,
        out_specs=[full] * 3,
        compiler_params=pltpu.CompilerParams(vmem_limit_bytes=VMEM_LIMIT),
    )(d, sea, pw, ek, nk, rows_in, strip1, strip2)


def slab_index(group, shift=0):
    if isinstance(group, int):
        return slice(8 + 8 * group + shift, 16 + 8 * group + shift)
    return pl.ds(pl.multiple_of(8 * group, 8) + 8 + shift, 8)


def over_groups(count, chunk, body):
    def turn_of(i, carry):
        for k in range(chunk):
            body(i * chunk + k)
        return carry

    lax.fori_loop(0, count // chunk, turn_of, 0)
    for group in range(count - count % chunk, count):
        body(group)


def east_of(x):
    lane = lanes_of(x[0].shape)
    a, b, s = (turn(v, -1) for v in x)
    return (
        jnp.where(lane == 127, s, a),
        jnp.where(lane == 63, s, b),
        jnp.where(lane == 127, a, jnp.where(lane == 63, b, s)),
    )


def west_of(x):
    lane = lanes_of(x[0].shape)
    a, b, s = (turn(v, 1) for v in x)
    return (
        jnp.where(lane == 0, s, a),
        jnp.where(lane == 64, s, b),
        jnp.where(lane == 0, a, jnp.where(lane == 64, b, s)),
    )


def coefficient_kernel(
    lon_axis, lat_axis, d, sea, pw, ek, nk, halo1, halo2, rows_in, field, weight, east_c, west_c, north_c, centre, ocean
):
    top = lax.axis_index(lat_axis) == 1
    even = lax.axis_index(lon_axis) % 2 == 0
    groups = d.shape[1] // 8
    half_groups = groups // 2
    lane = lanes_of((8, LANES))
    zero = jnp.zeros((8, LANES), f32)
    right = (lane & 63) < 32
    low = (lane < 32) | (lane >= 96)
    near = ((lane & 63) < 8) | ((lane & 63) >= 56)
    at = slab_index

    def beside_slabs(from_east, from_west, half):
        out = []
        for kind, extra in ((0, 0), (1, 0), (2, 0), (3, 0), (3, 64)):
            r = turn(from_east, extra - (place(kind, 0, half) + 8))
            w = turn(from_west, extra + 120 - place(kind, 0, half))
            out.append(jnp.where(right, r, w))
        pair, pair_turned = out[3:]
        out[3:] = [jnp.where(low, pair, pair_turned), jnp.where(low, pair_turned, pair)]
        out[1] = jnp.where(near, out[1], 0.0)
        return out

    def set_group(group, planes, side):
        ek_here, nk_here = planes[6], planes[7]
        d_s = (planes[0], turn(planes[1], 64), side[0])
        oc_s = (planes[2], turn(planes[3], 64), side[1])
        pw_s = (planes[4], turn(planes[5], 64), side[2])
        ek_s = (ek_here, turn(ek_here, 64), side[3])
        nk_s = (nk_here, turn(nk_here, 64), side[4])
        for s in range(3):
            ocean[s, at(group), :] = oc_s[s]
            field[s, at(group), :] = d_s[s] * oc_s[s]
            weight[s, at(group), :] = pw_s[s] * oc_s[s]
            east_c[s, at(group), :] = ek_s[s] * oc_s[s]
            north_c[s, at(group), :] = nk_s[s] * oc_s[s]

    last = groups + 2
    for s in range(3):
        for buffer in (ocean, north_c):
            buffer[s, 0:8, :] = zero
            buffer[s, 8 + 8 * last : 16 + 8 * last, :] = zero
    for group in range(groups):
        here = slice(8 * group, 8 * group + 8)
        half, inside = divmod(group, half_groups)
        there = slice(8 * inside, 8 * inside + 8)
        a, b = halo1[there, :], halo2[there, :]
        side = beside_slabs(jnp.where(even, a, b), jnp.where(even, b, a), half)
        planes = [d[0, here, :], d[1, here, :], sea[0, here, :].astype(f32), sea[1, here, :].astype(f32),
                  pw[0, here, :], pw[1, here, :], ek[here, :], nk[here, :]]
        set_group(group + 1, planes, side)
    planes = [rows_in[i] for i in range(8)]
    corner = slice(8 * half_groups, 8 * half_groups + 8)
    a, b = halo1[corner, :], halo2[corner, :]
    side = beside_slabs(jnp.where(even, a, b), jnp.where(even, b, a), 0)
    for group, used in ((0, top), (groups + 1, jnp.logical_not(top))):
        masked, masked_side = list(planes), list(side)
        masked[2] = jnp.where(used, planes[2], 0.0)
        masked[3] = jnp.where(used, planes[3], 0.0)
        masked_side[1] = jnp.where(used, side[1], 0.0)
        set_group(group, masked, masked_side)

    for group in range(groups + 2):
        here = at(group)
        oc = [ocean[s, here, :] for s in range(3)]
        half_face = [east_c[s, here, :] for s in range(3)]
        e, w = east_of(oc), west_of(half_face)
        for s in range(3):
            east_c[s, here, :] = half_face[s] * e[s]
            west_c[s, here, :] = oc[s] * w[s]
            north_c[s, here, :] = north_c[s, here, :] * ocean[s, at(group, 1), :]

    for group in range(groups + 2):
        for s in range(3):
            here = at(group)
            centre[s, here, :] = (
                1.0 - east_c[s, here, :] - west_c[s, here, :] - north_c[s, here, :] - north_c[s, at(group, -1), :]
            )


def coefficients(d, sea, pw, ek, nk, halo1, halo2, rows_in):
    full = pl.BlockSpec(memory_space=pltpu.VMEM)
    extended = (3, d.shape[1] + 32, LANES)
    return pl.pallas_call(
        functools.partial(coefficient_kernel, "lon", "lat"),
        out_shape=[jax.ShapeDtypeStruct(extended, f32)] * 6,
        in_specs=[full] * 8,
        out_specs=[full] * 6,
        scratch_shapes=[pltpu.VMEM(extended, f32)],
        compiler_params=pltpu.CompilerParams(vmem_limit_bytes=VMEM_LIMIT),
    )(d, sea, pw, ek, nk, halo1, halo2, rows_in)


def image_kernel(
    offsets, lon_axis, lat_axis,
    d, sea, res, first_field, weight, east_c, west_c, north_c, centre, partner, gathered_pieces,
    image, stats,
    blocks, folds, face_fold, field, other,
):
    lon = lax.axis_index(lon_axis)
    count = len(offsets)
    top = lax.axis_index(lat_axis) == 1
    groups = d.shape[1] // 8
    zero = jnp.zeros((8, LANES), f32)
    at = slab_index

    slot = 0
    for piece in gathered_pieces:
        for inside in range(piece.shape[0] // STRIP):
            block = lax.bitwise_xor(lon, offsets[slot])
            blocks[pl.ds(pl.multiple_of(block * STRIP, 8), STRIP), :] = piece[STRIP * inside : STRIP * (inside + 1), :]
            slot += 1
    wide = lanes_of((count, LANES))

    def strip_row(index, row):
        return blocks[pl.ds(STRIP_AT[index] + row, count, stride=STRIP), :]

    def strip_shift(values, to_east):
        step, edge = (-1, LANES - 1) if to_east else (1, 0)
        moved = [turn(x, step) for x in values]
        beside = [turn(x, step, 0) for x in moved]
        return [jnp.where(wide == edge, y, x) for x, y in zip(moved, beside)]

    partner_block = partner[...] >> 7
    partner_lane = partner[...] & (LANES - 1)

    def across(x):
        parts = []
        for first in range(0, count, 8):
            lanes_at = partner_lane[first : first + 8]
            block_at = partner_block[first : first + 8]
            total = jnp.zeros((8, LANES), f32)
            for block in range(count):
                source = jnp.broadcast_to(x[block : block + 1, :], (8, LANES))
                picked = jnp.take_along_axis(source, lanes_at, axis=1)
                total = jnp.where(block_at == block, picked, total)
            parts.append(total)
        return parts[0] if len(parts) == 1 else jnp.concatenate(parts, axis=0)

    @pl.when(top)
    def _():
        east_k = [strip_row(6, r) for r in range(HALO)]
        north_k = [strip_row(7, r) for r in range(HALO)]
        top_k = 0.5 * (north_k[-1] + across(north_k[-1]))
        both = range(2)
        oc = [[strip_row(2 + level, r) for r in range(HALO)] for level in both]
        u = [[strip_row(level, r) * oc[level][r] for r in range(HALO)] for level in both]
        oc_east = strip_shift([x for level in both for x in oc[level]], True)
        e = [[east_k[r] * oc[level][r] * oc_east[HALO * level + r] for r in range(HALO)] for level in both]
        w = strip_shift([x for level in both for x in e[level]], False)
        w = [w[:HALO], w[HALO:]]
        n = [[north_k[r] * oc[level][r] * oc[level][r + 1] for r in range(HALO - 1)] for level in both]
        for level in both:
            n[level].append(top_k * oc[level][-1] * across(oc[level][-1]))
            face_fold[level] = n[level][-1]
        c = [
            [None] + [1.0 - e[level][r] - w[level][r] - n[level][r] - n[level][r - 1] for r in range(1, HALO)]
            for level in both
        ]
        for t in range(HALO):
            if t == STEPS:
                for level in both:
                    for r in range(t, HALO):
                        u[level][r] = strip_row(4 + level, r) * oc[level][r] * u[level][r]
            beyond = [across(u[level][-1]) for level in both]
            for level in both:
                folds[t, level] = beyond[level]
            if t == HALO - 1:
                break
            rest = [(level, r) for level in both for r in range(t + 1, HALO)]
            east = strip_shift([u[level][r] for level, r in rest], True)
            west = strip_shift([u[level][r] for level, r in rest], False)
            new = [list(u[0]), list(u[1])]
            for (level, r), ue, uw in zip(rest, east, west):
                north = u[level][r + 1] if r + 1 < HALO else beyond[level]
                new[level][r] = (
                    c[level][r] * u[level][r]
                    + e[level][r] * ue
                    + w[level][r] * uw
                    + n[level][r] * north
                    + n[level][r - 1] * u[level][r - 1]
                )
            u = new

    def fold_rows(read):
        to_east = lax.rem(lon + 1, count)
        to_west = lax.rem(lon + count - 1, count)
        one = lanes_of((1, LANES))
        here0 = read(0, lon)
        here1 = turn(read(1, lon), 64)
        e0, w0 = read(0, to_east), read(0, to_west)
        e1, w1 = turn(read(1, to_east), 64), turn(read(1, to_west), 64)
        beside = jnp.where(one < 32, e0, jnp.where(one >= 96, w0, jnp.where(one >= 64, e1, w1)))
        return here0, here1, beside

    last = groups + 2
    fold_at = 8 + 8 * (groups + 1)
    for s in range(3):
        for buffer in (field, other):
            buffer[s, 0:8, :] = zero
            buffer[s, 8 + 8 * last : 16 + 8 * last, :] = zero
        for group in range(groups + 2):
            field[s, at(group), :] = first_field[s, at(group), :]

    def step(t, source, target):
        def one_group(group):
            here, up, down = at(group), at(group, 1), at(group, -1)
            u = [source[s, here, :] for s in range(3)]
            e, w = east_of(u), west_of(u)
            for s in range(3):
                target[s, here, :] = (
                    centre[s, here, :] * u[s]
                    + east_c[s, here, :] * e[s]
                    + west_c[s, here, :] * w[s]
                    + north_c[s, here, :] * source[s, up, :]
                    + north_c[s, down, :] * source[s, down, :]
                )

        over_groups(groups + 2, STEP_CHUNK, one_group)

        @pl.when(top)
        def _():
            face = fold_rows(lambda level, b: face_fold[level, pl.ds(b, 1), :])
            beyond = fold_rows(lambda level, b: folds[t, level, pl.ds(b, 1), :])
            row = slice(fold_at - 1, fold_at)
            for s in range(3):
                target[s, row, :] = target[s, row, :] + face[s] * (beyond[s] - source[s, row, :])

    def two_steps(i, carry):
        @pl.when(2 * i == STEPS)
        def _():
            for group in range(groups + 2):
                for s in range(3):
                    field[s, at(group), :] = field[s, at(group), :] * weight[s, at(group), :]

        step(2 * i, field, other)
        step(2 * i + 1, other, field)
        return carry

    lax.fori_loop(0, STEPS, two_steps, 0)

    rr = rq = dq = qq = zero
    for group in range(groups):
        here = slice(8 * group, 8 * group + 8)
        for level in range(2):
            u = turn(field[level, at(group + 1), :], 64 * level)
            o = sea[level, here, :].astype(f32)
            dv, rv = d[level, here, :], res[level, here, :]
            q = dv + o * u
            image[level, here, :] = q
            rr, rq, dq, qq = rr + rv * rv, rq + rv * q, dq + dv * q, qq + q * q
    rr, rq, dq, qq = (jnp.sum(x) for x in (rr, rq, dq, qq))
    a0 = jnp.where(qq > 0.0, rq / jnp.where(qq > 0.0, qq, 1.0), 0.0)
    ss = sq = zero
    for group in range(groups):
        here = slice(8 * group, 8 * group + 8)
        for level in range(2):
            q = image[level, here, :]
            s = res[level, here, :] - a0 * q
            ss, sq = ss + s * s, sq + s * q
    ss, sq = jnp.sum(ss), jnp.sum(sq)
    one = lanes_of((1, LANES))
    row = jnp.zeros((1, LANES), f32)
    for index, value in enumerate((rr, dq, ss, sq, qq, a0)):
        row = jnp.where(one == index, value, row)
    stats[...] = row


def image_and_stats(d, sea, res, coeffs, partner, pieces, offsets):
    count = len(offsets)
    full = pl.BlockSpec(memory_space=pltpu.VMEM)
    extended = coeffs[0].shape
    inputs = [d, sea, res, *coeffs, partner, *pieces]

    def kernel(*refs):
        image_kernel(offsets, "lon", "lat", *refs[:10], refs[10 : len(inputs)], *refs[len(inputs) :])

    return pl.pallas_call(
        kernel,
        out_shape=[jax.ShapeDtypeStruct(d.shape, f32), jax.ShapeDtypeStruct((1, LANES), f32)],
        in_specs=[full] * len(inputs),
        out_specs=[full] * 2,
        scratch_shapes=[
            pltpu.VMEM((STRIP * count, LANES), f32),
            pltpu.VMEM((HALO, 2, count, LANES), f32),
            pltpu.VMEM((2, count, LANES), f32),
            pltpu.VMEM(extended, f32),
            pltpu.VMEM(extended, f32),
        ],
        compiler_params=pltpu.CompilerParams(vmem_limit_bytes=VMEM_LIMIT),
    )(*inputs)


def update_kernel(count, *refs):
    parts = refs[:count]
    iterate, res, d, image, iterate_hbm, res_hbm, d_hbm, new_iterate, new_res, new_d, sent = refs[count:]
    table = jnp.concatenate([part[...] for part in parts], axis=0)
    lane = lanes_of(table.shape)
    sums = jnp.sum(table, axis=0, keepdims=True)
    one = lanes_of(sums.shape)
    pick = lambda row, index: jnp.sum(jnp.where(one == index, row, 0.0), axis=1, keepdims=True)
    old_norm = pick(sums, 0)
    alpha = old_norm / pick(sums, 1)
    t = alpha - turn(table, -3)
    norms = table + t * (t * turn(table, -2) - 2.0 * turn(table, -1))
    new_norm = pick(jnp.sum(norms, axis=0, keepdims=True), 2)
    beta = new_norm / old_norm
    rows = d.shape[1]
    pieces = 2
    alpha = jnp.broadcast_to(alpha, (8, LANES))
    beta = jnp.broadcast_to(beta, (8, LANES))
    copies = []
    for level in range(2):
        for piece in range(pieces):
            first, size = piece * (rows // pieces), rows // pieces
            for row in range(first, first + size, 8):
                here = slice(row, row + 8)
                dv = d[level, here, :]
                rv = res[level, here, :] - alpha * image[level, here, :]
                new_iterate[level, here, :] = iterate[level, here, :] + alpha * dv
                new_res[level, here, :] = rv
                new_d[level, here, :] = rv + beta * dv
            for index, (a, b) in enumerate(((new_iterate, iterate_hbm), (new_res, res_hbm), (new_d, d_hbm))):
                part = (level, pl.ds(first, size), slice(None))
                copies.append(pltpu.make_async_copy(a.at[part], b.at[part], sent.at[len(copies)]))
                copies[-1].start()
    for copy in copies:
        copy.wait()


def update(parts, iterate, res, d, image):
    full = pl.BlockSpec(memory_space=pltpu.VMEM)
    return pl.pallas_call(
        functools.partial(update_kernel, len(parts)),
        out_shape=[jax.ShapeDtypeStruct(d.shape, f32)] * 3,
        in_specs=[full] * (len(parts) + 4),
        out_specs=[pl.BlockSpec(memory_space=pltpu.HBM)] * 3,
        scratch_shapes=[pltpu.VMEM(d.shape, f32)] * 3 + [pltpu.SemaphoreType.DMA((12,))],
        compiler_params=pltpu.CompilerParams(vmem_limit_bytes=VMEM_LIMIT),
    )(*parts, iterate, res, d, image)


def swapped(value, axis, distance):
    return lax.ppermute(value, axis, [(i, i ^ distance) for i in range(lax.axis_size(axis))])


def odd_pairs(value, axis):
    count = lax.axis_size(axis)
    pairs = []
    for i in range(1, count, 2):
        pairs += [(i, (i + 1) % count), ((i + 1) % count, i)]
    return lax.ppermute(value, axis, pairs)


def distances(count):
    found = []
    while count > 1:
        count //= 2
        found.append(count)
    return found


def strip_swap(value, distance, alone=False):
    members, count, halves = (lax.axis_size(axis) for axis in ("member", "lon", "lat"))
    number = lambda m, i, t: (m * count + i) * halves + t
    other = lambda m, i, t: number(m, i ^ distance, t) if t or members % 2 else number(m ^ 1, i, t)
    places = [(m, i, t) for m in range(members) for i in range(count) for t in range(int(alone), halves)]
    return lax.ppermute(value, ("member", "lon", "lat"), [(number(*p), other(*p)) for p in places])


def butterfly(pieces, offsets, swap, order):
    pieces, offsets = list(pieces), list(offsets)
    for distance in order:
        whole = pieces[0] if len(pieces) == 1 else jnp.concatenate(pieces, axis=0)
        pieces.append(swap(whole, distance))
        offsets += [o ^ distance for o in offsets]
    return pieces, offsets


def shards(iterate, residual, direction, land_sea, precision_weight, east_kappa, north_kappa, fold_partner):
    count = lax.axis_size("lon")
    fields = (direction, land_sea, precision_weight, east_kappa, north_kappa)
    strip, edge, partner = rows_to_send(*fields, fold_partner.reshape(count, LANES))
    rows_in = swapped(edge, "lat", 1)
    strip2 = strip_swap(strip, count // 2, True)
    pay1, pay2, strips = columns_to_send(*fields, rows_in, strip, strip2)
    halo2 = odd_pairs(pay2, "lon")
    halo1 = swapped(pay1, "lon", 1)
    rest = distances(count)[1:]
    pieces, offsets = butterfly([strips], [0, count // 2], strip_swap, rest[:-1])
    pieces += [strip_swap(piece, rest[-1]) for piece in pieces]
    offsets += [o ^ rest[-1] for o in offsets]
    coeffs = coefficients(*fields, halo1, halo2, rows_in)
    image, stats = image_and_stats(direction, land_sea, residual, coeffs, partner, pieces, offsets)
    parts, _ = butterfly([stats], [0], lambda value, distance: swapped(value, "lon", distance), distances(count)[::-1])
    parts.append(swapped(jnp.concatenate(parts, axis=0), "lat", 1))
    return tuple(update(parts, iterate, residual, direction, image))


def solution(mesh):
    field = P("member", "lat", "lon")
    level = P(None, "lat", "lon")
    flat = P("lat", "lon")
    return jax.shard_map(
        shards,
        mesh=mesh,
        in_specs=(field, field, field, level, level, flat, flat, P()),
        out_specs=(field, field, field),
        check_vma=False,
    )
```

```python
import functools

import jax
import jax.numpy as jnp
from jax import lax
from jax.experimental import pallas as pl
from jax.experimental.pallas import tpu as pltpu
from jax.sharding import PartitionSpec as P

STEPS = 4
HALO = 2 * STEPS
LANES = 128
VMEM_LIMIT = 24 * 1024 * 1024
PAY_ROWS = 168
f32 = jnp.float32


def turn(value, shift, axis=1):
    shift = shift % value.shape[axis]
    return value if shift == 0 else pltpu.roll(value, shift, axis)


def lanes_of(shape):
    return lax.broadcasted_iota(jnp.int32, shape, 1)


def place(kind, level, half):
    return 8 * kind + 32 * half + 64 * level


STRIP = 56
STRIP_AT = (0, 8, 16, 24, 48 - STEPS, 52 - STEPS, 32, 40)


def rows_kernel(lat_axis, d, sea, pw, ek, nk, fold, strip, edge, partner, sea_strip, sea_edge, pw_strip, arrived):
    rows = d.shape[1]
    top_rows = pl.ds(rows - 8, 8)
    first = jnp.where(lax.axis_index(lat_axis) == 1, 0, rows - 8)
    edge_rows = pl.ds(pl.multiple_of(first, 8), 8)
    moves = [
        (sea.at[:, top_rows, :], sea_strip),
        (pw.at[:, top_rows, :], pw_strip),
        (sea.at[:, edge_rows, :], sea_edge),
        (d.at[0, top_rows, :], strip.at[0:8]),
        (d.at[1, top_rows, :], strip.at[8:16]),
        (ek.at[top_rows, :], strip.at[32:40]),
        (nk.at[top_rows, :], strip.at[40:48]),
        (d.at[:, edge_rows, :], edge.at[0:2]),
        (pw.at[:, edge_rows, :], edge.at[4:6]),
        (ek.at[edge_rows, :], edge.at[6]),
        (nk.at[edge_rows, :], edge.at[7]),
        (fold, partner),
    ]
    copies = [pltpu.make_async_copy(a, b, arrived.at[i]) for i, (a, b) in enumerate(moves)]
    for copy in copies:
        copy.start()
    for copy in copies:
        copy.wait()
    for level in range(2):
        strip[16 + 8 * level : 24 + 8 * level, :] = sea_strip[level].astype(f32)
    strip[48:56, :] = jnp.concatenate([pw_strip[0, STEPS:, :], pw_strip[1, STEPS:, :]], axis=0)
    edge[2:4] = sea_edge[...].astype(f32)


def rows_to_send(d, sea, pw, ek, nk, fold):
    full = pl.BlockSpec(memory_space=pltpu.VMEM)
    inputs = [pltpu.with_memory_space_constraint(x, pltpu.HBM) for x in (d, sea, pw, ek, nk, fold)]
    return pl.pallas_call(
        functools.partial(rows_kernel, "lat"),
        out_shape=[
            jax.ShapeDtypeStruct((STRIP, LANES), f32),
            jax.ShapeDtypeStruct((8, 8, LANES), f32),
            jax.ShapeDtypeStruct(fold.shape, jnp.int32),
        ],
        in_specs=[pl.BlockSpec(memory_space=pltpu.HBM)] * 6,
        out_specs=[full] * 3,
        scratch_shapes=[
            pltpu.VMEM((2, 8, LANES), jnp.int32),
            pltpu.VMEM((2, 8, LANES), jnp.int32),
            pltpu.VMEM((2, 8, LANES), f32),
            pltpu.SemaphoreType.DMA((12,)),
        ],
        compiler_params=pltpu.CompilerParams(vmem_limit_bytes=VMEM_LIMIT),
    )(*inputs)


def pack_kernel(lon_axis, d, sea, pw, ek, nk, rows_in, strip1, strip2, pay1, pay2, strips):
    strips[:STRIP, :] = strip1[...]
    strips[STRIP:, :] = strip2[...]
    rows = d.shape[1]
    groups = rows // 8
    half_groups = groups // 2
    even = lax.axis_index(lon_axis) % 2 == 0

    def plane(index, group):
        if group == groups:
            return rows_in[index]
        at = pl.ds(8 * group, 8)
        if index < 2:
            return d[index, at, :]
        if index < 4:
            return sea[index - 2, at, :].astype(f32)
        if index < 6:
            return pw[index - 4, at, :]
        return (ek, nk)[index - 6][at, :]

    lane = lanes_of((8, LANES))
    for line in range(half_groups + 1):
        east = jnp.zeros((8, LANES), f32)
        west = jnp.zeros((8, LANES), f32)
        for half, group in enumerate((line, line + half_groups) if line < half_groups else (groups,)):
            for kind in range(4):
                for level in range(2):
                    at = place(kind, level, half)
                    turned = turn(plane(2 * kind + level, group), at + 8)
                    east = jnp.where((lane >= at) & (lane < at + 8), turned, east)
                    first = (at + 8) % LANES
                    west = jnp.where((lane >= first) & (lane < first + 8), turned, west)
        pay1[8 * line : 8 * line + 8, :] = jnp.where(even, east, west)
        pay2[8 * line : 8 * line + 8, :] = jnp.where(even, west, east)


def columns_to_send(d, sea, pw, ek, nk, rows_in, strip1, strip2):
    size = PAY_ROWS
    full = pl.BlockSpec(memory_space=pltpu.VMEM)
    return pl.pallas_call(
        functools.partial(pack_kernel, "lon"),
        out_shape=[jax.ShapeDtypeStruct((size, LANES), f32) for size in (size, size, 2 * STRIP)],
        in_specs=[full] * 8,
        out_specs=[full] * 3,
        compiler_params=pltpu.CompilerParams(vmem_limit_bytes=VMEM_LIMIT),
    )(d, sea, pw, ek, nk, rows_in, strip1, strip2)


def slab_index(group, shift=0):
    return slice(8 + 8 * group + shift, 16 + 8 * group + shift)


def east_of(x):
    lane = lanes_of(x[0].shape)
    a, b, s = (turn(v, -1) for v in x)
    return (
        jnp.where(lane == 127, s, a),
        jnp.where(lane == 63, s, b),
        jnp.where(lane == 127, a, jnp.where(lane == 63, b, s)),
    )


def west_of(x):
    lane = lanes_of(x[0].shape)
    a, b, s = (turn(v, 1) for v in x)
    return (
        jnp.where(lane == 0, s, a),
        jnp.where(lane == 64, s, b),
        jnp.where(lane == 0, a, jnp.where(lane == 64, b, s)),
    )


def coefficient_kernel(
    lon_axis, lat_axis, d, sea, pw, ek, nk, halo1, halo2, rows_in, field, weight, east_c, west_c, north_c, ocean
):
    top = lax.axis_index(lat_axis) == 1
    even = lax.axis_index(lon_axis) % 2 == 0
    groups = d.shape[1] // 8
    half_groups = groups // 2
    lane = lanes_of((8, LANES))
    zero = jnp.zeros((8, LANES), f32)
    right = (lane & 63) < 32
    low = (lane < 32) | (lane >= 96)
    near = ((lane & 63) < 8) | ((lane & 63) >= 56)
    at = slab_index

    def beside_slabs(from_east, from_west, half):
        out = []
        for kind, extra in ((0, 0), (1, 0), (2, 0), (3, 0), (3, 64)):
            r = turn(from_east, extra - (place(kind, 0, half) + 8))
            w = turn(from_west, extra + 120 - place(kind, 0, half))
            out.append(jnp.where(right, r, w))
        pair, pair_turned = out[3:]
        out[3:] = [jnp.where(low, pair, pair_turned), jnp.where(low, pair_turned, pair)]
        out[1] = jnp.where(near, out[1], 0.0)
        return out

    def set_group(group, planes, side):
        ek_here, nk_here = planes[6], planes[7]
        d_s = (planes[0], turn(planes[1], 64), side[0])
        oc_s = (planes[2], turn(planes[3], 64), side[1])
        pw_s = (planes[4], turn(planes[5], 64), side[2])
        ek_s = (ek_here, turn(ek_here, 64), side[3])
        nk_s = (nk_here, turn(nk_here, 64), side[4])
        for s in range(3):
            ocean[s, at(group), :] = oc_s[s]
            field[s, at(group), :] = d_s[s] * oc_s[s]
            weight[s, at(group), :] = pw_s[s] * oc_s[s]
            east_c[s, at(group), :] = ek_s[s] * oc_s[s]
            north_c[s, at(group), :] = nk_s[s] * oc_s[s]

    last = groups + 2
    for s in range(3):
        for buffer in (ocean, north_c):
            buffer[s, 0:8, :] = zero
            buffer[s, 8 + 8 * last : 16 + 8 * last, :] = zero
    for group in range(groups):
        here = slice(8 * group, 8 * group + 8)
        half, inside = divmod(group, half_groups)
        there = slice(8 * inside, 8 * inside + 8)
        a, b = halo1[there, :], halo2[there, :]
        side = beside_slabs(jnp.where(even, a, b), jnp.where(even, b, a), half)
        planes = [d[0, here, :], d[1, here, :], sea[0, here, :].astype(f32), sea[1, here, :].astype(f32),
                  pw[0, here, :], pw[1, here, :], ek[here, :], nk[here, :]]
        set_group(group + 1, planes, side)
    planes = [rows_in[i] for i in range(8)]
    corner = slice(8 * half_groups, 8 * half_groups + 8)
    a, b = halo1[corner, :], halo2[corner, :]
    side = beside_slabs(jnp.where(even, a, b), jnp.where(even, b, a), 0)
    for group, used in ((0, top), (groups + 1, jnp.logical_not(top))):
        masked, masked_side = list(planes), list(side)
        masked[2] = jnp.where(used, planes[2], 0.0)
        masked[3] = jnp.where(used, planes[3], 0.0)
        masked_side[1] = jnp.where(used, side[1], 0.0)
        set_group(group, masked, masked_side)

    for group in range(groups + 2):
        here = at(group)
        oc = [ocean[s, here, :] for s in range(3)]
        half_face = [east_c[s, here, :] for s in range(3)]
        e, w = east_of(oc), west_of(half_face)
        for s in range(3):
            east_c[s, here, :] = half_face[s] * e[s]
            west_c[s, here, :] = oc[s] * w[s]
            north_c[s, here, :] = north_c[s, here, :] * ocean[s, at(group, 1), :]


def coefficients(d, sea, pw, ek, nk, halo1, halo2, rows_in):
    full = pl.BlockSpec(memory_space=pltpu.VMEM)
    extended = (3, d.shape[1] + 32, LANES)
    return pl.pallas_call(
        functools.partial(coefficient_kernel, "lon", "lat"),
        out_shape=[jax.ShapeDtypeStruct(extended, f32)] * 5,
        in_specs=[full] * 8,
        out_specs=[full] * 5,
        scratch_shapes=[pltpu.VMEM(extended, f32)],
        compiler_params=pltpu.CompilerParams(vmem_limit_bytes=VMEM_LIMIT),
    )(d, sea, pw, ek, nk, halo1, halo2, rows_in)


def strip_kernel(offsets, lon_axis, lat_axis, partner, gathered_pieces, beyond_out, face_out, blocks):
    lon = lax.axis_index(lon_axis)
    count = len(offsets)

    top = lax.axis_index(lat_axis) == 1

    @pl.when(jnp.logical_not(top))
    def _():
        beyond_out[...] = jnp.zeros(beyond_out.shape, f32)
        face_out[...] = jnp.zeros(face_out.shape, f32)

    @pl.when(top)
    def _():
        strip_steps(lon, count, offsets, partner, gathered_pieces, beyond_out, face_out, blocks)


def strip_steps(lon, count, offsets, partner, gathered_pieces, beyond_out, face_out, blocks):
    slot = 0
    for piece in gathered_pieces:
        for inside in range(piece.shape[0] // STRIP):
            block = lax.bitwise_xor(lon, offsets[slot])
            blocks[pl.ds(pl.multiple_of(block * STRIP, 8), STRIP), :] = piece[STRIP * inside : STRIP * (inside + 1), :]
            slot += 1
    wide = lanes_of((count, LANES))

    def strip_row(index, row):
        return blocks[pl.ds(STRIP_AT[index] + row, count, stride=STRIP), :]

    def strip_shift(values, to_east):
        step, edge = (-1, LANES - 1) if to_east else (1, 0)
        moved = [turn(x, step) for x in values]
        beside = [turn(x, step, 0) for x in moved]
        return [jnp.where(wide == edge, y, x) for x, y in zip(moved, beside)]

    partner_block = partner[...] >> 7
    partner_lane = partner[...] & (LANES - 1)

    def across(x):
        parts = []
        for first in range(0, count, 8):
            lanes_at = partner_lane[first : first + 8]
            block_at = partner_block[first : first + 8]
            total = jnp.zeros((8, LANES), f32)
            for block in range(count):
                source = jnp.broadcast_to(x[block : block + 1, :], (8, LANES))
                picked = jnp.take_along_axis(source, lanes_at, axis=1)
                total = jnp.where(block_at == block, picked, total)
            parts.append(total)
        return parts[0] if len(parts) == 1 else jnp.concatenate(parts, axis=0)

    block_index = lax.broadcasted_iota(jnp.int32, (count, LANES), 0)
    to_east = lax.rem(lon + 1, count)
    to_west = lax.rem(lon + count - 1, count)
    one = lanes_of((1, LANES))
    last_only = lax.broadcasted_iota(jnp.int32, (8, LANES), 0) == 7

    def write_rows(out, values):
        row = lambda level, block: jnp.sum(jnp.where(block_index == block, values[level], 0.0), axis=0, keepdims=True)
        here = [row(level, lon) for level in range(2)]
        east = [row(level, to_east) for level in range(2)]
        west = [row(level, to_west) for level in range(2)]
        turned = [turn(x, 64) for x in (here[1], east[1], west[1])]
        beside = jnp.where(one < 32, east[0], jnp.where(one >= 96, west[0], jnp.where(one >= 64, turned[1], turned[2])))
        for s, value in enumerate((here[0], turned[0], beside)):
            out[8 * s : 8 * s + 8, :] = jnp.where(last_only, jnp.broadcast_to(value, (8, LANES)), 0.0)

    east_k = [strip_row(6, r) for r in range(HALO)]
    north_k = [strip_row(7, r) for r in range(HALO)]
    top_k = 0.5 * (north_k[-1] + across(north_k[-1]))
    both = range(2)
    oc = [[strip_row(2 + level, r) for r in range(HALO)] for level in both]
    u = [[strip_row(level, r) * oc[level][r] for r in range(HALO)] for level in both]
    oc_east = strip_shift([x for level in both for x in oc[level]], True)
    e = [[east_k[r] * oc[level][r] * oc_east[HALO * level + r] for r in range(HALO)] for level in both]
    w = strip_shift([x for level in both for x in e[level]], False)
    w = [w[:HALO], w[HALO:]]
    n = [[north_k[r] * oc[level][r] * oc[level][r + 1] for r in range(HALO - 1)] for level in both]
    for level in both:
        n[level].append(top_k * oc[level][-1] * across(oc[level][-1]))
    write_rows(face_out, [n[0][-1], n[1][-1]])
    c = [
        [None] + [1.0 - e[level][r] - w[level][r] - n[level][r] - n[level][r - 1] for r in range(1, HALO)]
        for level in both
    ]
    for t in range(HALO):
        if t == STEPS:
            for level in both:
                for r in range(t, HALO):
                    u[level][r] = strip_row(4 + level, r) * oc[level][r] * u[level][r]
        beyond = [across(u[level][-1]) for level in both]
        write_rows(beyond_out.at[t], beyond)
        if t == HALO - 1:
            break
        rest = [(level, r) for level in both for r in range(t + 1, HALO)]
        east = strip_shift([u[level][r] for level, r in rest], True)
        west = strip_shift([u[level][r] for level, r in rest], False)
        new = [list(u[0]), list(u[1])]
        for (level, r), ue, uw in zip(rest, east, west):
            north = u[level][r + 1] if r + 1 < HALO else beyond[level]
            new[level][r] = (
                c[level][r] * u[level][r]
                + e[level][r] * ue
                + w[level][r] * uw
                + n[level][r] * north
                + n[level][r - 1] * u[level][r - 1]
            )
        u = new


def strip_rows(partner, pieces, offsets):
    count = len(offsets)
    full = pl.BlockSpec(memory_space=pltpu.VMEM)
    inputs = [partner, *pieces]

    def kernel(partner_ref, *refs):
        strip_kernel(offsets, "lon", "lat", partner_ref, refs[: len(pieces)], *refs[len(pieces) :])

    return pl.pallas_call(
        kernel,
        out_shape=[jax.ShapeDtypeStruct((HALO, 24, LANES), f32), jax.ShapeDtypeStruct((24, LANES), f32)],
        in_specs=[full] * len(inputs),
        out_specs=[full] * 2,
        scratch_shapes=[pltpu.VMEM((STRIP * count, LANES), f32)],
        compiler_params=pltpu.CompilerParams(vmem_limit_bytes=VMEM_LIMIT),
    )(*inputs)


def image_kernel(
    d, sea, res, first_field, weight, east_c, west_c, north_c, beyond, face, image, stats, field, other
):
    groups = d.shape[1] // 8
    zero = jnp.zeros((8, LANES), f32)
    at = slab_index

    first_row = lax.broadcasted_iota(jnp.int32, (8, LANES), 0) == 0
    last = groups + 2
    for s in range(3):
        for buffer in (field, other):
            buffer[s, 0:8, :] = zero
            buffer[s, 8 + 8 * last : 16 + 8 * last, :] = zero
        for group in range(groups + 2):
            field[s, at(group), :] = first_field[s, at(group), :]

    def step(t, source, target):
        before = [zero] * 3
        for group in range(groups + 2):
            here, up = at(group), at(group, 1)
            u = [source[s, here, :] for s in range(3)]
            e, w = east_of(u), west_of(u)
            for s in range(3):
                flux = north_c[s, here, :] * (source[s, up, :] - u[s])
                if group == groups:
                    fold = slice(8 * s, 8 * s + 8)
                    flux = flux + face[fold, :] * (beyond[t, fold, :] - u[s])
                moved = turn(flux, 1, 0)
                below = jnp.where(first_row, before[s], moved)
                before[s] = moved
                target[s, here, :] = (
                    u[s]
                    + east_c[s, here, :] * (e[s] - u[s])
                    - west_c[s, here, :] * (u[s] - w[s])
                    + flux
                    - below
                )

    def two_steps(i, carry):
        @pl.when(2 * i == STEPS)
        def _():
            for group in range(groups + 2):
                for s in range(3):
                    field[s, at(group), :] = field[s, at(group), :] * weight[s, at(group), :]

        step(2 * i, field, other)
        step(2 * i + 1, other, field)
        return carry

    lax.fori_loop(0, STEPS, two_steps, 0)

    rr = rq = dq = qq = zero
    for group in range(groups):
        here = slice(8 * group, 8 * group + 8)
        for level in range(2):
            u = turn(field[level, at(group + 1), :], 64 * level)
            o = sea[level, here, :].astype(f32)
            dv, rv = d[level, here, :], res[level, here, :]
            q = dv + o * u
            image[level, here, :] = q
            rr, rq, dq, qq = rr + rv * rv, rq + rv * q, dq + dv * q, qq + q * q
    rr, rq, dq, qq = (jnp.sum(x) for x in (rr, rq, dq, qq))
    a0 = jnp.where(qq > 0.0, rq / jnp.where(qq > 0.0, qq, 1.0), 0.0)
    ss = sq = zero
    for group in range(groups):
        here = slice(8 * group, 8 * group + 8)
        for level in range(2):
            q = image[level, here, :]
            s = res[level, here, :] - a0 * q
            ss, sq = ss + s * s, sq + s * q
    ss, sq = jnp.sum(ss), jnp.sum(sq)
    one = lanes_of((1, LANES))
    row = jnp.zeros((1, LANES), f32)
    for index, value in enumerate((rr, dq, ss, sq, qq, a0)):
        row = jnp.where(one == index, value, row)
    stats[...] = row


def image_and_stats(d, sea, res, coeffs, beyond, face):
    full = pl.BlockSpec(memory_space=pltpu.VMEM)
    inputs = [d, sea, res, *coeffs, beyond, face]
    return pl.pallas_call(
        image_kernel,
        out_shape=[jax.ShapeDtypeStruct(d.shape, f32), jax.ShapeDtypeStruct((1, LANES), f32)],
        in_specs=[full] * len(inputs),
        out_specs=[full] * 2,
        scratch_shapes=[pltpu.VMEM(coeffs[0].shape, f32)] * 2,
        compiler_params=pltpu.CompilerParams(vmem_limit_bytes=VMEM_LIMIT),
    )(*inputs)


def update_kernel(count, *refs):
    parts = refs[:count]
    iterate, res, d, image, iterate_hbm, res_hbm, d_hbm, new_iterate, new_res, new_d, sent = refs[count:]
    table = jnp.concatenate([part[...] for part in parts], axis=0)
    lane = lanes_of(table.shape)
    sums = jnp.sum(table, axis=0, keepdims=True)
    one = lanes_of(sums.shape)
    pick = lambda row, index: jnp.sum(jnp.where(one == index, row, 0.0), axis=1, keepdims=True)
    old_norm = pick(sums, 0)
    alpha = old_norm / pick(sums, 1)
    t = alpha - turn(table, -3)
    norms = table + t * (t * turn(table, -2) - 2.0 * turn(table, -1))
    new_norm = pick(jnp.sum(norms, axis=0, keepdims=True), 2)
    beta = new_norm / old_norm
    rows = d.shape[1]
    pieces = 2
    alpha = jnp.broadcast_to(alpha, (8, LANES))
    beta = jnp.broadcast_to(beta, (8, LANES))
    copies = []
    for level in range(2):
        for piece in range(pieces):
            first, size = piece * (rows // pieces), rows // pieces
            for row in range(first, first + size, 8):
                here = slice(row, row + 8)
                dv = d[level, here, :]
                rv = res[level, here, :] - alpha * image[level, here, :]
                new_iterate[level, here, :] = iterate[level, here, :] + alpha * dv
                new_res[level, here, :] = rv
                new_d[level, here, :] = rv + beta * dv
            for index, (a, b) in enumerate(((new_iterate, iterate_hbm), (new_res, res_hbm), (new_d, d_hbm))):
                part = (level, pl.ds(first, size), slice(None))
                copies.append(pltpu.make_async_copy(a.at[part], b.at[part], sent.at[len(copies)]))
                copies[-1].start()
    for copy in copies:
        copy.wait()


def update(parts, iterate, res, d, image):
    full = pl.BlockSpec(memory_space=pltpu.VMEM)
    return pl.pallas_call(
        functools.partial(update_kernel, len(parts)),
        out_shape=[jax.ShapeDtypeStruct(d.shape, f32)] * 3,
        in_specs=[full] * (len(parts) + 4),
        out_specs=[pl.BlockSpec(memory_space=pltpu.HBM)] * 3,
        scratch_shapes=[pltpu.VMEM(d.shape, f32)] * 3 + [pltpu.SemaphoreType.DMA((12,))],
        compiler_params=pltpu.CompilerParams(vmem_limit_bytes=VMEM_LIMIT),
    )(*parts, iterate, res, d, image)


def swapped(value, axis, distance):
    return lax.ppermute(value, axis, [(i, i ^ distance) for i in range(lax.axis_size(axis))])


def odd_pairs(value, axis):
    count = lax.axis_size(axis)
    pairs = []
    for i in range(1, count, 2):
        pairs += [(i, (i + 1) % count), ((i + 1) % count, i)]
    return lax.ppermute(value, axis, pairs)


def distances(count):
    found = []
    while count > 1:
        count //= 2
        found.append(count)
    return found


def strip_swap(value, distance, alone=False):
    members, count, halves = (lax.axis_size(axis) for axis in ("member", "lon", "lat"))
    number = lambda m, i, t: (m * count + i) * halves + t
    other = lambda m, i, t: number(m, i ^ distance, t) if t or members % 2 else number(m ^ 1, i, t)
    places = [(m, i, t) for m in range(members) for i in range(count) for t in range(int(alone), halves)]
    return lax.ppermute(value, ("member", "lon", "lat"), [(number(*p), other(*p)) for p in places])


def butterfly(pieces, offsets, swap, order):
    pieces, offsets = list(pieces), list(offsets)
    for distance in order:
        whole = pieces[0] if len(pieces) == 1 else jnp.concatenate(pieces, axis=0)
        pieces.append(swap(whole, distance))
        offsets += [o ^ distance for o in offsets]
    return pieces, offsets


def shards(iterate, residual, direction, land_sea, precision_weight, east_kappa, north_kappa, fold_partner):
    count = lax.axis_size("lon")
    fields = (direction, land_sea, precision_weight, east_kappa, north_kappa)
    strip, edge, partner = rows_to_send(*fields, fold_partner.reshape(count, LANES))
    rows_in = swapped(edge, "lat", 1)
    strip2 = strip_swap(strip, count // 2, True)
    pay1, pay2, strips = columns_to_send(*fields, rows_in, strip, strip2)
    halo2 = odd_pairs(pay2, "lon")
    halo1 = swapped(pay1, "lon", 1)
    rest = distances(count)[1:]
    pieces, offsets = butterfly([strips], [0, count // 2], strip_swap, rest[:-1])
    pieces += [strip_swap(piece, rest[-1]) for piece in pieces]
    offsets += [o ^ rest[-1] for o in offsets]
    coeffs = coefficients(*fields, halo1, halo2, rows_in)
    image, stats = image_and_stats(direction, land_sea, residual, coeffs, *strip_rows(partner, pieces, offsets))
    parts, _ = butterfly([stats], [0], lambda value, distance: swapped(value, "lon", distance), distances(count)[::-1])
    parts.append(swapped(jnp.concatenate(parts, axis=0), "lat", 1))
    return tuple(update(parts, iterate, residual, direction, image))


def solution(mesh):
    field = P("member", "lat", "lon")
    level = P(None, "lat", "lon")
    flat = P("lat", "lon")
    return jax.shard_map(
        shards,
        mesh=mesh,
        in_specs=(field, field, field, level, level, flat, flat, P()),
        out_specs=(field, field, field),
        check_vma=False,
    )
```

```python
import functools

import jax
import jax.numpy as jnp
from jax import lax
from jax.experimental import pallas as pl
from jax.experimental.pallas import tpu as pltpu
from jax.sharding import PartitionSpec as P

STEPS = 4
HALO = 2 * STEPS
LANES = 128
VMEM_LIMIT = 24 * 1024 * 1024
f32 = jnp.float32


def turn(value, shift, axis=1):
    shift = shift % value.shape[axis]
    return value if shift == 0 else pltpu.roll(value, shift, axis)


def lanes_of(shape):
    return lax.broadcasted_iota(jnp.int32, shape, 1)


def place(kind, level, half):
    return 8 * kind + 32 * half + 64 * level


STRIP = 56
STRIP_AT = (0, 8, 16, 24, 48 - STEPS, 52 - STEPS, 32, 40)


def rows_kernel(lat_axis, d, sea, pw, ek, nk, fold, strip, edge, partner, sea_strip, sea_edge, pw_strip, arrived):
    rows = d.shape[1]
    top_rows = pl.ds(rows - 8, 8)
    first = jnp.where(lax.axis_index(lat_axis) == 1, 0, rows - 8)
    edge_rows = pl.ds(pl.multiple_of(first, 8), 8)
    moves = [
        (sea.at[:, top_rows, :], sea_strip),
        (pw.at[:, top_rows, :], pw_strip),
        (sea.at[:, edge_rows, :], sea_edge),
        (d.at[0, top_rows, :], strip.at[0:8]),
        (d.at[1, top_rows, :], strip.at[8:16]),
        (ek.at[top_rows, :], strip.at[32:40]),
        (nk.at[top_rows, :], strip.at[40:48]),
        (d.at[:, edge_rows, :], edge.at[0:2]),
        (pw.at[:, edge_rows, :], edge.at[4:6]),
        (ek.at[edge_rows, :], edge.at[6]),
        (nk.at[edge_rows, :], edge.at[7]),
        (fold, partner),
    ]
    copies = [pltpu.make_async_copy(a, b, arrived.at[i]) for i, (a, b) in enumerate(moves)]
    for copy in copies:
        copy.start()
    for copy in copies:
        copy.wait()
    for level in range(2):
        strip[16 + 8 * level : 24 + 8 * level, :] = sea_strip[level].astype(f32)
    strip[48:56, :] = jnp.concatenate([pw_strip[0, STEPS:, :], pw_strip[1, STEPS:, :]], axis=0)
    edge[2:4] = sea_edge[...].astype(f32)


def rows_to_send(d, sea, pw, ek, nk, fold):
    full = pl.BlockSpec(memory_space=pltpu.VMEM)
    inputs = [pltpu.with_memory_space_constraint(x, pltpu.HBM) for x in (d, sea, pw, ek, nk, fold)]
    return pl.pallas_call(
        functools.partial(rows_kernel, "lat"),
        out_shape=[
            jax.ShapeDtypeStruct((STRIP, LANES), f32),
            jax.ShapeDtypeStruct((8, 8, LANES), f32),
            jax.ShapeDtypeStruct(fold.shape, jnp.int32),
        ],
        in_specs=[pl.BlockSpec(memory_space=pltpu.HBM)] * 6,
        out_specs=[full] * 3,
        scratch_shapes=[
            pltpu.VMEM((2, 8, LANES), jnp.int32),
            pltpu.VMEM((2, 8, LANES), jnp.int32),
            pltpu.VMEM((2, 8, LANES), f32),
            pltpu.SemaphoreType.DMA((12,)),
        ],
        compiler_params=pltpu.CompilerParams(vmem_limit_bytes=VMEM_LIMIT),
    )(*inputs)


def pack_kernel(lon_axis, d, sea, pw, ek, nk, rows_in, *refs):
    *pieces, pay1, pay2, strips = refs
    first = d.shape[1] // 2 + 8
    for target, at in ((strips, 0), (pay1, first), (pay2, first)):
        for piece in pieces:
            size = piece.shape[0]
            target[at : at + size, :] = piece[...]
            at += size
    rows = d.shape[1]
    groups = rows // 8
    half_groups = groups // 2
    even = lax.axis_index(lon_axis) % 2 == 0

    def plane(index, group):
        if group == groups:
            return rows_in[index]
        at = pl.ds(8 * group, 8)
        if index < 2:
            return d[index, at, :]
        if index < 4:
            return sea[index - 2, at, :].astype(f32)
        if index < 6:
            return pw[index - 4, at, :]
        return (ek, nk)[index - 6][at, :]

    lane = lanes_of((8, LANES))
    for line in range(half_groups + 1):
        east = jnp.zeros((8, LANES), f32)
        west = jnp.zeros((8, LANES), f32)
        for half, group in enumerate((line, line + half_groups) if line < half_groups else (groups,)):
            for kind in range(4):
                for level in range(2):
                    at = place(kind, level, half)
                    turned = turn(plane(2 * kind + level, group), at + 8)
                    east = jnp.where((lane >= at) & (lane < at + 8), turned, east)
                    first = (at + 8) % LANES
                    west = jnp.where((lane >= first) & (lane < first + 8), turned, west)
        pay1[8 * line : 8 * line + 8, :] = jnp.where(even, east, west)
        pay2[8 * line : 8 * line + 8, :] = jnp.where(even, west, east)


def columns_to_send(d, sea, pw, ek, nk, rows_in, pieces):
    strips = sum(piece.shape[0] for piece in pieces)
    size = d.shape[1] // 2 + 8 + strips
    full = pl.BlockSpec(memory_space=pltpu.VMEM)
    inputs = (d, sea, pw, ek, nk, rows_in, *pieces)
    return pl.pallas_call(
        functools.partial(pack_kernel, "lon"),
        out_shape=[jax.ShapeDtypeStruct((n, LANES), f32) for n in (size, size, strips)],
        in_specs=[full] * len(inputs),
        out_specs=[full] * 3,
        compiler_params=pltpu.CompilerParams(vmem_limit_bytes=VMEM_LIMIT),
    )(*inputs)


def slab_index(group, shift=0):
    return slice(8 + 8 * group + shift, 16 + 8 * group + shift)


def east_of(x):
    lane = lanes_of(x[0].shape)
    a, b, s = (turn(v, -1) for v in x)
    return (
        jnp.where(lane == 127, s, a),
        jnp.where(lane == 63, s, b),
        jnp.where(lane == 127, a, jnp.where(lane == 63, b, s)),
    )


def west_of(x):
    lane = lanes_of(x[0].shape)
    a, b, s = (turn(v, 1) for v in x)
    return (
        jnp.where(lane == 0, s, a),
        jnp.where(lane == 64, s, b),
        jnp.where(lane == 0, a, jnp.where(lane == 64, b, s)),
    )


def coefficient_kernel(
    lon_axis, lat_axis, d, sea, pw, ek, nk, res, halo1, halo2, rows_in, face_in,
    field, weight, east_c, west_c, north_c, squares, face, ocean,
):
    top = lax.axis_index(lat_axis) == 1
    even = lax.axis_index(lon_axis) % 2 == 0
    groups = d.shape[1] // 8
    half_groups = groups // 2
    lane = lanes_of((8, LANES))
    zero = jnp.zeros((8, LANES), f32)
    right = (lane & 63) < 32
    low = (lane < 32) | (lane >= 96)
    near = ((lane & 63) < 8) | ((lane & 63) >= 56)
    at = slab_index

    def beside_slabs(from_east, from_west, half):
        out = []
        for kind, extra in ((0, 0), (1, 0), (2, 0), (3, 0), (3, 64)):
            r = turn(from_east, extra - (place(kind, 0, half) + 8))
            w = turn(from_west, extra + 120 - place(kind, 0, half))
            out.append(jnp.where(right, r, w))
        pair, pair_turned = out[3:]
        out[3:] = [jnp.where(low, pair, pair_turned), jnp.where(low, pair_turned, pair)]
        out[1] = jnp.where(near, out[1], 0.0)
        return out

    def set_group(group, planes, side):
        ek_here, nk_here = planes[6], planes[7]
        d_s = (planes[0], turn(planes[1], 64), side[0])
        oc_s = (planes[2], turn(planes[3], 64), side[1])
        pw_s = (planes[4], turn(planes[5], 64), side[2])
        ek_s = (ek_here, turn(ek_here, 64), side[3])
        nk_s = (nk_here, turn(nk_here, 64), side[4])
        for s in range(3):
            ocean[s, at(group), :] = oc_s[s]
            field[s, at(group), :] = d_s[s] * oc_s[s]
            weight[s, at(group), :] = pw_s[s] * oc_s[s]
            east_c[s, at(group), :] = ek_s[s] * oc_s[s]
            north_c[s, at(group), :] = nk_s[s] * oc_s[s]

    last = groups + 2
    for s in range(3):
        for buffer in (ocean, north_c):
            buffer[s, 0:8, :] = zero
            buffer[s, 8 + 8 * last : 16 + 8 * last, :] = zero
    for group in range(groups):
        here = slice(8 * group, 8 * group + 8)
        half, inside = divmod(group, half_groups)
        there = slice(8 * inside, 8 * inside + 8)
        a, b = halo1[there, :], halo2[there, :]
        side = beside_slabs(jnp.where(even, a, b), jnp.where(even, b, a), half)
        planes = [d[0, here, :], d[1, here, :], sea[0, here, :].astype(f32), sea[1, here, :].astype(f32),
                  pw[0, here, :], pw[1, here, :], ek[here, :], nk[here, :]]
        set_group(group + 1, planes, side)
    planes = [rows_in[i] for i in range(8)]
    corner = slice(8 * half_groups, 8 * half_groups + 8)
    a, b = halo1[corner, :], halo2[corner, :]
    side = beside_slabs(jnp.where(even, a, b), jnp.where(even, b, a), 0)
    for group, used in ((0, top), (groups + 1, jnp.logical_not(top))):
        masked, masked_side = list(planes), list(side)
        masked[2] = jnp.where(used, planes[2], 0.0)
        masked[3] = jnp.where(used, planes[3], 0.0)
        masked_side[1] = jnp.where(used, side[1], 0.0)
        set_group(group, masked, masked_side)

    total = zero
    for level in range(2):
        for group in range(groups):
            r = res[level, 8 * group : 8 * group + 8, :]
            total = total + r * r
    squares[...] = total
    face[...] = face_in[...]

    for group in range(groups + 2):
        here = at(group)
        oc = [ocean[s, here, :] for s in range(3)]
        half_face = [east_c[s, here, :] for s in range(3)]
        e, w = east_of(oc), west_of(half_face)
        for s in range(3):
            east_c[s, here, :] = half_face[s] * e[s]
            west_c[s, here, :] = oc[s] * w[s]
            north_c[s, here, :] = north_c[s, here, :] * ocean[s, at(group, 1), :]


def coefficients(d, sea, pw, ek, nk, res, halo1, halo2, rows_in, face):
    full = pl.BlockSpec(memory_space=pltpu.VMEM)
    extended = (3, d.shape[1] + 32, LANES)
    return pl.pallas_call(
        functools.partial(coefficient_kernel, "lon", "lat"),
        out_shape=[jax.ShapeDtypeStruct(extended, f32)] * 5
        + [jax.ShapeDtypeStruct((8, LANES), f32), jax.ShapeDtypeStruct(face.shape, f32)],
        in_specs=[full] * 10,
        out_specs=[full] * 7,
        scratch_shapes=[pltpu.VMEM(extended, f32)],
        compiler_params=pltpu.CompilerParams(vmem_limit_bytes=VMEM_LIMIT),
    )(d, sea, pw, ek, nk, res, halo1, halo2, rows_in, face)


def strip_kernel(count, offsets, lon_axis, lat_axis, partner, gathered_pieces, beyond_out, face_out, blocks):
    lon = lax.axis_index(lon_axis)

    top = lax.axis_index(lat_axis) == 1

    @pl.when(jnp.logical_not(top))
    def _():
        beyond_out[...] = jnp.zeros(beyond_out.shape, f32)
        face_out[...] = jnp.zeros(face_out.shape, f32)

    @pl.when(top)
    def _():
        strip_steps(lon, count, offsets, partner, gathered_pieces, beyond_out, face_out, blocks)


def strip_steps(lon, count, offsets, partner, gathered_pieces, beyond_out, face_out, blocks):
    odd = lon % 2
    neighbour = lax.rem(lon + 2 * odd + count - 1, count)
    owners = (lon, lax.bitwise_xor(lon, 2), lax.bitwise_xor(lon, 1), neighbour)
    for piece, owner in zip(gathered_pieces, owners):
        first = piece.shape[0] - STRIP * len(offsets)
        for slot, offset in enumerate(offsets):
            block = lax.bitwise_xor(owner, offset)
            row = first + STRIP * slot
            blocks[pl.ds(pl.multiple_of(block * STRIP, 8), STRIP), :] = piece[row : row + STRIP, :]
    wide = lanes_of((count, LANES))

    def strip_row(index, row):
        return blocks[pl.ds(STRIP_AT[index] + row, count, stride=STRIP), :]

    def strip_shift(values, to_east):
        step, edge = (-1, LANES - 1) if to_east else (1, 0)
        moved = [turn(x, step) for x in values]
        beside = [turn(x, step, 0) for x in moved]
        return [jnp.where(wide == edge, y, x) for x, y in zip(moved, beside)]

    partner_block = partner[...] >> 7
    partner_lane = partner[...] & (LANES - 1)

    def across(x):
        parts = []
        for first in range(0, count, 8):
            lanes_at = partner_lane[first : first + 8]
            block_at = partner_block[first : first + 8]
            total = jnp.zeros((8, LANES), f32)
            for block in range(count):
                source = jnp.broadcast_to(x[block : block + 1, :], (8, LANES))
                picked = jnp.take_along_axis(source, lanes_at, axis=1)
                total = jnp.where(block_at == block, picked, total)
            parts.append(total)
        return parts[0] if len(parts) == 1 else jnp.concatenate(parts, axis=0)

    block_index = lax.broadcasted_iota(jnp.int32, (count, LANES), 0)
    to_east = lax.rem(lon + 1, count)
    to_west = lax.rem(lon + count - 1, count)
    one = lanes_of((1, LANES))
    last_only = lax.broadcasted_iota(jnp.int32, (8, LANES), 0) == 7

    def write_rows(out, values):
        row = lambda level, block: jnp.sum(jnp.where(block_index == block, values[level], 0.0), axis=0, keepdims=True)
        here = [row(level, lon) for level in range(2)]
        east = [row(level, to_east) for level in range(2)]
        west = [row(level, to_west) for level in range(2)]
        turned = [turn(x, 64) for x in (here[1], east[1], west[1])]
        beside = jnp.where(one < 32, east[0], jnp.where(one >= 96, west[0], jnp.where(one >= 64, turned[1], turned[2])))
        for s, value in enumerate((here[0], turned[0], beside)):
            out[8 * s : 8 * s + 8, :] = jnp.where(last_only, jnp.broadcast_to(value, (8, LANES)), 0.0)

    east_k = [strip_row(6, r) for r in range(HALO)]
    north_k = [strip_row(7, r) for r in range(HALO)]
    top_k = 0.5 * (north_k[-1] + across(north_k[-1]))
    both = range(2)
    oc = [[strip_row(2 + level, r) for r in range(HALO)] for level in both]
    u = [[strip_row(level, r) * oc[level][r] for r in range(HALO)] for level in both]
    oc_east = strip_shift([x for level in both for x in oc[level]], True)
    e = [[east_k[r] * oc[level][r] * oc_east[HALO * level + r] for r in range(HALO)] for level in both]
    w = strip_shift([x for level in both for x in e[level]], False)
    w = [w[:HALO], w[HALO:]]
    n = [[north_k[r] * oc[level][r] * oc[level][r + 1] for r in range(HALO - 1)] for level in both]
    for level in both:
        n[level].append(top_k * oc[level][-1] * across(oc[level][-1]))
    write_rows(face_out, [n[0][-1], n[1][-1]])
    c = [
        [None] + [1.0 - e[level][r] - w[level][r] - n[level][r] - n[level][r - 1] for r in range(1, HALO)]
        for level in both
    ]
    for t in range(HALO):
        if t == STEPS:
            for level in both:
                for r in range(t, HALO):
                    u[level][r] = strip_row(4 + level, r) * oc[level][r] * u[level][r]
        beyond = [across(u[level][-1]) for level in both]
        write_rows(beyond_out.at[t], beyond)
        if t == HALO - 1:
            break
        rest = [(level, r) for level in both for r in range(t + 1, HALO)]
        east = strip_shift([u[level][r] for level, r in rest], True)
        west = strip_shift([u[level][r] for level, r in rest], False)
        new = [list(u[0]), list(u[1])]
        for (level, r), ue, uw in zip(rest, east, west):
            north = u[level][r + 1] if r + 1 < HALO else beyond[level]
            new[level][r] = (
                c[level][r] * u[level][r]
                + e[level][r] * ue
                + w[level][r] * uw
                + n[level][r] * north
                + n[level][r - 1] * u[level][r - 1]
            )
        u = new


def strip_rows(partner, pieces, offsets):
    count = partner.shape[0]
    full = pl.BlockSpec(memory_space=pltpu.VMEM)
    inputs = [partner, *pieces]

    def kernel(partner_ref, *refs):
        strip_kernel(count, offsets, "lon", "lat", partner_ref, refs[: len(pieces)], *refs[len(pieces) :])

    return pl.pallas_call(
        kernel,
        out_shape=[jax.ShapeDtypeStruct((HALO, 24, LANES), f32), jax.ShapeDtypeStruct((24, LANES), f32)],
        in_specs=[full] * len(inputs),
        out_specs=[full] * 2,
        scratch_shapes=[pltpu.VMEM((STRIP * count, LANES), f32)],
        compiler_params=pltpu.CompilerParams(vmem_limit_bytes=VMEM_LIMIT),
    )(*inputs)


def image_kernel(
    d, sea, res, squares, first_field, weight, east_c, west_c, north_c, beyond, face, image, stats, field, other
):
    groups = d.shape[1] // 8
    zero = jnp.zeros((8, LANES), f32)
    at = slab_index

    first_row = lax.broadcasted_iota(jnp.int32, (8, LANES), 0) == 0
    last = groups + 2
    for s in range(3):
        for buffer in (field, other):
            buffer[s, 0:8, :] = zero
            buffer[s, 8 + 8 * last : 16 + 8 * last, :] = zero
        for group in range(groups + 2):
            field[s, at(group), :] = first_field[s, at(group), :]

    def step(t, source, target):
        before = [zero] * 3
        for group in range(groups + 2):
            here, up = at(group), at(group, 1)
            u = [source[s, here, :] for s in range(3)]
            e, w = east_of(u), west_of(u)
            for s in range(3):
                flux = north_c[s, here, :] * (source[s, up, :] - u[s])
                if group == groups:
                    fold = slice(8 * s, 8 * s + 8)
                    flux = flux + face[fold, :] * (beyond[t, fold, :] - u[s])
                moved = turn(flux, 1, 0)
                below = jnp.where(first_row, before[s], moved)
                before[s] = moved
                target[s, here, :] = (
                    u[s]
                    + east_c[s, here, :] * (e[s] - u[s])
                    - west_c[s, here, :] * (u[s] - w[s])
                    + flux
                    - below
                )

    def two_steps(i, carry):
        @pl.when(2 * i == STEPS)
        def _():
            for group in range(groups + 2):
                for s in range(3):
                    field[s, at(group), :] = field[s, at(group), :] * weight[s, at(group), :]

        step(2 * i, field, other)
        step(2 * i + 1, other, field)
        return carry

    lax.fori_loop(0, STEPS, two_steps, 0)

    rr, rq, dq, qq = squares[...], zero, zero, zero
    for group in range(groups):
        here = slice(8 * group, 8 * group + 8)
        for level in range(2):
            u = turn(field[level, at(group + 1), :], 64 * level)
            o = sea[level, here, :].astype(f32)
            dv, rv = d[level, here, :], res[level, here, :]
            q = dv + o * u
            image[level, here, :] = q
            rq, dq, qq = rq + rv * q, dq + dv * q, qq + q * q
    rr, rq, dq, qq = (jnp.sum(x) for x in (rr, rq, dq, qq))
    a0 = jnp.where(qq > 0.0, rq / jnp.where(qq > 0.0, qq, 1.0), 0.0)
    ss = sq = zero
    for group in range(groups):
        here = slice(8 * group, 8 * group + 8)
        for level in range(2):
            q = image[level, here, :]
            s = res[level, here, :] - a0 * q
            ss, sq = ss + s * s, sq + s * q
    ss, sq = jnp.sum(ss), jnp.sum(sq)
    one = lanes_of((1, LANES))
    row = jnp.zeros((1, LANES), f32)
    for index, value in enumerate((rr, dq, ss, sq, qq, a0)):
        row = jnp.where(one == index, value, row)
    stats[...] = row


def image_and_stats(d, sea, res, squares, coeffs, beyond, face):
    full = pl.BlockSpec(memory_space=pltpu.VMEM)
    inputs = [d, sea, res, squares, *coeffs, beyond, face]
    return pl.pallas_call(
        image_kernel,
        out_shape=[jax.ShapeDtypeStruct(d.shape, f32), jax.ShapeDtypeStruct((1, LANES), f32)],
        in_specs=[full] * len(inputs),
        out_specs=[full] * 2,
        scratch_shapes=[pltpu.VMEM(coeffs[0].shape, f32)] * 2,
        compiler_params=pltpu.CompilerParams(vmem_limit_bytes=VMEM_LIMIT),
    )(*inputs)


def update_kernel(count, *refs):
    parts = refs[:count]
    iterate, res, d, image, iterate_hbm, res_hbm, d_hbm, new_iterate, new_res, new_d, sent = refs[count:]
    table = jnp.concatenate([part[...] for part in parts], axis=0)
    lane = lanes_of(table.shape)
    sums = jnp.sum(table, axis=0, keepdims=True)
    one = lanes_of(sums.shape)
    pick = lambda row, index: jnp.sum(jnp.where(one == index, row, 0.0), axis=1, keepdims=True)
    old_norm = pick(sums, 0)
    alpha = old_norm / pick(sums, 1)
    t = alpha - turn(table, -3)
    norms = table + t * (t * turn(table, -2) - 2.0 * turn(table, -1))
    new_norm = pick(jnp.sum(norms, axis=0, keepdims=True), 2)
    beta = new_norm / old_norm
    rows = d.shape[1]
    pieces = 2
    alpha = jnp.broadcast_to(alpha, (8, LANES))
    beta = jnp.broadcast_to(beta, (8, LANES))
    copies = []
    for level in range(2):
        for piece in range(pieces):
            first, size = piece * (rows // pieces), rows // pieces
            for row in range(first, first + size, 8):
                here = slice(row, row + 8)
                dv = d[level, here, :]
                rv = res[level, here, :] - alpha * image[level, here, :]
                new_iterate[level, here, :] = iterate[level, here, :] + alpha * dv
                new_res[level, here, :] = rv
                new_d[level, here, :] = rv + beta * dv
            for index, (a, b) in enumerate(((new_iterate, iterate_hbm), (new_res, res_hbm), (new_d, d_hbm))):
                part = (level, pl.ds(first, size), slice(None))
                copies.append(pltpu.make_async_copy(a.at[part], b.at[part], sent.at[len(copies)]))
                copies[-1].start()
    for copy in copies:
        copy.wait()


def update(parts, iterate, res, d, image):
    full = pl.BlockSpec(memory_space=pltpu.VMEM)
    return pl.pallas_call(
        functools.partial(update_kernel, len(parts)),
        out_shape=[jax.ShapeDtypeStruct(d.shape, f32)] * 3,
        in_specs=[full] * (len(parts) + 4),
        out_specs=[pl.BlockSpec(memory_space=pltpu.HBM)] * 3,
        scratch_shapes=[pltpu.VMEM(d.shape, f32)] * 3 + [pltpu.SemaphoreType.DMA((12,))],
        compiler_params=pltpu.CompilerParams(vmem_limit_bytes=VMEM_LIMIT),
    )(*parts, iterate, res, d, image)


def swapped(value, axis, distance):
    return lax.ppermute(value, axis, [(i, i ^ distance) for i in range(lax.axis_size(axis))])


def odd_pairs(value, axis):
    count = lax.axis_size(axis)
    pairs = []
    for i in range(1, count, 2):
        pairs += [(i, (i + 1) % count), ((i + 1) % count, i)]
    return lax.ppermute(value, axis, pairs)


def distances(count):
    found = []
    while count > 1:
        count //= 2
        found.append(count)
    return found


def strip_swap(value, distance, alone=False):
    members, count, halves = (lax.axis_size(axis) for axis in ("member", "lon", "lat"))
    number = lambda m, i, t: (m * count + i) * halves + t
    other = lambda m, i, t: number(m, i ^ distance, t) if t or members % 2 else number(m ^ 1, i, t)
    places = [(m, i, t) for m in range(members) for i in range(count) for t in range(int(alone), halves)]
    return lax.ppermute(value, ("member", "lon", "lat"), [(number(*p), other(*p)) for p in places])


def butterfly(pieces, offsets, swap, order):
    pieces, offsets = list(pieces), list(offsets)
    for distance in order:
        whole = pieces[0] if len(pieces) == 1 else jnp.concatenate(pieces, axis=0)
        pieces.append(swap(whole, distance))
        offsets += [o ^ distance for o in offsets]
    return pieces, offsets


def shards(iterate, residual, direction, land_sea, precision_weight, east_kappa, north_kappa, fold_partner):
    count = lax.axis_size("lon")
    fields = (direction, land_sea, precision_weight, east_kappa, north_kappa)
    strip, edge, partner = rows_to_send(*fields, fold_partner.reshape(count, LANES))
    rows_in = swapped(edge, "lat", 1)
    far, *rest = distances(count)[:-2]
    pieces, offsets = butterfly([strip, strip_swap(strip, far, True)], [0, far], strip_swap, rest)
    pay1, pay2, strips = columns_to_send(*fields, rows_in, pieces)
    halo1 = swapped(pay1, "lon", 1)
    halo2 = odd_pairs(pay2, "lon")
    across_two = strip_swap(strips, 2)
    beyond, face = strip_rows(partner, [strips, across_two, halo1, halo2], offsets)
    *coeffs, squares, face = coefficients(*fields, residual, halo1, halo2, rows_in, face)
    image, stats = image_and_stats(direction, land_sea, residual, squares, coeffs, beyond, face)
    parts, _ = butterfly([stats], [0], lambda value, distance: swapped(value, "lon", distance), distances(count)[::-1])
    parts.append(swapped(jnp.concatenate(parts, axis=0), "lat", 1))
    return tuple(update(parts, iterate, residual, direction, image))


def solution(mesh):
    field = P("member", "lat", "lon")
    level = P(None, "lat", "lon")
    flat = P("lat", "lon")
    return jax.shard_map(
        shards,
        mesh=mesh,
        in_specs=(field, field, field, level, level, flat, flat, P()),
        out_specs=(field, field, field),
        check_vma=False,
    )
```

```python
import functools

import jax
import jax.numpy as jnp
from jax import lax
from jax.experimental import pallas as pl
from jax.experimental.pallas import tpu as pltpu
from jax.sharding import PartitionSpec as P

STEPS = 4
HALO = 2 * STEPS
LANES = 128
VMEM_LIMIT = 24 * 1024 * 1024
f32 = jnp.float32


def turn(value, shift, axis=1):
    shift = shift % value.shape[axis]
    return value if shift == 0 else pltpu.roll(value, shift, axis)


def lanes_of(shape):
    return lax.broadcasted_iota(jnp.int32, shape, 1)


def place(kind, level, half):
    return 8 * kind + 32 * half + 64 * level


STRIP = 56
STRIP_AT = (0, 8, 16, 24, 48 - STEPS, 52 - STEPS, 32, 40)


def rows_kernel(lat_axis, d, sea, pw, ek, nk, fold, strip, edge, partner, sea_strip, sea_edge, pw_strip, arrived):
    rows = d.shape[1]
    top_rows = pl.ds(rows - 8, 8)
    first = jnp.where(lax.axis_index(lat_axis) == 1, 0, rows - 8)
    edge_rows = pl.ds(pl.multiple_of(first, 8), 8)
    moves = [
        (sea.at[:, top_rows, :], sea_strip),
        (pw.at[:, top_rows, :], pw_strip),
        (sea.at[:, edge_rows, :], sea_edge),
        (d.at[0, top_rows, :], strip.at[0:8]),
        (d.at[1, top_rows, :], strip.at[8:16]),
        (ek.at[top_rows, :], strip.at[32:40]),
        (nk.at[top_rows, :], strip.at[40:48]),
        (d.at[:, edge_rows, :], edge.at[0:2]),
        (pw.at[:, edge_rows, :], edge.at[4:6]),
        (ek.at[edge_rows, :], edge.at[6]),
        (nk.at[edge_rows, :], edge.at[7]),
        (fold, partner),
    ]
    copies = [pltpu.make_async_copy(a, b, arrived.at[i]) for i, (a, b) in enumerate(moves)]
    for copy in copies:
        copy.start()
    for copy in copies:
        copy.wait()
    for level in range(2):
        strip[16 + 8 * level : 24 + 8 * level, :] = sea_strip[level].astype(f32)
    strip[48:56, :] = jnp.concatenate([pw_strip[0, STEPS:, :], pw_strip[1, STEPS:, :]], axis=0)
    edge[2:4] = sea_edge[...].astype(f32)


def rows_to_send(d, sea, pw, ek, nk, fold):
    full = pl.BlockSpec(memory_space=pltpu.VMEM)
    inputs = [pltpu.with_memory_space_constraint(x, pltpu.HBM) for x in (d, sea, pw, ek, nk, fold)]
    return pl.pallas_call(
        functools.partial(rows_kernel, "lat"),
        out_shape=[
            jax.ShapeDtypeStruct((STRIP, LANES), f32),
            jax.ShapeDtypeStruct((8, 8, LANES), f32),
            jax.ShapeDtypeStruct(fold.shape, jnp.int32),
        ],
        in_specs=[pl.BlockSpec(memory_space=pltpu.HBM)] * 6,
        out_specs=[full] * 3,
        scratch_shapes=[
            pltpu.VMEM((2, 8, LANES), jnp.int32),
            pltpu.VMEM((2, 8, LANES), jnp.int32),
            pltpu.VMEM((2, 8, LANES), f32),
            pltpu.SemaphoreType.DMA((12,)),
        ],
        compiler_params=pltpu.CompilerParams(vmem_limit_bytes=VMEM_LIMIT),
    )(*inputs)


def pack_kernel(lon_axis, d, sea, pw, ek, nk, rows_in, *refs):
    *pieces, pay1, pay2, strips = refs
    first = d.shape[1] // 2 + 8
    for target, at in ((strips, 0), (pay1, first), (pay2, first)):
        for piece in pieces:
            size = piece.shape[0]
            target[at : at + size, :] = piece[...]
            at += size
    rows = d.shape[1]
    groups = rows // 8
    half_groups = groups // 2
    even = lax.axis_index(lon_axis) % 2 == 0

    def plane(index, group):
        if group == groups:
            return rows_in[index]
        at = pl.ds(8 * group, 8)
        if index < 2:
            return d[index, at, :]
        if index < 4:
            return sea[index - 2, at, :].astype(f32)
        if index < 6:
            return pw[index - 4, at, :]
        return (ek, nk)[index - 6][at, :]

    lane = lanes_of((8, LANES))
    for line in range(half_groups + 1):
        east = jnp.zeros((8, LANES), f32)
        west = jnp.zeros((8, LANES), f32)
        for half, group in enumerate((line, line + half_groups) if line < half_groups else (groups,)):
            for kind in range(4):
                for level in range(2):
                    at = place(kind, level, half)
                    turned = turn(plane(2 * kind + level, group), at + 8)
                    east = jnp.where((lane >= at) & (lane < at + 8), turned, east)
                    first = (at + 8) % LANES
                    west = jnp.where((lane >= first) & (lane < first + 8), turned, west)
        pay1[8 * line : 8 * line + 8, :] = jnp.where(even, east, west)
        pay2[8 * line : 8 * line + 8, :] = jnp.where(even, west, east)


def columns_to_send(d, sea, pw, ek, nk, rows_in, pieces):
    strips = sum(piece.shape[0] for piece in pieces)
    size = d.shape[1] // 2 + 8 + strips
    full = pl.BlockSpec(memory_space=pltpu.VMEM)
    inputs = (d, sea, pw, ek, nk, rows_in, *pieces)
    return pl.pallas_call(
        functools.partial(pack_kernel, "lon"),
        out_shape=[jax.ShapeDtypeStruct((n, LANES), f32) for n in (size, size, strips)],
        in_specs=[full] * len(inputs),
        out_specs=[full] * 3,
        compiler_params=pltpu.CompilerParams(vmem_limit_bytes=VMEM_LIMIT),
    )(*inputs)


def slab_index(group, shift=0):
    return slice(8 + 8 * group + shift, 16 + 8 * group + shift)


def east_of(x):
    lane = lanes_of(x[0].shape)
    a, b, s = (turn(v, -1) for v in x)
    return (
        jnp.where(lane == 127, s, a),
        jnp.where(lane == 63, s, b),
        jnp.where(lane == 127, a, jnp.where(lane == 63, b, s)),
    )


def west_of(x):
    lane = lanes_of(x[0].shape)
    a, b, s = (turn(v, 1) for v in x)
    return (
        jnp.where(lane == 0, s, a),
        jnp.where(lane == 64, s, b),
        jnp.where(lane == 0, a, jnp.where(lane == 64, b, s)),
    )


def coefficient_kernel(
    lon_axis, lat_axis, d, sea, pw, ek, nk, res, halo1, halo2, rows_in, face_in,
    field, weight, east_c, west_c, north_c, squares, face, ocean,
):
    top = lax.axis_index(lat_axis) == 1
    even = lax.axis_index(lon_axis) % 2 == 0
    groups = d.shape[1] // 8
    half_groups = groups // 2
    lane = lanes_of((8, LANES))
    zero = jnp.zeros((8, LANES), f32)
    right = (lane & 63) < 32
    low = (lane < 32) | (lane >= 96)
    near = ((lane & 63) < 8) | ((lane & 63) >= 56)
    at = slab_index

    def beside_slabs(from_east, from_west, half):
        out = []
        for kind, extra in ((0, 0), (1, 0), (2, 0), (3, 0), (3, 64)):
            r = turn(from_east, extra - (place(kind, 0, half) + 8))
            w = turn(from_west, extra + 120 - place(kind, 0, half))
            out.append(jnp.where(right, r, w))
        pair, pair_turned = out[3:]
        out[3:] = [jnp.where(low, pair, pair_turned), jnp.where(low, pair_turned, pair)]
        out[1] = jnp.where(near, out[1], 0.0)
        return out

    def set_group(group, planes, side):
        ek_here, nk_here = planes[6], planes[7]
        d_s = (planes[0], turn(planes[1], 64), side[0])
        oc_s = (planes[2], turn(planes[3], 64), side[1])
        pw_s = (planes[4], turn(planes[5], 64), side[2])
        ek_s = (ek_here, turn(ek_here, 64), side[3])
        nk_s = (nk_here, turn(nk_here, 64), side[4])
        for s in range(3):
            ocean[s, at(group), :] = oc_s[s]
            field[s, at(group), :] = d_s[s] * oc_s[s]
            weight[s, at(group), :] = pw_s[s] * oc_s[s]
            east_c[s, at(group), :] = ek_s[s] * oc_s[s]
            north_c[s, at(group), :] = nk_s[s] * oc_s[s]

    last = groups + 2
    for s in range(3):
        for buffer in (ocean, north_c):
            buffer[s, 0:8, :] = zero
            buffer[s, 8 + 8 * last : 16 + 8 * last, :] = zero
    for group in range(groups):
        here = slice(8 * group, 8 * group + 8)
        half, inside = divmod(group, half_groups)
        there = slice(8 * inside, 8 * inside + 8)
        a, b = halo1[there, :], halo2[there, :]
        side = beside_slabs(jnp.where(even, a, b), jnp.where(even, b, a), half)
        planes = [d[0, here, :], d[1, here, :], sea[0, here, :].astype(f32), sea[1, here, :].astype(f32),
                  pw[0, here, :], pw[1, here, :], ek[here, :], nk[here, :]]
        set_group(group + 1, planes, side)
    planes = [rows_in[i] for i in range(8)]
    corner = slice(8 * half_groups, 8 * half_groups + 8)
    a, b = halo1[corner, :], halo2[corner, :]
    side = beside_slabs(jnp.where(even, a, b), jnp.where(even, b, a), 0)
    for group, used in ((0, top), (groups + 1, jnp.logical_not(top))):
        masked, masked_side = list(planes), list(side)
        masked[2] = jnp.where(used, planes[2], 0.0)
        masked[3] = jnp.where(used, planes[3], 0.0)
        masked_side[1] = jnp.where(used, side[1], 0.0)
        set_group(group, masked, masked_side)

    total = zero
    for level in range(2):
        for group in range(groups):
            r = res[level, 8 * group : 8 * group + 8, :]
            total = total + r * r
    squares[...] = total
    face[...] = face_in[...]

    for group in range(groups + 2):
        here = at(group)
        oc = [ocean[s, here, :] for s in range(3)]
        half_face = [east_c[s, here, :] for s in range(3)]
        e, w = east_of(oc), west_of(half_face)
        for s in range(3):
            east_c[s, here, :] = half_face[s] * e[s]
            west_c[s, here, :] = oc[s] * w[s]
            north_c[s, here, :] = north_c[s, here, :] * ocean[s, at(group, 1), :]


def coefficients(d, sea, pw, ek, nk, res, halo1, halo2, rows_in, face):
    full = pl.BlockSpec(memory_space=pltpu.VMEM)
    extended = (3, d.shape[1] + 40, LANES)
    return pl.pallas_call(
        functools.partial(coefficient_kernel, "lon", "lat"),
        out_shape=[jax.ShapeDtypeStruct(extended, f32)] * 5
        + [jax.ShapeDtypeStruct((8, LANES), f32), jax.ShapeDtypeStruct(face.shape, f32)],
        in_specs=[full] * 10,
        out_specs=[full] * 7,
        scratch_shapes=[pltpu.VMEM(extended, f32)],
        compiler_params=pltpu.CompilerParams(vmem_limit_bytes=VMEM_LIMIT),
    )(d, sea, pw, ek, nk, res, halo1, halo2, rows_in, face)


def strip_kernel(count, offsets, lon_axis, lat_axis, partner, gathered_pieces, beyond_out, face_out, blocks):
    lon = lax.axis_index(lon_axis)

    top = lax.axis_index(lat_axis) == 1

    @pl.when(jnp.logical_not(top))
    def _():
        beyond_out[...] = jnp.zeros(beyond_out.shape, f32)
        face_out[...] = jnp.zeros(face_out.shape, f32)

    @pl.when(top)
    def _():
        strip_steps(lon, count, offsets, partner, gathered_pieces, beyond_out, face_out, blocks)


def strip_steps(lon, count, offsets, partner, gathered_pieces, beyond_out, face_out, blocks):
    odd = lon % 2
    neighbour = lax.rem(lon + 2 * odd + count - 1, count)
    owners = (lon, lax.bitwise_xor(lon, 2), lax.bitwise_xor(lon, 1), neighbour)
    for piece, owner in zip(gathered_pieces, owners):
        first = piece.shape[0] - STRIP * len(offsets)
        for slot, offset in enumerate(offsets):
            block = lax.bitwise_xor(owner, offset)
            row = first + STRIP * slot
            blocks[pl.ds(pl.multiple_of(block * STRIP, 8), STRIP), :] = piece[row : row + STRIP, :]
    wide = lanes_of((count, LANES))

    def strip_row(index, row):
        return blocks[pl.ds(STRIP_AT[index] + row, count, stride=STRIP), :]

    def strip_shift(values, to_east):
        step, edge = (-1, LANES - 1) if to_east else (1, 0)
        moved = [turn(x, step) for x in values]
        beside = [turn(x, step, 0) for x in moved]
        return [jnp.where(wide == edge, y, x) for x, y in zip(moved, beside)]

    partner_block = partner[...] >> 7
    partner_lane = partner[...] & (LANES - 1)

    def across(x):
        parts = []
        for first in range(0, count, 8):
            lanes_at = partner_lane[first : first + 8]
            block_at = partner_block[first : first + 8]
            total = jnp.zeros((8, LANES), f32)
            for block in range(count):
                source = jnp.broadcast_to(x[block : block + 1, :], (8, LANES))
                picked = jnp.take_along_axis(source, lanes_at, axis=1)
                total = jnp.where(block_at == block, picked, total)
            parts.append(total)
        return parts[0] if len(parts) == 1 else jnp.concatenate(parts, axis=0)

    block_index = lax.broadcasted_iota(jnp.int32, (count, LANES), 0)
    to_east = lax.rem(lon + 1, count)
    to_west = lax.rem(lon + count - 1, count)
    one = lanes_of((1, LANES))
    last_only = lax.broadcasted_iota(jnp.int32, (8, LANES), 0) == 7

    def write_rows(out, values):
        row = lambda level, block: jnp.sum(jnp.where(block_index == block, values[level], 0.0), axis=0, keepdims=True)
        here = [row(level, lon) for level in range(2)]
        east = [row(level, to_east) for level in range(2)]
        west = [row(level, to_west) for level in range(2)]
        turned = [turn(x, 64) for x in (here[1], east[1], west[1])]
        beside = jnp.where(one < 32, east[0], jnp.where(one >= 96, west[0], jnp.where(one >= 64, turned[1], turned[2])))
        for s, value in enumerate((here[0], turned[0], beside)):
            out[8 * s : 8 * s + 8, :] = jnp.where(last_only, jnp.broadcast_to(value, (8, LANES)), 0.0)

    east_k = [strip_row(6, r) for r in range(HALO)]
    north_k = [strip_row(7, r) for r in range(HALO)]
    top_k = 0.5 * (north_k[-1] + across(north_k[-1]))
    both = range(2)
    oc = [[strip_row(2 + level, r) for r in range(HALO)] for level in both]
    u = [[strip_row(level, r) * oc[level][r] for r in range(HALO)] for level in both]
    oc_east = strip_shift([x for level in both for x in oc[level]], True)
    e = [[east_k[r] * oc[level][r] * oc_east[HALO * level + r] for r in range(HALO)] for level in both]
    w = strip_shift([x for level in both for x in e[level]], False)
    w = [w[:HALO], w[HALO:]]
    n = [[north_k[r] * oc[level][r] * oc[level][r + 1] for r in range(HALO - 1)] for level in both]
    for level in both:
        n[level].append(top_k * oc[level][-1] * across(oc[level][-1]))
    write_rows(face_out, [n[0][-1], n[1][-1]])
    c = [
        [None] + [1.0 - e[level][r] - w[level][r] - n[level][r] - n[level][r - 1] for r in range(1, HALO)]
        for level in both
    ]
    for t in range(HALO):
        if t == STEPS:
            for level in both:
                for r in range(t, HALO):
                    u[level][r] = strip_row(4 + level, r) * oc[level][r] * u[level][r]
        beyond = [across(u[level][-1]) for level in both]
        write_rows(beyond_out.at[t], beyond)
        if t == HALO - 1:
            break
        rest = [(level, r) for level in both for r in range(t + 1, HALO)]
        east = strip_shift([u[level][r] for level, r in rest], True)
        west = strip_shift([u[level][r] for level, r in rest], False)
        new = [list(u[0]), list(u[1])]
        for (level, r), ue, uw in zip(rest, east, west):
            north = u[level][r + 1] if r + 1 < HALO else beyond[level]
            new[level][r] = (
                c[level][r] * u[level][r]
                + e[level][r] * ue
                + w[level][r] * uw
                + n[level][r] * north
                + n[level][r - 1] * u[level][r - 1]
            )
        u = new


def strip_rows(partner, pieces, offsets):
    count = partner.shape[0]
    full = pl.BlockSpec(memory_space=pltpu.VMEM)
    inputs = [partner, *pieces]

    def kernel(partner_ref, *refs):
        strip_kernel(count, offsets, "lon", "lat", partner_ref, refs[: len(pieces)], *refs[len(pieces) :])

    return pl.pallas_call(
        kernel,
        out_shape=[jax.ShapeDtypeStruct((HALO, 24, LANES), f32), jax.ShapeDtypeStruct((24, LANES), f32)],
        in_specs=[full] * len(inputs),
        out_specs=[full] * 2,
        scratch_shapes=[pltpu.VMEM((STRIP * count, LANES), f32)],
        compiler_params=pltpu.CompilerParams(vmem_limit_bytes=VMEM_LIMIT),
    )(*inputs)


def image_kernel(
    d, sea, res, squares, first_field, weight, east_c, west_c, north_c, beyond, face, image, stats, field, other
):
    groups = d.shape[1] // 8
    zero = jnp.zeros((8, LANES), f32)
    at = slab_index

    first_row = lax.broadcasted_iota(jnp.int32, (8, LANES), 0) == 0
    last = groups + 2
    for s in range(3):
        for buffer in (field, other):
            buffer[s, 0:8, :] = zero
            buffer[s, 8 + 8 * last : 16 + 8 * last, :] = zero
        for group in range(groups + 2):
            field[s, at(group), :] = first_field[s, at(group), :]

    def step(t, source, target):
        before = [zero] * 3
        for group in range(groups + 2):
            here, up = at(group), at(group, 1)
            u = [source[s, here, :] for s in range(3)]
            e, w = east_of(u), west_of(u)
            for s in range(3):
                flux = north_c[s, here, :] * (source[s, up, :] - u[s])
                if group == groups:
                    fold = slice(8 * s, 8 * s + 8)
                    flux = flux + face[fold, :] * (beyond[t, fold, :] - u[s])
                moved = turn(flux, 1, 0)
                below = jnp.where(first_row, before[s], moved)
                before[s] = moved
                target[s, here, :] = (
                    u[s]
                    + east_c[s, here, :] * (e[s] - u[s])
                    - west_c[s, here, :] * (u[s] - w[s])
                    + flux
                    - below
                )

    def two_steps(i, carry):
        @pl.when(2 * i == STEPS)
        def _():
            for group in range(groups + 2):
                for s in range(3):
                    field[s, at(group), :] = field[s, at(group), :] * weight[s, at(group), :]

        step(2 * i, field, other)
        step(2 * i + 1, other, field)
        return carry

    lax.fori_loop(0, STEPS, two_steps, 0)

    rr, rq, dq, qq = squares[...], zero, zero, zero
    for group in range(groups):
        here = slice(8 * group, 8 * group + 8)
        for level in range(2):
            u = turn(field[level, at(group + 1), :], 64 * level)
            o = sea[level, here, :].astype(f32)
            dv, rv = d[level, here, :], res[level, here, :]
            q = dv + o * u
            image[level, here, :] = q
            rq, dq, qq = rq + rv * q, dq + dv * q, qq + q * q
    rr, rq, dq, qq = (jnp.sum(x) for x in (rr, rq, dq, qq))
    a0 = jnp.where(qq > 0.0, rq / jnp.where(qq > 0.0, qq, 1.0), 0.0)
    ss = sq = zero
    for group in range(groups):
        here = slice(8 * group, 8 * group + 8)
        for level in range(2):
            q = image[level, here, :]
            s = res[level, here, :] - a0 * q
            ss, sq = ss + s * s, sq + s * q
    ss, sq = jnp.sum(ss), jnp.sum(sq)
    one = lanes_of((1, LANES))
    row = jnp.zeros((1, LANES), f32)
    for index, value in enumerate((rr, dq, ss, sq, qq, a0)):
        row = jnp.where(one == index, value, row)
    stats[...] = row


def image_and_stats(d, sea, res, squares, coeffs, beyond, face):
    full = pl.BlockSpec(memory_space=pltpu.VMEM)
    inputs = [d, sea, res, squares, *coeffs, beyond, face]
    return pl.pallas_call(
        image_kernel,
        out_shape=[jax.ShapeDtypeStruct(d.shape, f32), jax.ShapeDtypeStruct((1, LANES), f32)],
        in_specs=[full] * len(inputs),
        out_specs=[full] * 2,
        scratch_shapes=[pltpu.VMEM(coeffs[0].shape, f32)] * 2,
        compiler_params=pltpu.CompilerParams(vmem_limit_bytes=VMEM_LIMIT),
    )(*inputs)


def update_kernel(count, *refs):
    parts = refs[:count]
    iterate, res, d, image, iterate_hbm, res_hbm, d_hbm, new_iterate, new_res, new_d, sent = refs[count:]
    table = jnp.concatenate([part[...] for part in parts], axis=0)
    lane = lanes_of(table.shape)
    sums = jnp.sum(table, axis=0, keepdims=True)
    one = lanes_of(sums.shape)
    pick = lambda row, index: jnp.sum(jnp.where(one == index, row, 0.0), axis=1, keepdims=True)
    old_norm = pick(sums, 0)
    alpha = old_norm / pick(sums, 1)
    t = alpha - turn(table, -3)
    norms = table + t * (t * turn(table, -2) - 2.0 * turn(table, -1))
    new_norm = pick(jnp.sum(norms, axis=0, keepdims=True), 2)
    beta = new_norm / old_norm
    rows = d.shape[1]
    pieces = 2
    alpha = jnp.broadcast_to(alpha, (8, LANES))
    beta = jnp.broadcast_to(beta, (8, LANES))
    copies = []

    def send(source, target, part):
        copies.append(pltpu.make_async_copy(source.at[part], target.at[part], sent.at[len(copies)]))
        copies[-1].start()

    size = rows // pieces
    parts_of = [(level, first) for level in range(2) for first in range(0, rows, size)]
    for level, first in parts_of:
        for row in range(first, first + size, 8):
            here = slice(row, row + 8)
            new_iterate[level, here, :] = iterate[level, here, :] + alpha * d[level, here, :]
            new_res[level, here, :] = res[level, here, :] - alpha * image[level, here, :]
        part = (level, pl.ds(first, size), slice(None))
        send(new_iterate, iterate_hbm, part)
        send(new_res, res_hbm, part)
    for level, first in parts_of:
        for row in range(first, first + size, 8):
            here = slice(row, row + 8)
            new_d[level, here, :] = new_res[level, here, :] + beta * d[level, here, :]
        send(new_d, d_hbm, (level, pl.ds(first, size), slice(None)))
    for copy in copies:
        copy.wait()


def update(parts, iterate, res, d, image):
    full = pl.BlockSpec(memory_space=pltpu.VMEM)
    return pl.pallas_call(
        functools.partial(update_kernel, len(parts)),
        out_shape=[jax.ShapeDtypeStruct(d.shape, f32)] * 3,
        in_specs=[full] * (len(parts) + 4),
        out_specs=[pl.BlockSpec(memory_space=pltpu.HBM)] * 3,
        scratch_shapes=[pltpu.VMEM(d.shape, f32)] * 3 + [pltpu.SemaphoreType.DMA((12,))],
        compiler_params=pltpu.CompilerParams(vmem_limit_bytes=VMEM_LIMIT),
    )(*parts, iterate, res, d, image)


def swapped(value, axis, distance):
    return lax.ppermute(value, axis, [(i, i ^ distance) for i in range(lax.axis_size(axis))])


def odd_pairs(value, axis):
    count = lax.axis_size(axis)
    pairs = []
    for i in range(1, count, 2):
        pairs += [(i, (i + 1) % count), ((i + 1) % count, i)]
    return lax.ppermute(value, axis, pairs)


def distances(count):
    found = []
    while count > 1:
        count //= 2
        found.append(count)
    return found


def strip_swap(value, distance, alone=False):
    members, count, halves = (lax.axis_size(axis) for axis in ("member", "lon", "lat"))
    number = lambda m, i, t: (m * count + i) * halves + t
    other = lambda m, i, t: number(m, i ^ distance, t) if t or members % 2 else number(m ^ 1, i, t)
    places = [(m, i, t) for m in range(members) for i in range(count) for t in range(int(alone), halves)]
    return lax.ppermute(value, ("member", "lon", "lat"), [(number(*p), other(*p)) for p in places])


def butterfly(pieces, offsets, swap, order):
    pieces, offsets = list(pieces), list(offsets)
    for distance in order:
        whole = pieces[0] if len(pieces) == 1 else jnp.concatenate(pieces, axis=0)
        pieces.append(swap(whole, distance))
        offsets += [o ^ distance for o in offsets]
    return pieces, offsets


def shards(iterate, residual, direction, land_sea, precision_weight, east_kappa, north_kappa, fold_partner):
    count = lax.axis_size("lon")
    fields = (direction, land_sea, precision_weight, east_kappa, north_kappa)
    strip, edge, partner = rows_to_send(*fields, fold_partner.reshape(count, LANES))
    rows_in = swapped(edge, "lat", 1)
    far, *rest = distances(count)[:-2]
    pieces, offsets = butterfly([strip, strip_swap(strip, far, True)], [0, far], strip_swap, rest)
    pay1, pay2, strips = columns_to_send(*fields, rows_in, pieces)
    halo1 = swapped(pay1, "lon", 1)
    halo2 = odd_pairs(pay2, "lon")
    across_two = strip_swap(strips, 2)
    beyond, face = strip_rows(partner, [strips, across_two, halo1, halo2], offsets)
    *coeffs, squares, face = coefficients(*fields, residual, halo1, halo2, rows_in, face)
    image, stats = image_and_stats(direction, land_sea, residual, squares, coeffs, beyond, face)
    parts, _ = butterfly([stats], [0], lambda value, distance: swapped(value, "lon", distance), distances(count)[::-1])
    parts.append(swapped(jnp.concatenate(parts, axis=0), "lat", 1))
    return tuple(update(parts, iterate, residual, direction, image))


def solution(mesh):
    field = P("member", "lat", "lon")
    level = P(None, "lat", "lon")
    flat = P("lat", "lon")
    return jax.shard_map(
        shards,
        mesh=mesh,
        in_specs=(field, field, field, level, level, flat, flat, P()),
        out_specs=(field, field, field),
        check_vma=False,
    )
```

```python
import functools

import jax
import jax.numpy as jnp
from jax import lax
from jax.experimental import pallas as pl
from jax.experimental.pallas import tpu as pltpu
from jax.sharding import PartitionSpec as P

STEPS = 4
HALO = 2 * STEPS
LANES = 128
VMEM_LIMIT = 24 * 1024 * 1024
f32 = jnp.float32


def turn(value, shift, axis=1):
    shift = shift % value.shape[axis]
    return value if shift == 0 else pltpu.roll(value, shift, axis)


def lanes_of(shape):
    return lax.broadcasted_iota(jnp.int32, shape, 1)


def place(kind, level, half):
    return 16 * kind + 8 * half + 64 * level


STRIP = 56
STRIP_AT = (0, 8, 16, 24, 48 - STEPS, 52 - STEPS, 32, 40)


def rows_kernel(lat_axis, d, sea, pw, ek, nk, fold, strip, edge, partner, sea_strip, sea_edge, pw_strip, arrived):
    rows = d.shape[1]
    top_rows = pl.ds(rows - 8, 8)
    first = jnp.where(lax.axis_index(lat_axis) == 1, 0, rows - 8)
    edge_rows = pl.ds(pl.multiple_of(first, 8), 8)
    moves = [
        (sea.at[:, top_rows, :], sea_strip),
        (pw.at[:, top_rows, :], pw_strip),
        (sea.at[:, edge_rows, :], sea_edge),
        (d.at[0, top_rows, :], strip.at[0:8]),
        (d.at[1, top_rows, :], strip.at[8:16]),
        (ek.at[top_rows, :], strip.at[32:40]),
        (nk.at[top_rows, :], strip.at[40:48]),
        (d.at[:, edge_rows, :], edge.at[0:2]),
        (pw.at[:, edge_rows, :], edge.at[4:6]),
        (ek.at[edge_rows, :], edge.at[6]),
        (nk.at[edge_rows, :], edge.at[7]),
        (fold, partner),
    ]
    copies = [pltpu.make_async_copy(a, b, arrived.at[i]) for i, (a, b) in enumerate(moves)]
    for copy in copies:
        copy.start()
    for copy in copies:
        copy.wait()
    for level in range(2):
        strip[16 + 8 * level : 24 + 8 * level, :] = sea_strip[level].astype(f32)
    strip[48:56, :] = jnp.concatenate([pw_strip[0, STEPS:, :], pw_strip[1, STEPS:, :]], axis=0)
    edge[2:4] = sea_edge[...].astype(f32)


def rows_to_send(d, sea, pw, ek, nk, fold):
    full = pl.BlockSpec(memory_space=pltpu.VMEM)
    inputs = [pltpu.with_memory_space_constraint(x, pltpu.HBM) for x in (d, sea, pw, ek, nk, fold)]
    return pl.pallas_call(
        functools.partial(rows_kernel, "lat"),
        out_shape=[
            jax.ShapeDtypeStruct((STRIP, LANES), f32),
            jax.ShapeDtypeStruct((8, 8, LANES), f32),
            jax.ShapeDtypeStruct(fold.shape, jnp.int32),
        ],
        in_specs=[pl.BlockSpec(memory_space=pltpu.HBM)] * 6,
        out_specs=[full] * 3,
        scratch_shapes=[
            pltpu.VMEM((2, 8, LANES), jnp.int32),
            pltpu.VMEM((2, 8, LANES), jnp.int32),
            pltpu.VMEM((2, 8, LANES), f32),
            pltpu.SemaphoreType.DMA((12,)),
        ],
        compiler_params=pltpu.CompilerParams(vmem_limit_bytes=VMEM_LIMIT),
    )(*inputs)


def pack_kernel(lon_axis, d, sea, pw, ek, nk, rows_in, *refs):
    *pieces, pay1, pay2, strips = refs
    first = d.shape[1] // 2 + 8
    for target, at in ((strips, 0), (pay1, first), (pay2, first)):
        for piece in pieces:
            size = piece.shape[0]
            target[at : at + size, :] = piece[...]
            at += size
    rows = d.shape[1]
    groups = rows // 8
    half_groups = groups // 2
    even = lax.axis_index(lon_axis) % 2 == 0

    def plane(index, group):
        if group == groups:
            return rows_in[index]
        at = pl.ds(8 * group, 8)
        if index < 2:
            return d[index, at, :]
        if index < 4:
            return sea[index - 2, at, :].astype(f32)
        if index < 6:
            return pw[index - 4, at, :]
        return (ek, nk)[index - 6][at, :]

    lane = lanes_of((8, LANES))
    for line in range(half_groups + 1):
        east = jnp.zeros((8, LANES), f32)
        west = jnp.zeros((8, LANES), f32)
        for half, group in enumerate((line, line + half_groups) if line < half_groups else (groups,)):
            for kind in range(4):
                for level in range(2):
                    at = place(kind, level, half)
                    turned = turn(plane(2 * kind + level, group), at + 8)
                    east = jnp.where((lane >= at) & (lane < at + 8), turned, east)
                    first = (at + 8) % LANES
                    west = jnp.where((lane >= first) & (lane < first + 8), turned, west)
        pay1[8 * line : 8 * line + 8, :] = jnp.where(even, east, west)
        pay2[8 * line : 8 * line + 8, :] = jnp.where(even, west, east)


def columns_to_send(d, sea, pw, ek, nk, rows_in, pieces):
    strips = sum(piece.shape[0] for piece in pieces)
    size = d.shape[1] // 2 + 8 + strips
    full = pl.BlockSpec(memory_space=pltpu.VMEM)
    inputs = (d, sea, pw, ek, nk, rows_in, *pieces)
    return pl.pallas_call(
        functools.partial(pack_kernel, "lon"),
        out_shape=[jax.ShapeDtypeStruct((n, LANES), f32) for n in (size, size, strips)],
        in_specs=[full] * len(inputs),
        out_specs=[full] * 3,
        compiler_params=pltpu.CompilerParams(vmem_limit_bytes=VMEM_LIMIT),
    )(*inputs)


def slab_index(group, shift=0):
    return slice(8 + 8 * group + shift, 16 + 8 * group + shift)


def east_of(x):
    lane = lanes_of(x[0].shape)
    a, b, s = (turn(v, -1) for v in x)
    return (
        jnp.where(lane == 127, s, a),
        jnp.where(lane == 63, s, b),
        jnp.where(lane == 127, a, jnp.where(lane == 63, b, s)),
    )


def west_of(x):
    lane = lanes_of(x[0].shape)
    a, b, s = (turn(v, 1) for v in x)
    return (
        jnp.where(lane == 0, s, a),
        jnp.where(lane == 64, s, b),
        jnp.where(lane == 0, a, jnp.where(lane == 64, b, s)),
    )


def coefficient_kernel(
    lon_axis, lat_axis, d, sea, pw, ek, nk, res, halo1, halo2, rows_in, face_in,
    field, weight, east_c, west_c, north_c, squares, face, ocean,
):
    top = lax.axis_index(lat_axis) == 1
    even = lax.axis_index(lon_axis) % 2 == 0
    groups = d.shape[1] // 8
    half_groups = groups // 2
    lane = lanes_of((8, LANES))
    zero = jnp.zeros((8, LANES), f32)
    low = (lane < 32) | (lane >= 96)
    near = ((lane & 63) < 8) | ((lane & 63) >= 56)
    at = slab_index

    def beside_slabs(from_east, from_west, half):
        both = jnp.where((lane & 8) == 8 * half, from_west, from_east)
        out = [turn(both, extra + 120 - place(kind, 0, half)) for kind, extra in ((0, 0), (1, 0), (2, 0), (3, 0), (3, 64))]
        pair, pair_turned = out[3:]
        out[3:] = [jnp.where(low, pair, pair_turned), jnp.where(low, pair_turned, pair)]
        out[1] = jnp.where(near, out[1], 0.0)
        return out

    def set_group(group, planes, side):
        ek_here, nk_here = planes[6], planes[7]
        d_s = (planes[0], turn(planes[1], 64), side[0])
        oc_s = (planes[2], turn(planes[3], 64), side[1])
        pw_s = (planes[4], turn(planes[5], 64), side[2])
        ek_s = (ek_here, turn(ek_here, 64), side[3])
        nk_s = (nk_here, turn(nk_here, 64), side[4])
        for s in range(3):
            ocean[s, at(group), :] = oc_s[s]
            field[s, at(group), :] = d_s[s] * oc_s[s]
            weight[s, at(group), :] = pw_s[s] * oc_s[s]
            east_c[s, at(group), :] = ek_s[s] * oc_s[s]
            north_c[s, at(group), :] = nk_s[s] * oc_s[s]

    last = groups + 2
    for s in range(3):
        for buffer in (ocean, north_c):
            buffer[s, 0:8, :] = zero
            buffer[s, 8 + 8 * last : 16 + 8 * last, :] = zero
    for group in range(groups):
        here = slice(8 * group, 8 * group + 8)
        half, inside = divmod(group, half_groups)
        there = slice(8 * inside, 8 * inside + 8)
        a, b = halo1[there, :], halo2[there, :]
        side = beside_slabs(jnp.where(even, a, b), jnp.where(even, b, a), half)
        planes = [d[0, here, :], d[1, here, :], sea[0, here, :].astype(f32), sea[1, here, :].astype(f32),
                  pw[0, here, :], pw[1, here, :], ek[here, :], nk[here, :]]
        set_group(group + 1, planes, side)
    planes = [rows_in[i] for i in range(8)]
    corner = slice(8 * half_groups, 8 * half_groups + 8)
    a, b = halo1[corner, :], halo2[corner, :]
    side = beside_slabs(jnp.where(even, a, b), jnp.where(even, b, a), 0)
    for group, used in ((0, top), (groups + 1, jnp.logical_not(top))):
        masked, masked_side = list(planes), list(side)
        masked[2] = jnp.where(used, planes[2], 0.0)
        masked[3] = jnp.where(used, planes[3], 0.0)
        masked_side[1] = jnp.where(used, side[1], 0.0)
        set_group(group, masked, masked_side)

    total = zero
    for level in range(2):
        for group in range(groups):
            r = res[level, 8 * group : 8 * group + 8, :]
            total = total + r * r
    squares[...] = total
    face[...] = face_in[...]

    for group in range(groups + 2):
        here = at(group)
        oc = [ocean[s, here, :] for s in range(3)]
        half_face = [east_c[s, here, :] for s in range(3)]
        e, w = east_of(oc), west_of(half_face)
        for s in range(3):
            east_c[s, here, :] = half_face[s] * e[s]
            west_c[s, here, :] = oc[s] * w[s]
            north_c[s, here, :] = north_c[s, here, :] * ocean[s, at(group, 1), :]


def coefficients(d, sea, pw, ek, nk, res, halo1, halo2, rows_in, face):
    full = pl.BlockSpec(memory_space=pltpu.VMEM)
    extended = (3, d.shape[1] + 40, LANES)
    return pl.pallas_call(
        functools.partial(coefficient_kernel, "lon", "lat"),
        out_shape=[jax.ShapeDtypeStruct(extended, f32)] * 5
        + [jax.ShapeDtypeStruct((8, LANES), f32), jax.ShapeDtypeStruct(face.shape, f32)],
        in_specs=[full] * 10,
        out_specs=[full] * 7,
        scratch_shapes=[pltpu.VMEM(extended, f32)],
        compiler_params=pltpu.CompilerParams(vmem_limit_bytes=VMEM_LIMIT),
    )(d, sea, pw, ek, nk, res, halo1, halo2, rows_in, face)


def strip_kernel(count, offsets, lon_axis, lat_axis, partner, gathered_pieces, beyond_out, face_out, blocks):
    lon = lax.axis_index(lon_axis)

    top = lax.axis_index(lat_axis) == 1

    @pl.when(jnp.logical_not(top))
    def _():
        beyond_out[...] = jnp.zeros(beyond_out.shape, f32)
        face_out[...] = jnp.zeros(face_out.shape, f32)

    @pl.when(top)
    def _():
        strip_steps(lon, count, offsets, partner, gathered_pieces, beyond_out, face_out, blocks)


def strip_steps(lon, count, offsets, partner, gathered_pieces, beyond_out, face_out, blocks):
    odd = lon % 2
    neighbour = lax.rem(lon + 2 * odd + count - 1, count)
    owners = (lon, lax.bitwise_xor(lon, 2), lax.bitwise_xor(lon, 1), neighbour)
    for piece, owner in zip(gathered_pieces, owners):
        first = piece.shape[0] - STRIP * len(offsets)
        for slot, offset in enumerate(offsets):
            block = lax.bitwise_xor(owner, offset)
            row = first + STRIP * slot
            blocks[pl.ds(pl.multiple_of(block * STRIP, 8), STRIP), :] = piece[row : row + STRIP, :]
    wide = lanes_of((count, LANES))

    def strip_row(index, row):
        return blocks[pl.ds(STRIP_AT[index] + row, count, stride=STRIP), :]

    def strip_shift(values, to_east):
        step, edge = (-1, LANES - 1) if to_east else (1, 0)
        moved = [turn(x, step) for x in values]
        beside = [turn(x, step, 0) for x in moved]
        return [jnp.where(wide == edge, y, x) for x, y in zip(moved, beside)]

    partner_block = partner[...] >> 7
    partner_lane = partner[...] & (LANES - 1)

    def across(x):
        parts = []
        for first in range(0, count, 8):
            lanes_at = partner_lane[first : first + 8]
            block_at = partner_block[first : first + 8]
            total = jnp.zeros((8, LANES), f32)
            for block in range(count):
                source = jnp.broadcast_to(x[block : block + 1, :], (8, LANES))
                picked = jnp.take_along_axis(source, lanes_at, axis=1)
                total = jnp.where(block_at == block, picked, total)
            parts.append(total)
        return parts[0] if len(parts) == 1 else jnp.concatenate(parts, axis=0)

    block_index = lax.broadcasted_iota(jnp.int32, (count, LANES), 0)
    to_east = lax.rem(lon + 1, count)
    to_west = lax.rem(lon + count - 1, count)
    one = lanes_of((1, LANES))
    last_only = lax.broadcasted_iota(jnp.int32, (8, LANES), 0) == 7

    def write_rows(out, values):
        row = lambda level, block: jnp.sum(jnp.where(block_index == block, values[level], 0.0), axis=0, keepdims=True)
        here = [row(level, lon) for level in range(2)]
        east = [row(level, to_east) for level in range(2)]
        west = [row(level, to_west) for level in range(2)]
        turned = [turn(x, 64) for x in (here[1], east[1], west[1])]
        beside = jnp.where(one < 32, east[0], jnp.where(one >= 96, west[0], jnp.where(one >= 64, turned[1], turned[2])))
        for s, value in enumerate((here[0], turned[0], beside)):
            out[8 * s : 8 * s + 8, :] = jnp.where(last_only, jnp.broadcast_to(value, (8, LANES)), 0.0)

    east_k = [strip_row(6, r) for r in range(HALO)]
    north_k = [strip_row(7, r) for r in range(HALO)]
    top_k = 0.5 * (north_k[-1] + across(north_k[-1]))
    both = range(2)
    oc = [[strip_row(2 + level, r) for r in range(HALO)] for level in both]
    u = [[strip_row(level, r) * oc[level][r] for r in range(HALO)] for level in both]
    oc_east = strip_shift([x for level in both for x in oc[level]], True)
    e = [[east_k[r] * oc[level][r] * oc_east[HALO * level + r] for r in range(HALO)] for level in both]
    w = strip_shift([x for level in both for x in e[level]], False)
    w = [w[:HALO], w[HALO:]]
    n = [[north_k[r] * oc[level][r] * oc[level][r + 1] for r in range(HALO - 1)] for level in both]
    for level in both:
        n[level].append(top_k * oc[level][-1] * across(oc[level][-1]))
    write_rows(face_out, [n[0][-1], n[1][-1]])
    c = [
        [None] + [1.0 - e[level][r] - w[level][r] - n[level][r] - n[level][r - 1] for r in range(1, HALO)]
        for level in both
    ]
    for t in range(HALO):
        if t == STEPS:
            for level in both:
                for r in range(t, HALO):
                    u[level][r] = strip_row(4 + level, r) * oc[level][r] * u[level][r]
        beyond = [across(u[level][-1]) for level in both]
        write_rows(beyond_out.at[t], beyond)
        if t == HALO - 1:
            break
        rest = [(level, r) for level in both for r in range(t + 1, HALO)]
        east = strip_shift([u[level][r] for level, r in rest], True)
        west = strip_shift([u[level][r] for level, r in rest], False)
        new = [list(u[0]), list(u[1])]
        for (level, r), ue, uw in zip(rest, east, west):
            north = u[level][r + 1] if r + 1 < HALO else beyond[level]
            new[level][r] = (
                c[level][r] * u[level][r]
                + e[level][r] * ue
                + w[level][r] * uw
                + n[level][r] * north
                + n[level][r - 1] * u[level][r - 1]
            )
        u = new


def strip_rows(partner, pieces, offsets):
    count = partner.shape[0]
    full = pl.BlockSpec(memory_space=pltpu.VMEM)
    inputs = [partner, *pieces]

    def kernel(partner_ref, *refs):
        strip_kernel(count, offsets, "lon", "lat", partner_ref, refs[: len(pieces)], *refs[len(pieces) :])

    return pl.pallas_call(
        kernel,
        out_shape=[jax.ShapeDtypeStruct((HALO, 24, LANES), f32), jax.ShapeDtypeStruct((24, LANES), f32)],
        in_specs=[full] * len(inputs),
        out_specs=[full] * 2,
        scratch_shapes=[pltpu.VMEM((STRIP * count, LANES), f32)],
        compiler_params=pltpu.CompilerParams(vmem_limit_bytes=VMEM_LIMIT),
    )(*inputs)


def image_kernel(
    d, sea, res, squares, first_field, weight, east_c, west_c, north_c, beyond, face, image, stats, field, other
):
    groups = d.shape[1] // 8
    zero = jnp.zeros((8, LANES), f32)
    at = slab_index

    first_row = lax.broadcasted_iota(jnp.int32, (8, LANES), 0) == 0
    last = groups + 2
    for s in range(3):
        for buffer in (field, other):
            buffer[s, 0:8, :] = zero
            buffer[s, 8 + 8 * last : 16 + 8 * last, :] = zero
        for group in range(groups + 2):
            field[s, at(group), :] = first_field[s, at(group), :]

    def step(t, source, target):
        before = [zero] * 3
        for group in range(groups + 2):
            here, up = at(group), at(group, 1)
            u = [source[s, here, :] for s in range(3)]
            e, w = east_of(u), west_of(u)
            for s in range(3):
                flux = north_c[s, here, :] * (source[s, up, :] - u[s])
                if group == groups:
                    fold = slice(8 * s, 8 * s + 8)
                    flux = flux + face[fold, :] * (beyond[t, fold, :] - u[s])
                moved = turn(flux, 1, 0)
                below = jnp.where(first_row, before[s], moved)
                before[s] = moved
                target[s, here, :] = (
                    u[s]
                    + east_c[s, here, :] * (e[s] - u[s])
                    - west_c[s, here, :] * (u[s] - w[s])
                    + flux
                    - below
                )

    def two_steps(i, carry):
        @pl.when(2 * i == STEPS)
        def _():
            for group in range(groups + 2):
                for s in range(3):
                    field[s, at(group), :] = field[s, at(group), :] * weight[s, at(group), :]

        step(2 * i, field, other)
        step(2 * i + 1, other, field)
        return carry

    lax.fori_loop(0, STEPS, two_steps, 0)

    rr, rq, dq, qq = squares[...], zero, zero, zero
    for group in range(groups):
        here = slice(8 * group, 8 * group + 8)
        for level in range(2):
            u = turn(field[level, at(group + 1), :], 64 * level)
            o = sea[level, here, :].astype(f32)
            dv, rv = d[level, here, :], res[level, here, :]
            q = dv + o * u
            image[level, here, :] = q
            rq, dq, qq = rq + rv * q, dq + dv * q, qq + q * q
    rr, rq, dq, qq = (jnp.sum(x) for x in (rr, rq, dq, qq))
    a0 = jnp.where(qq > 0.0, rq / jnp.where(qq > 0.0, qq, 1.0), 0.0)
    ss = sq = zero
    for group in range(groups):
        here = slice(8 * group, 8 * group + 8)
        for level in range(2):
            q = image[level, here, :]
            s = res[level, here, :] - a0 * q
            ss, sq = ss + s * s, sq + s * q
    ss, sq = jnp.sum(ss), jnp.sum(sq)
    one = lanes_of((1, LANES))
    row = jnp.zeros((1, LANES), f32)
    for index, value in enumerate((rr, dq, ss, sq, qq, a0)):
        row = jnp.where(one == index, value, row)
    stats[...] = row


def image_and_stats(d, sea, res, squares, coeffs, beyond, face):
    full = pl.BlockSpec(memory_space=pltpu.VMEM)
    inputs = [d, sea, res, squares, *coeffs, beyond, face]
    return pl.pallas_call(
        image_kernel,
        out_shape=[jax.ShapeDtypeStruct(d.shape, f32), jax.ShapeDtypeStruct((1, LANES), f32)],
        in_specs=[full] * len(inputs),
        out_specs=[full] * 2,
        scratch_shapes=[pltpu.VMEM(coeffs[0].shape, f32)] * 2,
        compiler_params=pltpu.CompilerParams(vmem_limit_bytes=VMEM_LIMIT),
    )(*inputs)


def update_kernel(count, *refs):
    parts = refs[:count]
    iterate, res, d, image, iterate_hbm, res_hbm, d_hbm, new_iterate, new_res, new_d, sent = refs[count:]
    table = jnp.concatenate([part[...] for part in parts], axis=0)
    lane = lanes_of(table.shape)
    sums = jnp.sum(table, axis=0, keepdims=True)
    one = lanes_of(sums.shape)
    pick = lambda row, index: jnp.sum(jnp.where(one == index, row, 0.0), axis=1, keepdims=True)
    old_norm = pick(sums, 0)
    alpha = old_norm / pick(sums, 1)
    t = alpha - turn(table, -3)
    norms = table + t * (t * turn(table, -2) - 2.0 * turn(table, -1))
    new_norm = pick(jnp.sum(norms, axis=0, keepdims=True), 2)
    beta = new_norm / old_norm
    rows = d.shape[1]
    pieces = 2
    alpha = jnp.broadcast_to(alpha, (8, LANES))
    beta = jnp.broadcast_to(beta, (8, LANES))
    copies = []

    def send(source, target, part):
        copies.append(pltpu.make_async_copy(source.at[part], target.at[part], sent.at[len(copies)]))
        copies[-1].start()

    size = rows // pieces
    parts_of = [(level, first) for level in range(2) for first in range(0, rows, size)]
    for level, first in parts_of:
        for row in range(first, first + size, 8):
            here = slice(row, row + 8)
            new_iterate[level, here, :] = iterate[level, here, :] + alpha * d[level, here, :]
            new_res[level, here, :] = res[level, here, :] - alpha * image[level, here, :]
        part = (level, pl.ds(first, size), slice(None))
        send(new_iterate, iterate_hbm, part)
        send(new_res, res_hbm, part)
    for level, first in parts_of:
        for row in range(first, first + size, 8):
            here = slice(row, row + 8)
            new_d[level, here, :] = new_res[level, here, :] + beta * d[level, here, :]
        send(new_d, d_hbm, (level, pl.ds(first, size), slice(None)))
    for copy in copies:
        copy.wait()


def update(parts, iterate, res, d, image):
    full = pl.BlockSpec(memory_space=pltpu.VMEM)
    return pl.pallas_call(
        functools.partial(update_kernel, len(parts)),
        out_shape=[jax.ShapeDtypeStruct(d.shape, f32)] * 3,
        in_specs=[full] * (len(parts) + 4),
        out_specs=[pl.BlockSpec(memory_space=pltpu.HBM)] * 3,
        scratch_shapes=[pltpu.VMEM(d.shape, f32)] * 3 + [pltpu.SemaphoreType.DMA((12,))],
        compiler_params=pltpu.CompilerParams(vmem_limit_bytes=VMEM_LIMIT),
    )(*parts, iterate, res, d, image)


def swapped(value, axis, distance):
    return lax.ppermute(value, axis, [(i, i ^ distance) for i in range(lax.axis_size(axis))])


def odd_pairs(value, axis):
    count = lax.axis_size(axis)
    pairs = []
    for i in range(1, count, 2):
        pairs += [(i, (i + 1) % count), ((i + 1) % count, i)]
    return lax.ppermute(value, axis, pairs)


def distances(count):
    found = []
    while count > 1:
        count //= 2
        found.append(count)
    return found


def strip_swap(value, distance, alone=False):
    members, count, halves = (lax.axis_size(axis) for axis in ("member", "lon", "lat"))
    number = lambda m, i, t: (m * count + i) * halves + t
    other = lambda m, i, t: number(m, i ^ distance, t) if t or members % 2 else number(m ^ 1, i, t)
    places = [(m, i, t) for m in range(members) for i in range(count) for t in range(int(alone), halves)]
    return lax.ppermute(value, ("member", "lon", "lat"), [(number(*p), other(*p)) for p in places])


def butterfly(pieces, offsets, swap, order):
    pieces, offsets = list(pieces), list(offsets)
    for distance in order:
        whole = pieces[0] if len(pieces) == 1 else jnp.concatenate(pieces, axis=0)
        pieces.append(swap(whole, distance))
        offsets += [o ^ distance for o in offsets]
    return pieces, offsets


def shards(iterate, residual, direction, land_sea, precision_weight, east_kappa, north_kappa, fold_partner):
    count = lax.axis_size("lon")
    fields = (direction, land_sea, precision_weight, east_kappa, north_kappa)
    strip, edge, partner = rows_to_send(*fields, fold_partner.reshape(count, LANES))
    rows_in = swapped(edge, "lat", 1)
    far, *rest = distances(count)[:-2]
    pieces, offsets = butterfly([strip, strip_swap(strip, far, True)], [0, far], strip_swap, rest)
    pay1, pay2, strips = columns_to_send(*fields, rows_in, pieces)
    halo1 = swapped(pay1, "lon", 1)
    halo2 = odd_pairs(pay2, "lon")
    across_two = strip_swap(strips, 2)
    beyond, face = strip_rows(partner, [strips, across_two, halo1, halo2], offsets)
    *coeffs, squares, face = coefficients(*fields, residual, halo1, halo2, rows_in, face)
    image, stats = image_and_stats(direction, land_sea, residual, squares, coeffs, beyond, face)
    parts, _ = butterfly([stats], [0], lambda value, distance: swapped(value, "lon", distance), distances(count)[::-1])
    parts.append(swapped(jnp.concatenate(parts, axis=0), "lat", 1))
    return tuple(update(parts, iterate, residual, direction, image))


def solution(mesh):
    field = P("member", "lat", "lon")
    level = P(None, "lat", "lon")
    flat = P("lat", "lon")
    return jax.shard_map(
        shards,
        mesh=mesh,
        in_specs=(field, field, field, level, level, flat, flat, P()),
        out_specs=(field, field, field),
        check_vma=False,
    )
```

```python
import functools

import jax
import jax.numpy as jnp
from jax import lax
from jax.experimental import pallas as pl
from jax.experimental.pallas import tpu as pltpu
from jax.sharding import PartitionSpec as P

STEPS = 4
HALO = 2 * STEPS
LANES = 128
VMEM_LIMIT = 24 * 1024 * 1024
f32 = jnp.float32


def turn(value, shift, axis=1):
    shift = shift % value.shape[axis]
    return value if shift == 0 else pltpu.roll(value, shift, axis)


def lanes_of(shape):
    return lax.broadcasted_iota(jnp.int32, shape, 1)


def place(kind, level, half):
    return 16 * kind + 8 * half + 64 * level


STRIP = 56
STRIP_AT = (0, 8, 16, 24, 48 - STEPS, 52 - STEPS, 32, 40)


def rows_kernel(lat_axis, d, sea, pw, ek, nk, fold, strip, edge, partner, sea_strip, sea_edge, pw_strip, arrived):
    rows = d.shape[1]
    top_rows = pl.ds(rows - 8, 8)
    first = jnp.where(lax.axis_index(lat_axis) == 1, 0, rows - 8)
    edge_rows = pl.ds(pl.multiple_of(first, 8), 8)
    moves = [
        (sea.at[:, top_rows, :], sea_strip),
        (pw.at[:, top_rows, :], pw_strip),
        (sea.at[:, edge_rows, :], sea_edge),
        (d.at[0, top_rows, :], strip.at[0:8]),
        (d.at[1, top_rows, :], strip.at[8:16]),
        (ek.at[top_rows, :], strip.at[32:40]),
        (nk.at[top_rows, :], strip.at[40:48]),
        (d.at[:, edge_rows, :], edge.at[0:2]),
        (pw.at[:, edge_rows, :], edge.at[4:6]),
        (ek.at[edge_rows, :], edge.at[6]),
        (nk.at[edge_rows, :], edge.at[7]),
        (fold, partner),
    ]
    copies = [pltpu.make_async_copy(a, b, arrived.at[i]) for i, (a, b) in enumerate(moves)]
    for copy in copies:
        copy.start()
    for copy in copies:
        copy.wait()
    for level in range(2):
        strip[16 + 8 * level : 24 + 8 * level, :] = sea_strip[level].astype(f32)
    strip[48:56, :] = jnp.concatenate([pw_strip[0, STEPS:, :], pw_strip[1, STEPS:, :]], axis=0)
    edge[2:4] = sea_edge[...].astype(f32)


def rows_to_send(d, sea, pw, ek, nk, fold):
    full = pl.BlockSpec(memory_space=pltpu.VMEM)
    inputs = [pltpu.with_memory_space_constraint(x, pltpu.HBM) for x in (d, sea, pw, ek, nk, fold)]
    return pl.pallas_call(
        functools.partial(rows_kernel, "lat"),
        out_shape=[
            jax.ShapeDtypeStruct((STRIP, LANES), f32),
            jax.ShapeDtypeStruct((8, 8, LANES), f32),
            jax.ShapeDtypeStruct(fold.shape, jnp.int32),
        ],
        in_specs=[pl.BlockSpec(memory_space=pltpu.HBM)] * 6,
        out_specs=[full] * 3,
        scratch_shapes=[
            pltpu.VMEM((2, 8, LANES), jnp.int32),
            pltpu.VMEM((2, 8, LANES), jnp.int32),
            pltpu.VMEM((2, 8, LANES), f32),
            pltpu.SemaphoreType.DMA((12,)),
        ],
        compiler_params=pltpu.CompilerParams(vmem_limit_bytes=VMEM_LIMIT),
    )(*inputs)


def pack_kernel(lon_axis, d, sea, pw, ek, nk, rows_in, *refs):
    *pieces, pay1, pay2, strips = refs
    first = d.shape[1] // 2 + 8
    for target, at in ((strips, 0), (pay1, first), (pay2, first)):
        for piece in pieces:
            size = piece.shape[0]
            target[at : at + size, :] = piece[...]
            at += size
    rows = d.shape[1]
    groups = rows // 8
    half_groups = groups // 2
    even = lax.axis_index(lon_axis) % 2 == 0

    def plane(index, group):
        if group == groups:
            return rows_in[index]
        at = pl.ds(8 * group, 8)
        if index < 2:
            return d[index, at, :]
        if index < 4:
            return sea[index - 2, at, :].astype(f32)
        if index < 6:
            return pw[index - 4, at, :]
        return (ek, nk)[index - 6][at, :]

    lane = lanes_of((8, LANES))
    for line in range(half_groups + 1):
        east = jnp.zeros((8, LANES), f32)
        west = jnp.zeros((8, LANES), f32)
        for half, group in enumerate((line, line + half_groups) if line < half_groups else (groups,)):
            for kind in range(4):
                for level in range(2):
                    at = place(kind, level, half)
                    turned = turn(plane(2 * kind + level, group), at + 8)
                    east = jnp.where((lane >= at) & (lane < at + 8), turned, east)
                    first = (at + 8) % LANES
                    west = jnp.where((lane >= first) & (lane < first + 8), turned, west)
        pay1[8 * line : 8 * line + 8, :] = jnp.where(even, east, west)
        pay2[8 * line : 8 * line + 8, :] = jnp.where(even, west, east)


def columns_to_send(d, sea, pw, ek, nk, rows_in, pieces):
    strips = sum(piece.shape[0] for piece in pieces)
    size = d.shape[1] // 2 + 8 + strips
    full = pl.BlockSpec(memory_space=pltpu.VMEM)
    inputs = (d, sea, pw, ek, nk, rows_in, *pieces)
    return pl.pallas_call(
        functools.partial(pack_kernel, "lon"),
        out_shape=[jax.ShapeDtypeStruct((n, LANES), f32) for n in (size, size, strips)],
        in_specs=[full] * len(inputs),
        out_specs=[full] * 3,
        compiler_params=pltpu.CompilerParams(vmem_limit_bytes=VMEM_LIMIT),
    )(*inputs)


def slab_index(group, shift=0):
    return slice(8 + 8 * group + shift, 16 + 8 * group + shift)


def east_of(x):
    lane = lanes_of(x[0].shape)
    a, b, s = (turn(v, -1) for v in x)
    return (
        jnp.where(lane == 127, s, a),
        jnp.where(lane == 63, s, b),
        jnp.where(lane == 127, a, jnp.where(lane == 63, b, s)),
    )


def west_of(x):
    lane = lanes_of(x[0].shape)
    a, b, s = (turn(v, 1) for v in x)
    return (
        jnp.where(lane == 0, s, a),
        jnp.where(lane == 64, s, b),
        jnp.where(lane == 0, a, jnp.where(lane == 64, b, s)),
    )


def own_kernel(
    lat_axis, d, sea, pw, ek, nk, res, rows_in,
    field, weight, east_c, west_c, north_c, oc_edge, ek_edge, squares, ocean,
):
    top = lax.axis_index(lat_axis) == 1
    groups = d.shape[1] // 8
    lane = lanes_of((8, LANES))
    zero = jnp.zeros((8, LANES), f32)
    at = slab_index

    def set_group(group, planes):
        d0, d1, oc0, oc1, pw0, pw1, ek_here, nk_here = planes
        turned = [turn(x, 64) for x in (d1, oc1, pw1, ek_here, nk_here)]
        for s, (dv, oc, weights, east, north) in enumerate(((d0, oc0, pw0, ek_here, nk_here), turned)):
            ocean[s, at(group), :] = oc
            field[s, at(group), :] = dv * oc
            weight[s, at(group), :] = weights * oc
            east_c[s, at(group), :] = east * oc
            north_c[s, at(group), :] = north * oc

    for s in range(2):
        ocean[s, at(groups + 2), :] = zero
    for group in range(groups):
        here = slice(8 * group, 8 * group + 8)
        set_group(
            group + 1,
            [d[0, here, :], d[1, here, :], sea[0, here, :].astype(f32), sea[1, here, :].astype(f32),
             pw[0, here, :], pw[1, here, :], ek[here, :], nk[here, :]],
        )
    for group, used in ((0, top), (groups + 1, jnp.logical_not(top))):
        planes = [rows_in[i] for i in range(8)]
        planes[2:4] = [jnp.where(used, x, 0.0) for x in planes[2:4]]
        set_group(group, planes)

    total = zero
    for level in range(2):
        for group in range(groups):
            r = res[level, 8 * group : 8 * group + 8, :]
            total = total + r * r
    squares[...] = total

    for group in range(groups + 2):
        here = at(group)
        oc = [ocean[s, here, :] for s in range(2)]
        half_face = [east_c[s, here, :] for s in range(2)]
        e = [turn(x, -1) for x in oc]
        w = [turn(x, 1) for x in half_face]
        for s in range(2):
            east_c[s, here, :] = jnp.where(lane == 127 - 64 * s, half_face[s], half_face[s] * e[s])
            west_c[s, here, :] = jnp.where(lane == 64 * s, oc[s], oc[s] * w[s])
            north_c[s, here, :] = north_c[s, here, :] * ocean[s, at(group, 1), :]
        oc_edge[here, :] = jnp.where(lane == 63, e[1], e[0])
        ek_edge[here, :] = jnp.where(lane == 64, w[1], w[0])


def own_coefficients(d, sea, pw, ek, nk, res, rows_in):
    full = pl.BlockSpec(memory_space=pltpu.VMEM)
    rows = d.shape[1] + 40
    return pl.pallas_call(
        functools.partial(own_kernel, "lat"),
        out_shape=[jax.ShapeDtypeStruct((3, rows, LANES), f32)] * 5
        + [jax.ShapeDtypeStruct((n, LANES), f32) for n in (rows, rows, 8)],
        in_specs=[full] * 7,
        out_specs=[full] * 8,
        scratch_shapes=[pltpu.VMEM((2, rows, LANES), f32)],
        compiler_params=pltpu.CompilerParams(vmem_limit_bytes=VMEM_LIMIT),
    )(d, sea, pw, ek, nk, res, rows_in)


def beside_kernel(
    lon_axis, lat_axis, groups, oc_edge, ek_edge, halo1, halo2, face_in, field_in, weight_in, east_in, west_in, north_in,
    field, weight, east_c, west_c, north_c, face, ocean,
):
    top = lax.axis_index(lat_axis) == 1
    even = lax.axis_index(lon_axis) % 2 == 0
    half_groups = groups // 2
    lane = lanes_of((8, LANES))
    low = (lane < 32) | (lane >= 96)
    near = ((lane & 63) < 8) | ((lane & 63) >= 56)
    at = slab_index

    def set_group(group, line, half, used=None):
        there = slice(8 * line, 8 * line + 8)
        a, b = halo1[there, :], halo2[there, :]
        from_east, from_west = jnp.where(even, a, b), jnp.where(even, b, a)
        both = jnp.where((lane & 8) == 8 * half, from_west, from_east)
        dv, oc, weights, pair, pair_turned = (
            turn(both, extra + 120 - place(kind, 0, half)) for kind, extra in ((0, 0), (1, 0), (2, 0), (3, 0), (3, 64))
        )
        oc = jnp.where(near if used is None else near & used, oc, 0.0)
        ocean[at(group), :] = oc
        field[2, at(group), :] = dv * oc
        weight[2, at(group), :] = weights * oc
        east_c[2, at(group), :] = jnp.where(low, pair, pair_turned) * oc
        north_c[2, at(group), :] = jnp.where(low, pair_turned, pair) * oc

    ocean[at(groups + 2), :] = jnp.zeros((8, LANES), f32)
    for group in range(groups):
        set_group(group + 1, group % half_groups, group // half_groups)
    set_group(0, half_groups, 0, top)
    set_group(groups + 1, half_groups, 0, jnp.logical_not(top))
    face[...] = face_in[...]

    for group in range(groups + 2):
        here = at(group)
        oc, half_face = ocean[here, :], east_c[2, here, :]
        e, w = turn(oc, -1), turn(half_face, 1)
        east_c[2, here, :] = half_face * jnp.where((lane & 63) == 63, oc_edge[here, :], e)
        west_c[2, here, :] = oc * jnp.where((lane & 63) == 0, ek_edge[here, :], w)
        north_c[2, here, :] = north_c[2, here, :] * ocean[at(group, 1), :]
        for s in range(2):
            east, west = east_in[s, here, :], west_in[s, here, :]
            east_c[s, here, :] = jnp.where(lane == 127 - 64 * s, east * e, east)
            west_c[s, here, :] = jnp.where(lane == 64 * s, west * w, west)


def with_columns_beside(groups, own, edges, halo1, halo2, face):
    full = pl.BlockSpec(memory_space=pltpu.VMEM)
    inputs = [*edges, halo1, halo2, face, *own]
    return pl.pallas_call(
        functools.partial(beside_kernel, "lon", "lat", groups),
        out_shape=[jax.ShapeDtypeStruct(x.shape, f32) for x in (*own, face)],
        in_specs=[full] * len(inputs),
        out_specs=[full] * 6,
        scratch_shapes=[pltpu.VMEM(edges[0].shape, f32)],
        input_output_aliases={5 + i: i for i in range(5)},
        compiler_params=pltpu.CompilerParams(vmem_limit_bytes=VMEM_LIMIT),
    )(*inputs)


def strip_kernel(count, offsets, lon_axis, lat_axis, partner, gathered_pieces, beyond_out, face_out, blocks):
    lon = lax.axis_index(lon_axis)

    top = lax.axis_index(lat_axis) == 1

    @pl.when(jnp.logical_not(top))
    def _():
        beyond_out[...] = jnp.zeros(beyond_out.shape, f32)
        face_out[...] = jnp.zeros(face_out.shape, f32)

    @pl.when(top)
    def _():
        strip_steps(lon, count, offsets, partner, gathered_pieces, beyond_out, face_out, blocks)


def strip_steps(lon, count, offsets, partner, gathered_pieces, beyond_out, face_out, blocks):
    odd = lon % 2
    neighbour = lax.rem(lon + 2 * odd + count - 1, count)
    owners = (lon, lax.bitwise_xor(lon, 2), lax.bitwise_xor(lon, 1), neighbour)
    for piece, owner in zip(gathered_pieces, owners):
        first = piece.shape[0] - STRIP * len(offsets)
        for slot, offset in enumerate(offsets):
            block = lax.bitwise_xor(owner, offset)
            row = first + STRIP * slot
            blocks[pl.ds(pl.multiple_of(block * STRIP, 8), STRIP), :] = piece[row : row + STRIP, :]
    wide = lanes_of((count, LANES))

    def strip_row(index, row):
        return blocks[pl.ds(STRIP_AT[index] + row, count, stride=STRIP), :]

    def strip_shift(values, to_east):
        step, edge = (-1, LANES - 1) if to_east else (1, 0)
        moved = [turn(x, step) for x in values]
        beside = [turn(x, step, 0) for x in moved]
        return [jnp.where(wide == edge, y, x) for x, y in zip(moved, beside)]

    partner_block = partner[...] >> 7
    partner_lane = partner[...] & (LANES - 1)

    def across(x):
        parts = []
        for first in range(0, count, 8):
            lanes_at = partner_lane[first : first + 8]
            block_at = partner_block[first : first + 8]
            total = jnp.zeros((8, LANES), f32)
            for block in range(count):
                source = jnp.broadcast_to(x[block : block + 1, :], (8, LANES))
                picked = jnp.take_along_axis(source, lanes_at, axis=1)
                total = jnp.where(block_at == block, picked, total)
            parts.append(total)
        return parts[0] if len(parts) == 1 else jnp.concatenate(parts, axis=0)

    block_index = lax.broadcasted_iota(jnp.int32, (count, LANES), 0)
    to_east = lax.rem(lon + 1, count)
    to_west = lax.rem(lon + count - 1, count)
    one = lanes_of((1, LANES))
    last_only = lax.broadcasted_iota(jnp.int32, (8, LANES), 0) == 7

    def write_rows(out, values):
        row = lambda level, block: jnp.sum(jnp.where(block_index == block, values[level], 0.0), axis=0, keepdims=True)
        here = [row(level, lon) for level in range(2)]
        east = [row(level, to_east) for level in range(2)]
        west = [row(level, to_west) for level in range(2)]
        turned = [turn(x, 64) for x in (here[1], east[1], west[1])]
        beside = jnp.where(one < 32, east[0], jnp.where(one >= 96, west[0], jnp.where(one >= 64, turned[1], turned[2])))
        for s, value in enumerate((here[0], turned[0], beside)):
            out[8 * s : 8 * s + 8, :] = jnp.where(last_only, jnp.broadcast_to(value, (8, LANES)), 0.0)

    east_k = [strip_row(6, r) for r in range(HALO)]
    north_k = [strip_row(7, r) for r in range(HALO)]
    top_k = 0.5 * (north_k[-1] + across(north_k[-1]))
    both = range(2)
    oc = [[strip_row(2 + level, r) for r in range(HALO)] for level in both]
    u = [[strip_row(level, r) * oc[level][r] for r in range(HALO)] for level in both]
    oc_east = strip_shift([x for level in both for x in oc[level]], True)
    e = [[east_k[r] * oc[level][r] * oc_east[HALO * level + r] for r in range(HALO)] for level in both]
    w = strip_shift([x for level in both for x in e[level]], False)
    w = [w[:HALO], w[HALO:]]
    n = [[north_k[r] * oc[level][r] * oc[level][r + 1] for r in range(HALO - 1)] for level in both]
    for level in both:
        n[level].append(top_k * oc[level][-1] * across(oc[level][-1]))
    write_rows(face_out, [n[0][-1], n[1][-1]])
    c = [
        [None] + [1.0 - e[level][r] - w[level][r] - n[level][r] - n[level][r - 1] for r in range(1, HALO)]
        for level in both
    ]
    for t in range(HALO):
        if t == STEPS:
            for level in both:
                for r in range(t, HALO):
                    u[level][r] = strip_row(4 + level, r) * oc[level][r] * u[level][r]
        beyond = [across(u[level][-1]) for level in both]
        write_rows(beyond_out.at[t], beyond)
        if t == HALO - 1:
            break
        rest = [(level, r) for level in both for r in range(t + 1, HALO)]
        east = strip_shift([u[level][r] for level, r in rest], True)
        west = strip_shift([u[level][r] for level, r in rest], False)
        new = [list(u[0]), list(u[1])]
        for (level, r), ue, uw in zip(rest, east, west):
            north = u[level][r + 1] if r + 1 < HALO else beyond[level]
            new[level][r] = (
                c[level][r] * u[level][r]
                + e[level][r] * ue
                + w[level][r] * uw
                + n[level][r] * north
                + n[level][r - 1] * u[level][r - 1]
            )
        u = new


def strip_rows(partner, pieces, offsets):
    count = partner.shape[0]
    full = pl.BlockSpec(memory_space=pltpu.VMEM)
    inputs = [partner, *pieces]

    def kernel(partner_ref, *refs):
        strip_kernel(count, offsets, "lon", "lat", partner_ref, refs[: len(pieces)], *refs[len(pieces) :])

    return pl.pallas_call(
        kernel,
        out_shape=[jax.ShapeDtypeStruct((HALO, 24, LANES), f32), jax.ShapeDtypeStruct((24, LANES), f32)],
        in_specs=[full] * len(inputs),
        out_specs=[full] * 2,
        scratch_shapes=[pltpu.VMEM((STRIP * count, LANES), f32)],
        compiler_params=pltpu.CompilerParams(vmem_limit_bytes=VMEM_LIMIT),
    )(*inputs)


def image_kernel(
    d, sea, res, squares, first_field, weight, east_c, west_c, north_c, beyond, face, image, stats, field, other
):
    groups = d.shape[1] // 8
    zero = jnp.zeros((8, LANES), f32)
    at = slab_index

    first_row = lax.broadcasted_iota(jnp.int32, (8, LANES), 0) == 0
    last = groups + 2
    for s in range(3):
        for buffer in (field, other):
            buffer[s, 0:8, :] = zero
            buffer[s, 8 + 8 * last : 16 + 8 * last, :] = zero
        for group in range(groups + 2):
            field[s, at(group), :] = first_field[s, at(group), :]

    def step(t, source, target):
        before = [zero] * 3
        for group in range(groups + 2):
            here, up = at(group), at(group, 1)
            u = [source[s, here, :] for s in range(3)]
            e, w = east_of(u), west_of(u)
            for s in range(3):
                flux = north_c[s, here, :] * (source[s, up, :] - u[s])
                if group == groups:
                    fold = slice(8 * s, 8 * s + 8)
                    flux = flux + face[fold, :] * (beyond[t, fold, :] - u[s])
                moved = turn(flux, 1, 0)
                below = jnp.where(first_row, before[s], moved)
                before[s] = moved
                target[s, here, :] = (
                    u[s]
                    + east_c[s, here, :] * (e[s] - u[s])
                    - west_c[s, here, :] * (u[s] - w[s])
                    + flux
                    - below
                )

    def two_steps(i, carry):
        @pl.when(2 * i == STEPS)
        def _():
            for group in range(groups + 2):
                for s in range(3):
                    field[s, at(group), :] = field[s, at(group), :] * weight[s, at(group), :]

        step(2 * i, field, other)
        step(2 * i + 1, other, field)
        return carry

    lax.fori_loop(0, STEPS, two_steps, 0)

    rr, rq, dq, qq = squares[...], zero, zero, zero
    for group in range(groups):
        here = slice(8 * group, 8 * group + 8)
        for level in range(2):
            u = turn(field[level, at(group + 1), :], 64 * level)
            o = sea[level, here, :].astype(f32)
            dv, rv = d[level, here, :], res[level, here, :]
            q = dv + o * u
            image[level, here, :] = q
            rq, dq, qq = rq + rv * q, dq + dv * q, qq + q * q
    rr, rq, dq, qq = (jnp.sum(x) for x in (rr, rq, dq, qq))
    a0 = jnp.where(qq > 0.0, rq / jnp.where(qq > 0.0, qq, 1.0), 0.0)
    ss = sq = zero
    for group in range(groups):
        here = slice(8 * group, 8 * group + 8)
        for level in range(2):
            q = image[level, here, :]
            s = res[level, here, :] - a0 * q
            ss, sq = ss + s * s, sq + s * q
    ss, sq = jnp.sum(ss), jnp.sum(sq)
    one = lanes_of((1, LANES))
    row = jnp.zeros((1, LANES), f32)
    for index, value in enumerate((rr, dq, ss, sq, qq, a0)):
        row = jnp.where(one == index, value, row)
    stats[...] = row


def image_and_stats(d, sea, res, squares, coeffs, beyond, face):
    full = pl.BlockSpec(memory_space=pltpu.VMEM)
    inputs = [d, sea, res, squares, *coeffs, beyond, face]
    return pl.pallas_call(
        image_kernel,
        out_shape=[jax.ShapeDtypeStruct(d.shape, f32), jax.ShapeDtypeStruct((1, LANES), f32)],
        in_specs=[full] * len(inputs),
        out_specs=[full] * 2,
        scratch_shapes=[pltpu.VMEM(coeffs[0].shape, f32)] * 2,
        compiler_params=pltpu.CompilerParams(vmem_limit_bytes=VMEM_LIMIT),
    )(*inputs)


def update_kernel(count, *refs):
    parts = refs[:count]
    iterate, res, d, image, iterate_hbm, res_hbm, d_hbm, new_iterate, new_res, new_d, sent = refs[count:]
    table = jnp.concatenate([part[...] for part in parts], axis=0)
    lane = lanes_of(table.shape)
    sums = jnp.sum(table, axis=0, keepdims=True)
    one = lanes_of(sums.shape)
    pick = lambda row, index: jnp.sum(jnp.where(one == index, row, 0.0), axis=1, keepdims=True)
    old_norm = pick(sums, 0)
    alpha = old_norm / pick(sums, 1)
    t = alpha - turn(table, -3)
    norms = table + t * (t * turn(table, -2) - 2.0 * turn(table, -1))
    new_norm = pick(jnp.sum(norms, axis=0, keepdims=True), 2)
    beta = new_norm / old_norm
    rows = d.shape[1]
    pieces = 2
    alpha = jnp.broadcast_to(alpha, (8, LANES))
    beta = jnp.broadcast_to(beta, (8, LANES))
    copies = []

    def send(source, target, part):
        copies.append(pltpu.make_async_copy(source.at[part], target.at[part], sent.at[len(copies)]))
        copies[-1].start()

    size = rows // pieces
    parts_of = [(level, first) for level in range(2) for first in range(0, rows, size)]
    for level, first in parts_of:
        for row in range(first, first + size, 8):
            here = slice(row, row + 8)
            new_iterate[level, here, :] = iterate[level, here, :] + alpha * d[level, here, :]
            new_res[level, here, :] = res[level, here, :] - alpha * image[level, here, :]
        part = (level, pl.ds(first, size), slice(None))
        send(new_iterate, iterate_hbm, part)
        send(new_res, res_hbm, part)
    for level, first in parts_of:
        for row in range(first, first + size, 8):
            here = slice(row, row + 8)
            new_d[level, here, :] = new_res[level, here, :] + beta * d[level, here, :]
        send(new_d, d_hbm, (level, pl.ds(first, size), slice(None)))
    for copy in copies:
        copy.wait()


def update(parts, iterate, res, d, image):
    full = pl.BlockSpec(memory_space=pltpu.VMEM)
    return pl.pallas_call(
        functools.partial(update_kernel, len(parts)),
        out_shape=[jax.ShapeDtypeStruct(d.shape, f32)] * 3,
        in_specs=[full] * (len(parts) + 4),
        out_specs=[pl.BlockSpec(memory_space=pltpu.HBM)] * 3,
        scratch_shapes=[pltpu.VMEM(d.shape, f32)] * 3 + [pltpu.SemaphoreType.DMA((12,))],
        compiler_params=pltpu.CompilerParams(vmem_limit_bytes=VMEM_LIMIT),
    )(*parts, iterate, res, d, image)


def swapped(value, axis, distance):
    return lax.ppermute(value, axis, [(i, i ^ distance) for i in range(lax.axis_size(axis))])


def odd_pairs(value, axis):
    count = lax.axis_size(axis)
    pairs = []
    for i in range(1, count, 2):
        pairs += [(i, (i + 1) % count), ((i + 1) % count, i)]
    return lax.ppermute(value, axis, pairs)


def distances(count):
    found = []
    while count > 1:
        count //= 2
        found.append(count)
    return found


def strip_swap(value, distance, alone=False):
    members, count, halves = (lax.axis_size(axis) for axis in ("member", "lon", "lat"))
    number = lambda m, i, t: (m * count + i) * halves + t
    other = lambda m, i, t: number(m, i ^ distance, t) if t or members % 2 else number(m ^ 1, i, t)
    places = [(m, i, t) for m in range(members) for i in range(count) for t in range(int(alone), halves)]
    return lax.ppermute(value, ("member", "lon", "lat"), [(number(*p), other(*p)) for p in places])


def butterfly(pieces, offsets, swap, order):
    pieces, offsets = list(pieces), list(offsets)
    for distance in order:
        whole = pieces[0] if len(pieces) == 1 else jnp.concatenate(pieces, axis=0)
        pieces.append(swap(whole, distance))
        offsets += [o ^ distance for o in offsets]
    return pieces, offsets


def shards(iterate, residual, direction, land_sea, precision_weight, east_kappa, north_kappa, fold_partner):
    count = lax.axis_size("lon")
    fields = (direction, land_sea, precision_weight, east_kappa, north_kappa)
    strip, edge, partner = rows_to_send(*fields, fold_partner.reshape(count, LANES))
    rows_in = swapped(edge, "lat", 1)
    far, *rest = distances(count)[:-2]
    pieces, offsets = butterfly([strip, strip_swap(strip, far, True)], [0, far], strip_swap, rest)
    pay1, pay2, strips = columns_to_send(*fields, rows_in, pieces)
    halo1 = swapped(pay1, "lon", 1)
    halo2 = odd_pairs(pay2, "lon")
    across_two = strip_swap(strips, 2)
    beyond, face = strip_rows(partner, [strips, across_two, halo1, halo2], offsets)
    *own, oc_edge, ek_edge, squares = own_coefficients(*fields, residual, rows_in)
    groups = direction.shape[1] // 8
    *coeffs, face = with_columns_beside(groups, own, (oc_edge, ek_edge), halo1, halo2, face)
    image, stats = image_and_stats(direction, land_sea, residual, squares, coeffs, beyond, face)
    parts, _ = butterfly([stats], [0], lambda value, distance: swapped(value, "lon", distance), distances(count)[::-1])
    parts.append(swapped(jnp.concatenate(parts, axis=0), "lat", 1))
    return tuple(update(parts, iterate, residual, direction, image))


def solution(mesh):
    field = P("member", "lat", "lon")
    level = P(None, "lat", "lon")
    flat = P("lat", "lon")
    return jax.shard_map(
        shards,
        mesh=mesh,
        in_specs=(field, field, field, level, level, flat, flat, P()),
        out_specs=(field, field, field),
        check_vma=False,
    )
```

```python
import functools

import jax
import jax.numpy as jnp
from jax import lax
from jax.experimental import pallas as pl
from jax.experimental.pallas import tpu as pltpu
from jax.sharding import PartitionSpec as P

STEPS = 4
HALO = 2 * STEPS
LANES = 128
VMEM_LIMIT = 24 * 1024 * 1024
f32 = jnp.float32


def turn(value, shift, axis=1):
    shift = shift % value.shape[axis]
    return value if shift == 0 else pltpu.roll(value, shift, axis)


def lanes_of(shape):
    return lax.broadcasted_iota(jnp.int32, shape, 1)


def place(kind, level, half):
    return 16 * kind + 8 * half + 64 * level


STRIP = 56
STRIP_AT = (0, 8, 16, 24, 48 - STEPS, 52 - STEPS, 32, 40)


def rows_kernel(lat_axis, d, sea, pw, ek, nk, fold, strip, edge, partner, sea_strip, sea_edge, pw_strip, arrived):
    rows = d.shape[1]
    top_rows = pl.ds(rows - 8, 8)
    first = jnp.where(lax.axis_index(lat_axis) == 1, 0, rows - 8)
    edge_rows = pl.ds(pl.multiple_of(first, 8), 8)
    moves = [
        (sea.at[:, top_rows, :], sea_strip),
        (pw.at[:, top_rows, :], pw_strip),
        (sea.at[:, edge_rows, :], sea_edge),
        (d.at[0, top_rows, :], strip.at[0:8]),
        (d.at[1, top_rows, :], strip.at[8:16]),
        (ek.at[top_rows, :], strip.at[32:40]),
        (nk.at[top_rows, :], strip.at[40:48]),
        (d.at[:, edge_rows, :], edge.at[0:2]),
        (pw.at[:, edge_rows, :], edge.at[4:6]),
        (ek.at[edge_rows, :], edge.at[6]),
        (nk.at[edge_rows, :], edge.at[7]),
        (fold, partner),
    ]
    copies = [pltpu.make_async_copy(a, b, arrived.at[i]) for i, (a, b) in enumerate(moves)]
    for copy in copies:
        copy.start()
    for copy in copies:
        copy.wait()
    for level in range(2):
        strip[16 + 8 * level : 24 + 8 * level, :] = sea_strip[level].astype(f32)
    strip[48:56, :] = jnp.concatenate([pw_strip[0, STEPS:, :], pw_strip[1, STEPS:, :]], axis=0)
    edge[2:4] = sea_edge[...].astype(f32)


def rows_to_send(d, sea, pw, ek, nk, fold):
    full = pl.BlockSpec(memory_space=pltpu.VMEM)
    inputs = [pltpu.with_memory_space_constraint(x, pltpu.HBM) for x in (d, sea, pw, ek, nk, fold)]
    return pl.pallas_call(
        functools.partial(rows_kernel, "lat"),
        out_shape=[
            jax.ShapeDtypeStruct((STRIP, LANES), f32),
            jax.ShapeDtypeStruct((8, 8, LANES), f32),
            jax.ShapeDtypeStruct(fold.shape, jnp.int32),
        ],
        in_specs=[pl.BlockSpec(memory_space=pltpu.HBM)] * 6,
        out_specs=[full] * 3,
        scratch_shapes=[
            pltpu.VMEM((2, 8, LANES), jnp.int32),
            pltpu.VMEM((2, 8, LANES), jnp.int32),
            pltpu.VMEM((2, 8, LANES), f32),
            pltpu.SemaphoreType.DMA((12,)),
        ],
        compiler_params=pltpu.CompilerParams(vmem_limit_bytes=VMEM_LIMIT),
    )(*inputs)


def pack_kernel(lon_axis, d, sea, pw, ek, nk, rows_in, *refs):
    *pieces, pay1, pay2, strips = refs
    first = d.shape[1] // 2 + 8
    for target, at in ((strips, 0), (pay1, first), (pay2, first)):
        for piece in pieces:
            size = piece.shape[0]
            target[at : at + size, :] = piece[...]
            at += size
    rows = d.shape[1]
    groups = rows // 8
    half_groups = groups // 2
    even = lax.axis_index(lon_axis) % 2 == 0

    def plane(index, group):
        if group == groups:
            return rows_in[index]
        at = pl.ds(8 * group, 8)
        if index < 2:
            return d[index, at, :]
        if index < 4:
            return sea[index - 2, at, :].astype(f32)
        if index < 6:
            return pw[index - 4, at, :]
        return (ek, nk)[index - 6][at, :]

    lane = lanes_of((8, LANES))
    for line in range(half_groups + 1):
        east = jnp.zeros((8, LANES), f32)
        west = jnp.zeros((8, LANES), f32)
        for half, group in enumerate((line, line + half_groups) if line < half_groups else (groups,)):
            for kind in range(4):
                for level in range(2):
                    at = place(kind, level, half)
                    turned = turn(plane(2 * kind + level, group), at + 8)
                    east = jnp.where((lane >= at) & (lane < at + 8), turned, east)
                    first = (at + 8) % LANES
                    west = jnp.where((lane >= first) & (lane < first + 8), turned, west)
        pay1[8 * line : 8 * line + 8, :] = jnp.where(even, east, west)
        pay2[8 * line : 8 * line + 8, :] = jnp.where(even, west, east)


def columns_to_send(d, sea, pw, ek, nk, rows_in, pieces):
    strips = sum(piece.shape[0] for piece in pieces)
    size = d.shape[1] // 2 + 8 + strips
    full = pl.BlockSpec(memory_space=pltpu.VMEM)
    inputs = (d, sea, pw, ek, nk, rows_in, *pieces)
    return pl.pallas_call(
        functools.partial(pack_kernel, "lon"),
        out_shape=[jax.ShapeDtypeStruct((n, LANES), f32) for n in (size, size, strips)],
        in_specs=[full] * len(inputs),
        out_specs=[full] * 3,
        compiler_params=pltpu.CompilerParams(vmem_limit_bytes=VMEM_LIMIT),
    )(*inputs)


def slab_index(group, shift=0):
    return slice(8 + 8 * group + shift, 16 + 8 * group + shift)


def east_of(x):
    lane = lanes_of(x[0].shape)
    a, b, s = (turn(v, -1) for v in x)
    return (
        jnp.where(lane == 127, s, a),
        jnp.where(lane == 63, s, b),
        jnp.where(lane == 127, a, jnp.where(lane == 63, b, s)),
    )


def west_of(x):
    lane = lanes_of(x[0].shape)
    a, b, s = (turn(v, 1) for v in x)
    return (
        jnp.where(lane == 0, s, a),
        jnp.where(lane == 64, s, b),
        jnp.where(lane == 0, a, jnp.where(lane == 64, b, s)),
    )


def own_kernel(
    lat_axis, d, sea, pw, ek, nk, res, rows_in,
    field, weight, east_c, west_c, north_c, oc_edge, ek_edge, squares, ocean,
):
    top = lax.axis_index(lat_axis) == 1
    groups = d.shape[1] // 8
    lane = lanes_of((8, LANES))
    zero = jnp.zeros((8, LANES), f32)
    at = slab_index

    def set_group(group, planes):
        d0, d1, oc0, oc1, pw0, pw1, ek_here, nk_here = planes
        turned = [turn(x, 64) for x in (d1, oc1, pw1, ek_here, nk_here)]
        for s, (dv, oc, weights, east, north) in enumerate(((d0, oc0, pw0, ek_here, nk_here), turned)):
            ocean[s, at(group), :] = oc
            field[s, at(group), :] = dv * oc
            weight[s, at(group), :] = weights * oc
            east_c[s, at(group), :] = east * oc
            north_c[s, at(group), :] = north * oc

    for s in range(2):
        ocean[s, at(groups + 2), :] = zero
        field[s, at(groups + 2), :] = zero
    for group in range(groups):
        here = slice(8 * group, 8 * group + 8)
        set_group(
            group + 1,
            [d[0, here, :], d[1, here, :], sea[0, here, :].astype(f32), sea[1, here, :].astype(f32),
             pw[0, here, :], pw[1, here, :], ek[here, :], nk[here, :]],
        )
    for group, used in ((0, top), (groups + 1, jnp.logical_not(top))):
        planes = [rows_in[i] for i in range(8)]
        planes[2:4] = [jnp.where(used, x, 0.0) for x in planes[2:4]]
        set_group(group, planes)

    total = zero
    for level in range(2):
        for group in range(groups):
            r = res[level, 8 * group : 8 * group + 8, :]
            total = total + r * r
    squares[...] = total

    for group in range(groups + 2):
        here = at(group)
        oc = [ocean[s, here, :] for s in range(2)]
        half_face = [east_c[s, here, :] for s in range(2)]
        e = [turn(x, -1) for x in oc]
        w = [turn(x, 1) for x in half_face]
        for s in range(2):
            east_c[s, here, :] = jnp.where(lane == 127 - 64 * s, half_face[s], half_face[s] * e[s])
            west_c[s, here, :] = jnp.where(lane == 64 * s, oc[s], oc[s] * w[s])
            north_c[s, here, :] = north_c[s, here, :] * ocean[s, at(group, 1), :]
        oc_edge[here, :] = jnp.where(lane == 63, e[1], e[0])
        ek_edge[here, :] = jnp.where(lane == 64, w[1], w[0])


def own_coefficients(d, sea, pw, ek, nk, res, rows_in):
    full = pl.BlockSpec(memory_space=pltpu.VMEM)
    rows = d.shape[1] + 40
    return pl.pallas_call(
        functools.partial(own_kernel, "lat"),
        out_shape=[jax.ShapeDtypeStruct((3, rows, LANES), f32)] * 5
        + [jax.ShapeDtypeStruct((n, LANES), f32) for n in (rows, rows, 8)],
        in_specs=[full] * 7,
        out_specs=[full] * 8,
        scratch_shapes=[pltpu.VMEM((2, rows, LANES), f32)],
        compiler_params=pltpu.CompilerParams(vmem_limit_bytes=VMEM_LIMIT),
    )(d, sea, pw, ek, nk, res, rows_in)


def beside_kernel(
    lon_axis, lat_axis, groups, oc_edge, ek_edge, halo1, halo2, face_in, field_in, weight_in, east_in, west_in, north_in,
    field, weight, east_c, west_c, north_c, face, ocean,
):
    top = lax.axis_index(lat_axis) == 1
    even = lax.axis_index(lon_axis) % 2 == 0
    half_groups = groups // 2
    lane = lanes_of((8, LANES))
    low = (lane < 32) | (lane >= 96)
    near = ((lane & 63) < 8) | ((lane & 63) >= 56)
    at = slab_index

    def set_group(group, line, half, used=None):
        there = slice(8 * line, 8 * line + 8)
        a, b = halo1[there, :], halo2[there, :]
        from_east, from_west = jnp.where(even, a, b), jnp.where(even, b, a)
        both = jnp.where((lane & 8) == 8 * half, from_west, from_east)
        dv, oc, weights, pair, pair_turned = (
            turn(both, extra + 120 - place(kind, 0, half)) for kind, extra in ((0, 0), (1, 0), (2, 0), (3, 0), (3, 64))
        )
        oc = jnp.where(near if used is None else near & used, oc, 0.0)
        ocean[at(group), :] = oc
        field[2, at(group), :] = dv * oc
        weight[2, at(group), :] = weights * oc
        east_c[2, at(group), :] = jnp.where(low, pair, pair_turned) * oc
        north_c[2, at(group), :] = jnp.where(low, pair_turned, pair) * oc

    ocean[at(groups + 2), :] = jnp.zeros((8, LANES), f32)
    field[2, at(groups + 2), :] = jnp.zeros((8, LANES), f32)
    for group in range(groups):
        set_group(group + 1, group % half_groups, group // half_groups)
    set_group(0, half_groups, 0, top)
    set_group(groups + 1, half_groups, 0, jnp.logical_not(top))
    face[...] = face_in[...]

    for group in range(groups + 2):
        here = at(group)
        oc, half_face = ocean[here, :], east_c[2, here, :]
        e, w = turn(oc, -1), turn(half_face, 1)
        east_c[2, here, :] = half_face * jnp.where((lane & 63) == 63, oc_edge[here, :], e)
        west_c[2, here, :] = oc * jnp.where((lane & 63) == 0, ek_edge[here, :], w)
        north_c[2, here, :] = north_c[2, here, :] * ocean[at(group, 1), :]
        for s in range(2):
            east, west = east_in[s, here, :], west_in[s, here, :]
            east_c[s, here, :] = jnp.where(lane == 127 - 64 * s, east * e, east)
            west_c[s, here, :] = jnp.where(lane == 64 * s, west * w, west)


def with_columns_beside(groups, own, edges, halo1, halo2, face):
    full = pl.BlockSpec(memory_space=pltpu.VMEM)
    inputs = [*edges, halo1, halo2, face, *own]
    return pl.pallas_call(
        functools.partial(beside_kernel, "lon", "lat", groups),
        out_shape=[jax.ShapeDtypeStruct(x.shape, f32) for x in (*own, face)],
        in_specs=[full] * len(inputs),
        out_specs=[full] * 6,
        scratch_shapes=[pltpu.VMEM(edges[0].shape, f32)],
        input_output_aliases={5 + i: i for i in range(5)},
        compiler_params=pltpu.CompilerParams(vmem_limit_bytes=VMEM_LIMIT),
    )(*inputs)


def strip_kernel(count, offsets, lon_axis, lat_axis, partner, gathered_pieces, beyond_out, face_out, blocks):
    lon = lax.axis_index(lon_axis)

    top = lax.axis_index(lat_axis) == 1

    @pl.when(jnp.logical_not(top))
    def _():
        beyond_out[...] = jnp.zeros(beyond_out.shape, f32)
        face_out[...] = jnp.zeros(face_out.shape, f32)

    @pl.when(top)
    def _():
        strip_steps(lon, count, offsets, partner, gathered_pieces, beyond_out, face_out, blocks)


def strip_steps(lon, count, offsets, partner, gathered_pieces, beyond_out, face_out, blocks):
    odd = lon % 2
    neighbour = lax.rem(lon + 2 * odd + count - 1, count)
    owners = (lon, lax.bitwise_xor(lon, 2), lax.bitwise_xor(lon, 1), neighbour)
    for piece, owner in zip(gathered_pieces, owners):
        first = piece.shape[0] - STRIP * len(offsets)
        for slot, offset in enumerate(offsets):
            block = lax.bitwise_xor(owner, offset)
            row = first + STRIP * slot
            blocks[pl.ds(pl.multiple_of(block * STRIP, 8), STRIP), :] = piece[row : row + STRIP, :]
    wide = lanes_of((count, LANES))

    def strip_row(index, row):
        return blocks[pl.ds(STRIP_AT[index] + row, count, stride=STRIP), :]

    def strip_shift(values, to_east):
        step, edge = (-1, LANES - 1) if to_east else (1, 0)
        moved = [turn(x, step) for x in values]
        beside = [turn(x, step, 0) for x in moved]
        return [jnp.where(wide == edge, y, x) for x, y in zip(moved, beside)]

    partner_block = partner[...] >> 7
    partner_lane = partner[...] & (LANES - 1)

    def across(x):
        parts = []
        for first in range(0, count, 8):
            lanes_at = partner_lane[first : first + 8]
            block_at = partner_block[first : first + 8]
            total = jnp.zeros((8, LANES), f32)
            for block in range(count):
                source = jnp.broadcast_to(x[block : block + 1, :], (8, LANES))
                picked = jnp.take_along_axis(source, lanes_at, axis=1)
                total = jnp.where(block_at == block, picked, total)
            parts.append(total)
        return parts[0] if len(parts) == 1 else jnp.concatenate(parts, axis=0)

    block_index = lax.broadcasted_iota(jnp.int32, (count, LANES), 0)
    to_east = lax.rem(lon + 1, count)
    to_west = lax.rem(lon + count - 1, count)
    one = lanes_of((1, LANES))
    last_only = lax.broadcasted_iota(jnp.int32, (8, LANES), 0) == 7

    def write_rows(out, values):
        row = lambda level, block: jnp.sum(jnp.where(block_index == block, values[level], 0.0), axis=0, keepdims=True)
        here = [row(level, lon) for level in range(2)]
        east = [row(level, to_east) for level in range(2)]
        west = [row(level, to_west) for level in range(2)]
        turned = [turn(x, 64) for x in (here[1], east[1], west[1])]
        beside = jnp.where(one < 32, east[0], jnp.where(one >= 96, west[0], jnp.where(one >= 64, turned[1], turned[2])))
        for s, value in enumerate((here[0], turned[0], beside)):
            out[8 * s : 8 * s + 8, :] = jnp.where(last_only, jnp.broadcast_to(value, (8, LANES)), 0.0)

    east_k = [strip_row(6, r) for r in range(HALO)]
    north_k = [strip_row(7, r) for r in range(HALO)]
    top_k = 0.5 * (north_k[-1] + across(north_k[-1]))
    both = range(2)
    oc = [[strip_row(2 + level, r) for r in range(HALO)] for level in both]
    u = [[strip_row(level, r) * oc[level][r] for r in range(HALO)] for level in both]
    oc_east = strip_shift([x for level in both for x in oc[level]], True)
    e = [[east_k[r] * oc[level][r] * oc_east[HALO * level + r] for r in range(HALO)] for level in both]
    w = strip_shift([x for level in both for x in e[level]], False)
    w = [w[:HALO], w[HALO:]]
    n = [[north_k[r] * oc[level][r] * oc[level][r + 1] for r in range(HALO - 1)] for level in both]
    for level in both:
        n[level].append(top_k * oc[level][-1] * across(oc[level][-1]))
    write_rows(face_out, [n[0][-1], n[1][-1]])
    c = [
        [None] + [1.0 - e[level][r] - w[level][r] - n[level][r] - n[level][r - 1] for r in range(1, HALO)]
        for level in both
    ]
    for t in range(HALO):
        if t == STEPS:
            for level in both:
                for r in range(t, HALO):
                    u[level][r] = strip_row(4 + level, r) * oc[level][r] * u[level][r]
        beyond = [across(u[level][-1]) for level in both]
        write_rows(beyond_out.at[t], beyond)
        if t == HALO - 1:
            break
        rest = [(level, r) for level in both for r in range(t + 1, HALO)]
        east = strip_shift([u[level][r] for level, r in rest], True)
        west = strip_shift([u[level][r] for level, r in rest], False)
        new = [list(u[0]), list(u[1])]
        for (level, r), ue, uw in zip(rest, east, west):
            north = u[level][r + 1] if r + 1 < HALO else beyond[level]
            new[level][r] = (
                c[level][r] * u[level][r]
                + e[level][r] * ue
                + w[level][r] * uw
                + n[level][r] * north
                + n[level][r - 1] * u[level][r - 1]
            )
        u = new


def strip_rows(partner, pieces, offsets):
    count = partner.shape[0]
    full = pl.BlockSpec(memory_space=pltpu.VMEM)
    inputs = [partner, *pieces]

    def kernel(partner_ref, *refs):
        strip_kernel(count, offsets, "lon", "lat", partner_ref, refs[: len(pieces)], *refs[len(pieces) :])

    return pl.pallas_call(
        kernel,
        out_shape=[jax.ShapeDtypeStruct((HALO, 24, LANES), f32), jax.ShapeDtypeStruct((24, LANES), f32)],
        in_specs=[full] * len(inputs),
        out_specs=[full] * 2,
        scratch_shapes=[pltpu.VMEM((STRIP * count, LANES), f32)],
        compiler_params=pltpu.CompilerParams(vmem_limit_bytes=VMEM_LIMIT),
    )(*inputs)


def image_kernel(
    d, sea, res, squares, _, weight, east_c, west_c, north_c, beyond, face, image, stats, field, other
):
    groups = d.shape[1] // 8
    zero = jnp.zeros((8, LANES), f32)
    at = slab_index

    first_row = lax.broadcasted_iota(jnp.int32, (8, LANES), 0) == 0
    last = groups + 2
    for s in range(3):
        other[s, at(last), :] = zero

    def step(t, source, target):
        before = [zero] * 3
        for group in range(groups + 2):
            here, up = at(group), at(group, 1)
            u = [source[s, here, :] for s in range(3)]
            e, w = east_of(u), west_of(u)
            for s in range(3):
                flux = north_c[s, here, :] * (source[s, up, :] - u[s])
                if group == groups:
                    fold = slice(8 * s, 8 * s + 8)
                    flux = flux + face[fold, :] * (beyond[t, fold, :] - u[s])
                moved = turn(flux, 1, 0)
                below = jnp.where(first_row, before[s], moved)
                before[s] = moved
                target[s, here, :] = (
                    u[s]
                    + east_c[s, here, :] * (e[s] - u[s])
                    - west_c[s, here, :] * (u[s] - w[s])
                    + flux
                    - below
                )

    def two_steps(i, carry):
        @pl.when(2 * i == STEPS)
        def _():
            for group in range(groups + 2):
                for s in range(3):
                    field[s, at(group), :] = field[s, at(group), :] * weight[s, at(group), :]

        step(2 * i, field, other)
        step(2 * i + 1, other, field)
        return carry

    lax.fori_loop(0, STEPS, two_steps, 0)

    rr, rq, dq, qq = squares[...], zero, zero, zero
    for group in range(groups):
        here = slice(8 * group, 8 * group + 8)
        for level in range(2):
            u = turn(field[level, at(group + 1), :], 64 * level)
            o = sea[level, here, :].astype(f32)
            dv, rv = d[level, here, :], res[level, here, :]
            q = dv + o * u
            image[level, here, :] = q
            rq, dq, qq = rq + rv * q, dq + dv * q, qq + q * q
    own = jnp.where(qq > 0.0, rq / jnp.where(qq > 0.0, qq, 1.0), 0.0)
    ss = sq = zero
    for group in range(groups):
        here = slice(8 * group, 8 * group + 8)
        for level in range(2):
            q = image[level, here, :]
            s = res[level, here, :] - own * q
            ss, sq = ss + s * s, sq + s * q
    rr, rq, dq, qq_all = (jnp.sum(x) for x in (rr, rq, dq, qq))
    a0 = jnp.where(qq_all > 0.0, rq / jnp.where(qq_all > 0.0, qq_all, 1.0), 0.0)
    t = a0 - own
    ss = jnp.sum(ss + t * (t * qq - 2.0 * sq))
    sq = jnp.sum(sq - t * qq)
    qq = qq_all
    one = lanes_of((1, LANES))
    row = jnp.zeros((1, LANES), f32)
    for index, value in enumerate((rr, dq, ss, sq, qq, a0)):
        row = jnp.where(one == index, value, row)
    stats[...] = row


def image_and_stats(d, sea, res, squares, coeffs, beyond, face):
    full = pl.BlockSpec(memory_space=pltpu.VMEM)
    inputs = [d, sea, res, squares, *coeffs, beyond, face]
    image, stats, _ = pl.pallas_call(
        image_kernel,
        out_shape=[jax.ShapeDtypeStruct(x, f32) for x in (d.shape, (1, LANES), coeffs[0].shape)],
        in_specs=[full] * len(inputs),
        out_specs=[full] * 3,
        scratch_shapes=[pltpu.VMEM(coeffs[0].shape, f32)],
        input_output_aliases={4: 2},
        compiler_params=pltpu.CompilerParams(vmem_limit_bytes=VMEM_LIMIT),
    )(*inputs)
    return image, stats


def update_kernel(count, *refs):
    parts = refs[:count]
    iterate, res, d, image, iterate_hbm, res_hbm, d_hbm, new_iterate, new_res, new_d, sent = refs[count:]
    table = jnp.concatenate([part[...] for part in parts], axis=0)
    lane = lanes_of(table.shape)
    sums = jnp.sum(table, axis=0, keepdims=True)
    one = lanes_of(sums.shape)
    pick = lambda row, index: jnp.sum(jnp.where(one == index, row, 0.0), axis=1, keepdims=True)
    old_norm = pick(sums, 0)
    alpha = old_norm / pick(sums, 1)
    t = alpha - turn(table, -3)
    norms = table + t * (t * turn(table, -2) - 2.0 * turn(table, -1))
    new_norm = pick(jnp.sum(norms, axis=0, keepdims=True), 2)
    beta = new_norm / old_norm
    rows = d.shape[1]
    pieces = 1
    alpha = jnp.broadcast_to(alpha, (8, LANES))
    beta = jnp.broadcast_to(beta, (8, LANES))
    copies = []

    def send(source, target, part):
        copies.append(pltpu.make_async_copy(source.at[part], target.at[part], sent.at[len(copies)]))
        copies[-1].start()

    size = rows // pieces
    parts_of = [(level, first) for level in range(2) for first in range(0, rows, size)]
    for level, first in parts_of:
        for row in range(first, first + size, 8):
            here = slice(row, row + 8)
            new_iterate[level, here, :] = iterate[level, here, :] + alpha * d[level, here, :]
            new_res[level, here, :] = res[level, here, :] - alpha * image[level, here, :]
        part = (level, pl.ds(first, size), slice(None))
        send(new_iterate, iterate_hbm, part)
        send(new_res, res_hbm, part)
    for level, first in parts_of:
        for row in range(first, first + size, 8):
            here = slice(row, row + 8)
            new_d[level, here, :] = new_res[level, here, :] + beta * d[level, here, :]
        send(new_d, d_hbm, (level, pl.ds(first, size), slice(None)))
    for copy in copies:
        copy.wait()


def update(parts, iterate, res, d, image):
    full = pl.BlockSpec(memory_space=pltpu.VMEM)
    return pl.pallas_call(
        functools.partial(update_kernel, len(parts)),
        out_shape=[jax.ShapeDtypeStruct(d.shape, f32)] * 3,
        in_specs=[full] * (len(parts) + 4),
        out_specs=[pl.BlockSpec(memory_space=pltpu.HBM)] * 3,
        scratch_shapes=[pltpu.VMEM(d.shape, f32)] * 3 + [pltpu.SemaphoreType.DMA((12,))],
        compiler_params=pltpu.CompilerParams(vmem_limit_bytes=VMEM_LIMIT),
    )(*parts, iterate, res, d, image)


def swapped(value, axis, distance):
    return lax.ppermute(value, axis, [(i, i ^ distance) for i in range(lax.axis_size(axis))])


def odd_pairs(value, axis):
    count = lax.axis_size(axis)
    pairs = []
    for i in range(1, count, 2):
        pairs += [(i, (i + 1) % count), ((i + 1) % count, i)]
    return lax.ppermute(value, axis, pairs)


def distances(count):
    found = []
    while count > 1:
        count //= 2
        found.append(count)
    return found


def strip_swap(value, distance, alone=False):
    members, count, halves = (lax.axis_size(axis) for axis in ("member", "lon", "lat"))
    number = lambda m, i, t: (m * count + i) * halves + t
    other = lambda m, i, t: number(m, i ^ distance, t) if t or members % 2 else number(m ^ 1, i, t)
    places = [(m, i, t) for m in range(members) for i in range(count) for t in range(int(alone), halves)]
    return lax.ppermute(value, ("member", "lon", "lat"), [(number(*p), other(*p)) for p in places])


def butterfly(pieces, offsets, swap, order):
    pieces, offsets = list(pieces), list(offsets)
    for distance in order:
        whole = pieces[0] if len(pieces) == 1 else jnp.concatenate(pieces, axis=0)
        pieces.append(swap(whole, distance))
        offsets += [o ^ distance for o in offsets]
    return pieces, offsets


def shards(iterate, residual, direction, land_sea, precision_weight, east_kappa, north_kappa, fold_partner):
    count = lax.axis_size("lon")
    fields = (direction, land_sea, precision_weight, east_kappa, north_kappa)
    strip, edge, partner = rows_to_send(*fields, fold_partner.reshape(count, LANES))
    rows_in = swapped(edge, "lat", 1)
    far, *rest = distances(count)[:-2]
    pieces, offsets = butterfly([strip, strip_swap(strip, far, True)], [0, far], strip_swap, rest)
    pay1, pay2, strips = columns_to_send(*fields, rows_in, pieces)
    halo1 = swapped(pay1, "lon", 1)
    halo2 = odd_pairs(pay2, "lon")
    across_two = strip_swap(strips, 2)
    beyond, face = strip_rows(partner, [strips, across_two, halo1, halo2], offsets)
    *own, oc_edge, ek_edge, squares = own_coefficients(*fields, residual, rows_in)
    groups = direction.shape[1] // 8
    *coeffs, face = with_columns_beside(groups, own, (oc_edge, ek_edge), halo1, halo2, face)
    image, stats = image_and_stats(direction, land_sea, residual, squares, coeffs, beyond, face)
    parts, _ = butterfly([stats], [0], lambda value, distance: swapped(value, "lon", distance), distances(count)[::-1])
    parts.append(swapped(jnp.concatenate(parts, axis=0), "lat", 1))
    return tuple(update(parts, iterate, residual, direction, image))


def solution(mesh):
    field = P("member", "lat", "lon")
    level = P(None, "lat", "lon")
    flat = P("lat", "lon")
    return jax.shard_map(
        shards,
        mesh=mesh,
        in_specs=(field, field, field, level, level, flat, flat, P()),
        out_specs=(field, field, field),
        check_vma=False,
    )
```

```python
import functools

import jax
import jax.numpy as jnp
from jax import lax
from jax.experimental import pallas as pl
from jax.experimental.pallas import tpu as pltpu
from jax.sharding import PartitionSpec as P

STEPS = 4
HALO = 2 * STEPS
LANES = 128
VMEM_LIMIT = 24 * 1024 * 1024
f32 = jnp.float32


def turn(value, shift, axis=1):
    shift = shift % value.shape[axis]
    return value if shift == 0 else pltpu.roll(value, shift, axis)


def lanes_of(shape):
    return lax.broadcasted_iota(jnp.int32, shape, 1)


def place(kind, level, half):
    return 16 * kind + 8 * half + 64 * level


STRIP = 56
STRIP_AT = (0, 8, 16, 24, 48 - STEPS, 52 - STEPS, 32, 40)


def rows_kernel(lat_axis, d, sea, pw, ek, nk, fold, strip, edge, partner, sea_strip, sea_edge, pw_strip, arrived):
    rows = d.shape[1]
    top_rows = pl.ds(rows - 8, 8)
    first = jnp.where(lax.axis_index(lat_axis) == 1, 0, rows - 8)
    edge_rows = pl.ds(pl.multiple_of(first, 8), 8)
    moves = [
        (sea.at[:, top_rows, :], sea_strip),
        (pw.at[:, top_rows, :], pw_strip),
        (sea.at[:, edge_rows, :], sea_edge),
        (d.at[0, top_rows, :], strip.at[0:8]),
        (d.at[1, top_rows, :], strip.at[8:16]),
        (ek.at[top_rows, :], strip.at[32:40]),
        (nk.at[top_rows, :], strip.at[40:48]),
        (d.at[:, edge_rows, :], edge.at[0:2]),
        (pw.at[:, edge_rows, :], edge.at[4:6]),
        (ek.at[edge_rows, :], edge.at[6]),
        (nk.at[edge_rows, :], edge.at[7]),
        (fold, partner),
    ]
    copies = [pltpu.make_async_copy(a, b, arrived.at[i]) for i, (a, b) in enumerate(moves)]
    for copy in copies:
        copy.start()
    for copy in copies:
        copy.wait()
    for level in range(2):
        strip[16 + 8 * level : 24 + 8 * level, :] = sea_strip[level].astype(f32)
    strip[48:56, :] = jnp.concatenate([pw_strip[0, STEPS:, :], pw_strip[1, STEPS:, :]], axis=0)
    edge[2:4] = sea_edge[...].astype(f32)


def rows_to_send(d, sea, pw, ek, nk, fold):
    full = pl.BlockSpec(memory_space=pltpu.VMEM)
    inputs = [pltpu.with_memory_space_constraint(x, pltpu.HBM) for x in (d, sea, pw, ek, nk, fold)]
    return pl.pallas_call(
        functools.partial(rows_kernel, "lat"),
        out_shape=[
            jax.ShapeDtypeStruct((STRIP, LANES), f32),
            jax.ShapeDtypeStruct((8, 8, LANES), f32),
            jax.ShapeDtypeStruct(fold.shape, jnp.int32),
        ],
        in_specs=[pl.BlockSpec(memory_space=pltpu.HBM)] * 6,
        out_specs=[full] * 3,
        scratch_shapes=[
            pltpu.VMEM((2, 8, LANES), jnp.int32),
            pltpu.VMEM((2, 8, LANES), jnp.int32),
            pltpu.VMEM((2, 8, LANES), f32),
            pltpu.SemaphoreType.DMA((12,)),
        ],
        compiler_params=pltpu.CompilerParams(vmem_limit_bytes=VMEM_LIMIT),
    )(*inputs)


def pack_kernel(lon_axis, d, sea, pw, ek, nk, rows_in, *refs):
    *pieces, pay1, pay2, strips = refs
    first = d.shape[1] // 2 + 8
    for target, at in ((strips, 0), (pay1, first), (pay2, first)):
        for piece in pieces:
            size = piece.shape[0]
            target[at : at + size, :] = piece[...]
            at += size
    rows = d.shape[1]
    groups = rows // 8
    half_groups = groups // 2
    even = lax.axis_index(lon_axis) % 2 == 0

    def plane(index, group):
        if group == groups:
            return rows_in[index]
        at = pl.ds(8 * group, 8)
        if index < 2:
            return d[index, at, :]
        if index < 4:
            return sea[index - 2, at, :].astype(f32)
        if index < 6:
            return pw[index - 4, at, :]
        return (ek, nk)[index - 6][at, :]

    lane = lanes_of((8, LANES))
    for line in range(half_groups + 1):
        east = jnp.zeros((8, LANES), f32)
        west = jnp.zeros((8, LANES), f32)
        for half, group in enumerate((line, line + half_groups) if line < half_groups else (groups,)):
            for kind in range(4):
                for level in range(2):
                    at = place(kind, level, half)
                    turned = turn(plane(2 * kind + level, group), at + 8)
                    east = jnp.where((lane >= at) & (lane < at + 8), turned, east)
                    first = (at + 8) % LANES
                    west = jnp.where((lane >= first) & (lane < first + 8), turned, west)
        pay1[8 * line : 8 * line + 8, :] = jnp.where(even, east, west)
        pay2[8 * line : 8 * line + 8, :] = jnp.where(even, west, east)


def columns_to_send(d, sea, pw, ek, nk, rows_in, pieces):
    strips = sum(piece.shape[0] for piece in pieces)
    size = d.shape[1] // 2 + 8 + strips
    full = pl.BlockSpec(memory_space=pltpu.VMEM)
    inputs = (d, sea, pw, ek, nk, rows_in, *pieces)
    return pl.pallas_call(
        functools.partial(pack_kernel, "lon"),
        out_shape=[jax.ShapeDtypeStruct((n, LANES), f32) for n in (size, size, strips)],
        in_specs=[full] * len(inputs),
        out_specs=[full] * 3,
        compiler_params=pltpu.CompilerParams(vmem_limit_bytes=VMEM_LIMIT),
    )(*inputs)


def slab_index(group, shift=0):
    return slice(8 + 8 * group + shift, 16 + 8 * group + shift)


def east_of(x):
    lane = lanes_of(x[0].shape)
    a, b, s = (turn(v, -1) for v in x)
    return (
        jnp.where(lane == 127, s, a),
        jnp.where(lane == 63, s, b),
        jnp.where(lane == 127, a, jnp.where(lane == 63, b, s)),
    )


def west_of(x):
    lane = lanes_of(x[0].shape)
    a, b, s = (turn(v, 1) for v in x)
    return (
        jnp.where(lane == 0, s, a),
        jnp.where(lane == 64, s, b),
        jnp.where(lane == 0, a, jnp.where(lane == 64, b, s)),
    )


def own_kernel(
    lat_axis, d, sea, pw, ek, nk, res, rows_in,
    field, weight, east_c, west_c, north_c, oc_edge, ek_edge, squares, ocean,
):
    top = lax.axis_index(lat_axis) == 1
    groups = d.shape[1] // 8
    lane = lanes_of((8, LANES))
    zero = jnp.zeros((8, LANES), f32)
    at = slab_index

    def set_group(group, planes):
        d0, d1, oc0, oc1, pw0, pw1, ek_here, nk_here = planes
        turned = [turn(x, 64) for x in (d1, oc1, pw1, ek_here, nk_here)]
        for s, (dv, oc, weights, east, north) in enumerate(((d0, oc0, pw0, ek_here, nk_here), turned)):
            ocean[s, at(group), :] = oc
            field[s, at(group), :] = dv * oc
            weight[s, at(group), :] = weights * oc
            east_c[s, at(group), :] = east * oc
            north_c[s, at(group), :] = north * oc

    for s in range(2):
        ocean[s, at(groups + 2), :] = zero
        field[s, at(groups + 2), :] = zero
    for group in range(groups):
        here = slice(8 * group, 8 * group + 8)
        set_group(
            group + 1,
            [d[0, here, :], d[1, here, :], sea[0, here, :].astype(f32), sea[1, here, :].astype(f32),
             pw[0, here, :], pw[1, here, :], ek[here, :], nk[here, :]],
        )
    for group, used in ((0, top), (groups + 1, jnp.logical_not(top))):
        planes = [rows_in[i] for i in range(8)]
        planes[2:4] = [jnp.where(used, x, 0.0) for x in planes[2:4]]
        set_group(group, planes)

    total = zero
    for level in range(2):
        for group in range(groups):
            r = res[level, 8 * group : 8 * group + 8, :]
            total = total + r * r
    squares[...] = total

    for group in range(groups + 2):
        here = at(group)
        oc = [ocean[s, here, :] for s in range(2)]
        half_face = [east_c[s, here, :] for s in range(2)]
        e = [turn(x, -1) for x in oc]
        w = [turn(x, 1) for x in half_face]
        for s in range(2):
            east_c[s, here, :] = jnp.where(lane == 127 - 64 * s, half_face[s], half_face[s] * e[s])
            west_c[s, here, :] = jnp.where(lane == 64 * s, oc[s], oc[s] * w[s])
            north_c[s, here, :] = north_c[s, here, :] * ocean[s, at(group, 1), :]
        oc_edge[here, :] = jnp.where(lane == 63, e[1], e[0])
        ek_edge[here, :] = jnp.where(lane == 64, w[1], w[0])


def own_coefficients(d, sea, pw, ek, nk, res, rows_in):
    full = pl.BlockSpec(memory_space=pltpu.VMEM)
    rows = d.shape[1] + 56
    return pl.pallas_call(
        functools.partial(own_kernel, "lat"),
        out_shape=[jax.ShapeDtypeStruct((3, rows, LANES), f32)] * 5
        + [jax.ShapeDtypeStruct((n, LANES), f32) for n in (rows, rows, 8)],
        in_specs=[full] * 7,
        out_specs=[full] * 8,
        scratch_shapes=[pltpu.VMEM((2, rows, LANES), f32)],
        compiler_params=pltpu.CompilerParams(vmem_limit_bytes=VMEM_LIMIT),
    )(d, sea, pw, ek, nk, res, rows_in)


def beside_kernel(
    lon_axis, lat_axis, groups, oc_edge, ek_edge, halo1, halo2, face_in, field_in, weight_in, east_in, west_in, north_in,
    field, weight, east_c, west_c, north_c, face, ocean,
):
    top = lax.axis_index(lat_axis) == 1
    even = lax.axis_index(lon_axis) % 2 == 0
    half_groups = groups // 2
    lane = lanes_of((8, LANES))
    low = (lane < 32) | (lane >= 96)
    near = ((lane & 63) < 8) | ((lane & 63) >= 56)
    at = slab_index

    def set_group(group, line, half, used=None):
        there = slice(8 * line, 8 * line + 8)
        a, b = halo1[there, :], halo2[there, :]
        from_east, from_west = jnp.where(even, a, b), jnp.where(even, b, a)
        both = jnp.where((lane & 8) == 8 * half, from_west, from_east)
        dv, oc, weights, pair, pair_turned = (
            turn(both, extra + 120 - place(kind, 0, half)) for kind, extra in ((0, 0), (1, 0), (2, 0), (3, 0), (3, 64))
        )
        oc = jnp.where(near if used is None else near & used, oc, 0.0)
        ocean[at(group), :] = oc
        field[2, at(group), :] = dv * oc
        weight[2, at(group), :] = weights * oc
        east_c[2, at(group), :] = jnp.where(low, pair, pair_turned) * oc
        north_c[2, at(group), :] = jnp.where(low, pair_turned, pair) * oc

    ocean[at(groups + 2), :] = jnp.zeros((8, LANES), f32)
    field[2, at(groups + 2), :] = jnp.zeros((8, LANES), f32)
    for group in range(groups):
        set_group(group + 1, group % half_groups, group // half_groups)
    set_group(0, half_groups, 0, top)
    set_group(groups + 1, half_groups, 0, jnp.logical_not(top))
    face[...] = face_in[...]

    for group in range(groups + 2):
        here = at(group)
        oc, half_face = ocean[here, :], east_c[2, here, :]
        e, w = turn(oc, -1), turn(half_face, 1)
        east_c[2, here, :] = half_face * jnp.where((lane & 63) == 63, oc_edge[here, :], e)
        west_c[2, here, :] = oc * jnp.where((lane & 63) == 0, ek_edge[here, :], w)
        north_c[2, here, :] = north_c[2, here, :] * ocean[at(group, 1), :]
        for s in range(2):
            east, west = east_in[s, here, :], west_in[s, here, :]
            east_c[s, here, :] = jnp.where(lane == 127 - 64 * s, east * e, east)
            west_c[s, here, :] = jnp.where(lane == 64 * s, west * w, west)


def with_columns_beside(groups, own, edges, halo1, halo2, face):
    full = pl.BlockSpec(memory_space=pltpu.VMEM)
    inputs = [*edges, halo1, halo2, face, *own]
    return pl.pallas_call(
        functools.partial(beside_kernel, "lon", "lat", groups),
        out_shape=[jax.ShapeDtypeStruct(x.shape, f32) for x in (*own, face)],
        in_specs=[full] * len(inputs),
        out_specs=[full] * 6,
        scratch_shapes=[pltpu.VMEM(edges[0].shape, f32)],
        input_output_aliases={5 + i: i for i in range(5)},
        compiler_params=pltpu.CompilerParams(vmem_limit_bytes=VMEM_LIMIT),
    )(*inputs)


def strip_kernel(count, offsets, lon_axis, lat_axis, partner, gathered_pieces, beyond_out, face_out, blocks):
    lon = lax.axis_index(lon_axis)

    top = lax.axis_index(lat_axis) == 1

    @pl.when(jnp.logical_not(top))
    def _():
        beyond_out[...] = jnp.zeros(beyond_out.shape, f32)
        face_out[...] = jnp.zeros(face_out.shape, f32)

    @pl.when(top)
    def _():
        strip_steps(lon, count, offsets, partner, gathered_pieces, beyond_out, face_out, blocks)


def strip_steps(lon, count, offsets, partner, gathered_pieces, beyond_out, face_out, blocks):
    odd = lon % 2
    neighbour = lax.rem(lon + 2 * odd + count - 1, count)
    owners = (lon, lax.bitwise_xor(lon, 2), lax.bitwise_xor(lon, 1), neighbour)
    for piece, owner in zip(gathered_pieces, owners):
        first = piece.shape[0] - STRIP * len(offsets)
        for slot, offset in enumerate(offsets):
            block = lax.bitwise_xor(owner, offset)
            row = first + STRIP * slot
            blocks[pl.ds(pl.multiple_of(block * STRIP, 8), STRIP), :] = piece[row : row + STRIP, :]
    wide = lanes_of((count, LANES))

    def strip_row(index, row):
        return blocks[pl.ds(STRIP_AT[index] + row, count, stride=STRIP), :]

    def strip_shift(values, to_east):
        step, edge = (-1, LANES - 1) if to_east else (1, 0)
        moved = [turn(x, step) for x in values]
        beside = [turn(x, step, 0) for x in moved]
        return [jnp.where(wide == edge, y, x) for x, y in zip(moved, beside)]

    partner_block = partner[...] >> 7
    partner_lane = partner[...] & (LANES - 1)

    def across(x):
        parts = []
        for first in range(0, count, 8):
            lanes_at = partner_lane[first : first + 8]
            block_at = partner_block[first : first + 8]
            total = jnp.zeros((8, LANES), f32)
            for block in range(count):
                source = jnp.broadcast_to(x[block : block + 1, :], (8, LANES))
                picked = jnp.take_along_axis(source, lanes_at, axis=1)
                total = jnp.where(block_at == block, picked, total)
            parts.append(total)
        return parts[0] if len(parts) == 1 else jnp.concatenate(parts, axis=0)

    block_index = lax.broadcasted_iota(jnp.int32, (count, LANES), 0)
    to_east = lax.rem(lon + 1, count)
    to_west = lax.rem(lon + count - 1, count)
    one = lanes_of((1, LANES))
    last_only = lax.broadcasted_iota(jnp.int32, (8, LANES), 0) == 7

    def write_rows(out, values):
        row = lambda level, block: jnp.sum(jnp.where(block_index == block, values[level], 0.0), axis=0, keepdims=True)
        here = [row(level, lon) for level in range(2)]
        east = [row(level, to_east) for level in range(2)]
        west = [row(level, to_west) for level in range(2)]
        turned = [turn(x, 64) for x in (here[1], east[1], west[1])]
        beside = jnp.where(one < 32, east[0], jnp.where(one >= 96, west[0], jnp.where(one >= 64, turned[1], turned[2])))
        for s, value in enumerate((here[0], turned[0], beside)):
            out[8 * s : 8 * s + 8, :] = jnp.where(last_only, jnp.broadcast_to(value, (8, LANES)), 0.0)

    east_k = [strip_row(6, r) for r in range(HALO)]
    north_k = [strip_row(7, r) for r in range(HALO)]
    top_k = 0.5 * (north_k[-1] + across(north_k[-1]))
    both = range(2)
    oc = [[strip_row(2 + level, r) for r in range(HALO)] for level in both]
    u = [[strip_row(level, r) * oc[level][r] for r in range(HALO)] for level in both]
    oc_east = strip_shift([x for level in both for x in oc[level]], True)
    e = [[east_k[r] * oc[level][r] * oc_east[HALO * level + r] for r in range(HALO)] for level in both]
    w = strip_shift([x for level in both for x in e[level]], False)
    w = [w[:HALO], w[HALO:]]
    n = [[north_k[r] * oc[level][r] * oc[level][r + 1] for r in range(HALO - 1)] for level in both]
    for level in both:
        n[level].append(top_k * oc[level][-1] * across(oc[level][-1]))
    write_rows(face_out, [n[0][-1], n[1][-1]])
    c = [
        [None] + [1.0 - e[level][r] - w[level][r] - n[level][r] - n[level][r - 1] for r in range(1, HALO)]
        for level in both
    ]
    for t in range(HALO):
        if t == STEPS:
            for level in both:
                for r in range(t, HALO):
                    u[level][r] = strip_row(4 + level, r) * oc[level][r] * u[level][r]
        beyond = [across(u[level][-1]) for level in both]
        write_rows(beyond_out.at[t], beyond)
        if t == HALO - 1:
            break
        rest = [(level, r) for level in both for r in range(t + 1, HALO)]
        east = strip_shift([u[level][r] for level, r in rest], True)
        west = strip_shift([u[level][r] for level, r in rest], False)
        new = [list(u[0]), list(u[1])]
        for (level, r), ue, uw in zip(rest, east, west):
            north = u[level][r + 1] if r + 1 < HALO else beyond[level]
            new[level][r] = (
                c[level][r] * u[level][r]
                + e[level][r] * ue
                + w[level][r] * uw
                + n[level][r] * north
                + n[level][r - 1] * u[level][r - 1]
            )
        u = new


def strip_rows(partner, pieces, offsets):
    count = partner.shape[0]
    full = pl.BlockSpec(memory_space=pltpu.VMEM)
    inputs = [partner, *pieces]

    def kernel(partner_ref, *refs):
        strip_kernel(count, offsets, "lon", "lat", partner_ref, refs[: len(pieces)], *refs[len(pieces) :])

    return pl.pallas_call(
        kernel,
        out_shape=[jax.ShapeDtypeStruct((HALO, 24, LANES), f32), jax.ShapeDtypeStruct((24, LANES), f32)],
        in_specs=[full] * len(inputs),
        out_specs=[full] * 2,
        scratch_shapes=[pltpu.VMEM((STRIP * count, LANES), f32)],
        compiler_params=pltpu.CompilerParams(vmem_limit_bytes=VMEM_LIMIT),
    )(*inputs)


def image_kernel(
    d, sea, res, squares, _, weight, east_c, west_c, north_c, beyond, face, image, stats, field, other
):
    groups = d.shape[1] // 8
    zero = jnp.zeros((8, LANES), f32)
    at = slab_index

    first_row = lax.broadcasted_iota(jnp.int32, (8, LANES), 0) == 0
    last = groups + 2
    for s in range(3):
        other[s, at(last), :] = zero

    def step(t, source, target):
        before = [zero] * 3
        for group in range(groups + 2):
            here, up = at(group), at(group, 1)
            u = [source[s, here, :] for s in range(3)]
            e, w = east_of(u), west_of(u)
            for s in range(3):
                flux = north_c[s, here, :] * (source[s, up, :] - u[s])
                if group == groups:
                    fold = slice(8 * s, 8 * s + 8)
                    flux = flux + face[fold, :] * (beyond[t, fold, :] - u[s])
                moved = turn(flux, 1, 0)
                below = jnp.where(first_row, before[s], moved)
                before[s] = moved
                target[s, here, :] = (
                    u[s]
                    + east_c[s, here, :] * (e[s] - u[s])
                    - west_c[s, here, :] * (u[s] - w[s])
                    + flux
                    - below
                )

    def two_steps(i, carry):
        @pl.when(2 * i == STEPS)
        def _():
            for group in range(groups + 2):
                for s in range(3):
                    field[s, at(group), :] = field[s, at(group), :] * weight[s, at(group), :]

        step(2 * i, field, other)
        step(2 * i + 1, other, field)
        return carry

    lax.fori_loop(0, STEPS, two_steps, 0)

    rr, rq, dq, qq = squares[...], zero, zero, zero
    for group in range(groups):
        here = slice(8 * group, 8 * group + 8)
        for level in range(2):
            u = turn(field[level, at(group + 1), :], 64 * level)
            o = sea[level, here, :].astype(f32)
            dv, rv = d[level, here, :], res[level, here, :]
            q = dv + o * u
            image[level, here, :] = q
            rq, dq, qq = rq + rv * q, dq + dv * q, qq + q * q
    own = jnp.where(qq > 0.0, rq / jnp.where(qq > 0.0, qq, 1.0), 0.0)
    ss = sq = zero
    for group in range(groups):
        here = slice(8 * group, 8 * group + 8)
        for level in range(2):
            q = image[level, here, :]
            s = res[level, here, :] - own * q
            ss, sq = ss + s * s, sq + s * q
    rr, rq, dq, qq_all = (jnp.sum(x) for x in (rr, rq, dq, qq))
    a0 = jnp.where(qq_all > 0.0, rq / jnp.where(qq_all > 0.0, qq_all, 1.0), 0.0)
    t = a0 - own
    ss = jnp.sum(ss + t * (t * qq - 2.0 * sq))
    sq = jnp.sum(sq - t * qq)
    qq = qq_all
    one = lanes_of((1, LANES))
    row = jnp.zeros((1, LANES), f32)
    for index, value in enumerate((rr, dq, ss, sq, qq, a0)):
        row = jnp.where(one == index, value, row)
    stats[...] = row


def image_and_stats(d, sea, res, squares, coeffs, beyond, face):
    full = pl.BlockSpec(memory_space=pltpu.VMEM)
    inputs = [d, sea, res, squares, *coeffs, beyond, face]
    image, stats, _ = pl.pallas_call(
        image_kernel,
        out_shape=[jax.ShapeDtypeStruct(x, f32) for x in (d.shape, (1, LANES), coeffs[0].shape)],
        in_specs=[full] * len(inputs),
        out_specs=[full] * 3,
        scratch_shapes=[pltpu.VMEM(coeffs[0].shape, f32)],
        input_output_aliases={4: 2},
        compiler_params=pltpu.CompilerParams(vmem_limit_bytes=VMEM_LIMIT),
    )(*inputs)
    return image, stats


def update_kernel(count, *refs):
    parts = refs[:count]
    iterate, res, d, image, iterate_hbm, res_hbm, d_hbm, new_iterate, new_res, new_d, sent = refs[count:]
    table = jnp.concatenate([part[...] for part in parts], axis=0)
    lane = lanes_of(table.shape)
    sums = jnp.sum(table, axis=0, keepdims=True)
    one = lanes_of(sums.shape)
    pick = lambda row, index: jnp.sum(jnp.where(one == index, row, 0.0), axis=1, keepdims=True)
    old_norm = pick(sums, 0)
    alpha = old_norm / pick(sums, 1)
    t = alpha - turn(table, -3)
    norms = table + t * (t * turn(table, -2) - 2.0 * turn(table, -1))
    new_norm = pick(jnp.sum(norms, axis=0, keepdims=True), 2)
    beta = new_norm / old_norm
    rows = d.shape[1]
    pieces = 1
    alpha = jnp.broadcast_to(alpha, (8, LANES))
    beta = jnp.broadcast_to(beta, (8, LANES))
    copies = []

    def send(source, target, part):
        copies.append(pltpu.make_async_copy(source.at[part], target.at[part], sent.at[len(copies)]))
        copies[-1].start()

    size = rows // pieces
    parts_of = [(level, first) for level in range(2) for first in range(0, rows, size)]
    for level, first in parts_of:
        for row in range(first, first + size, 8):
            here = slice(row, row + 8)
            new_iterate[level, here, :] = iterate[level, here, :] + alpha * d[level, here, :]
            new_res[level, here, :] = res[level, here, :] - alpha * image[level, here, :]
        part = (level, pl.ds(first, size), slice(None))
        send(new_iterate, iterate_hbm, part)
        send(new_res, res_hbm, part)
    for level, first in parts_of:
        for row in range(first, first + size, 8):
            here = slice(row, row + 8)
            new_d[level, here, :] = new_res[level, here, :] + beta * d[level, here, :]
        send(new_d, d_hbm, (level, pl.ds(first, size), slice(None)))
    for copy in copies:
        copy.wait()


def update(parts, iterate, res, d, image):
    full = pl.BlockSpec(memory_space=pltpu.VMEM)
    return pl.pallas_call(
        functools.partial(update_kernel, len(parts)),
        out_shape=[jax.ShapeDtypeStruct(d.shape, f32)] * 3,
        in_specs=[full] * (len(parts) + 4),
        out_specs=[pl.BlockSpec(memory_space=pltpu.HBM)] * 3,
        scratch_shapes=[pltpu.VMEM(d.shape, f32)] * 3 + [pltpu.SemaphoreType.DMA((12,))],
        compiler_params=pltpu.CompilerParams(vmem_limit_bytes=VMEM_LIMIT),
    )(*parts, iterate, res, d, image)


def swapped(value, axis, distance):
    return lax.ppermute(value, axis, [(i, i ^ distance) for i in range(lax.axis_size(axis))])


def odd_pairs(value, axis):
    count = lax.axis_size(axis)
    pairs = []
    for i in range(1, count, 2):
        pairs += [(i, (i + 1) % count), ((i + 1) % count, i)]
    return lax.ppermute(value, axis, pairs)


def distances(count):
    found = []
    while count > 1:
        count //= 2
        found.append(count)
    return found


def strip_swap(value, distance, alone=False):
    members, count, halves = (lax.axis_size(axis) for axis in ("member", "lon", "lat"))
    number = lambda m, i, t: (m * count + i) * halves + t
    other = lambda m, i, t: number(m, i ^ distance, t) if t or members % 2 else number(m ^ 1, i, t)
    places = [(m, i, t) for m in range(members) for i in range(count) for t in range(int(alone), halves)]
    return lax.ppermute(value, ("member", "lon", "lat"), [(number(*p), other(*p)) for p in places])


def butterfly(pieces, offsets, swap, order):
    pieces, offsets = list(pieces), list(offsets)
    for distance in order:
        whole = pieces[0] if len(pieces) == 1 else jnp.concatenate(pieces, axis=0)
        pieces.append(swap(whole, distance))
        offsets += [o ^ distance for o in offsets]
    return pieces, offsets


def shards(iterate, residual, direction, land_sea, precision_weight, east_kappa, north_kappa, fold_partner):
    count = lax.axis_size("lon")
    fields = (direction, land_sea, precision_weight, east_kappa, north_kappa)
    strip, edge, partner = rows_to_send(*fields, fold_partner.reshape(count, LANES))
    rows_in = swapped(edge, "lat", 1)
    far, *rest = distances(count)[:-2]
    pieces, offsets = butterfly([strip, strip_swap(strip, far, True)], [0, far], strip_swap, rest)
    pay1, pay2, strips = columns_to_send(*fields, rows_in, pieces)
    halo1 = swapped(pay1, "lon", 1)
    halo2 = odd_pairs(pay2, "lon")
    across_two = strip_swap(strips, 2)
    beyond, face = strip_rows(partner, [strips, across_two, halo1, halo2], offsets)
    *own, oc_edge, ek_edge, squares = own_coefficients(*fields, residual, rows_in)
    groups = direction.shape[1] // 8
    *coeffs, face = with_columns_beside(groups, own, (oc_edge, ek_edge), halo1, halo2, face)
    image, stats = image_and_stats(direction, land_sea, residual, squares, coeffs, beyond, face)
    parts, _ = butterfly([stats], [0], lambda value, distance: swapped(value, "lon", distance), distances(count)[::-1])
    parts.append(swapped(jnp.concatenate(parts, axis=0), "lat", 1))
    return tuple(update(parts, iterate, residual, direction, image))


def solution(mesh):
    field = P("member", "lat", "lon")
    level = P(None, "lat", "lon")
    flat = P("lat", "lon")
    return jax.shard_map(
        shards,
        mesh=mesh,
        in_specs=(field, field, field, level, level, flat, flat, P()),
        out_specs=(field, field, field),
        check_vma=False,
    )
```
